256 devices in a mesh: gx: 16 (over x, y), gy: 16 (over z, core).
Axes of the slice: x: 4, y: 4, z: 8, core: 2. Of those that a mesh axis runs over, the one named last changes fastest.
Arguments:
- populations: float32 [19, 128, 512, 128], P(None, 'gx', 'gy'), as said below
- fluid: int32 [128, 512, 128], P('gx', 'gy'), may hold values from 0 to 1
Outputs:
- velocity_image: float32 [3, 32, 128, 32], P(None, 'gx', None, 'gy')
- magnitude: float32 [32, 128, 32], P('gx', None, 'gy')
The draws below stay inside these ranges and needn't reach their ends.
Inputs may be any that keep to these rules, and one draw needn't show every extreme that they name: `populations`: every population is positive.
All inputs are finite; a program needn't handle non-finite values.
Results may differ from the reference program's by a relative error of at most 0.00025.
Values sent between devices are 32-bit elements; how exact they have to be, the bound alone decides.
A program may use at most 128 MiB of HBM per device.

```python
import jax
import jax.numpy as jnp
from jax import lax

STEPS = 2
NX = 128
NY = 512
NZ = 128


def draw_populations(key, part):
    weights = jnp.array([1.0 / 3.0] + [1.0 / 18.0] * 6 + [1.0 / 36.0] * 12, jnp.float32)
    first_key, second_key = jax.random.split(key)
    spread_range = 0.4
    site_scale = jnp.exp(jax.random.uniform(first_key, (NX, NY, NZ), jnp.float32, -0.2, 0.2))
    noise = jnp.exp(jax.random.uniform(second_key, (19, NX, NY, NZ), jnp.float32, -spread_range, spread_range))
    return weights[:, None, None, None] * site_scale[None] * noise


def draw_fluid(key, part):
    first_key, second_key, third_key = jax.random.split(jax.random.fold_in(key, 11), 3)
    coarse = jax.random.randint(first_key, (NX // 4, NY // 4, NZ // 4), 0, 4)
    finer = jax.random.randint(second_key, (NX, NY, NZ), 0, 8)
    region = jax.random.randint(third_key, (NX // 16, NY // 16, NZ // 16), 0, 20)
    coarse_full = jnp.repeat(jnp.repeat(jnp.repeat(coarse, 4, 0), 4, 1), 4, 2)
    region_full = jnp.repeat(jnp.repeat(jnp.repeat(region, 16, 0), 16, 1), 16, 2)
    return ((coarse_full > 0) & (finer > 0) & (region_full >= 7)).astype(jnp.int32)


def setup_inputs(seed: int = 0) -> dict:
    keys = jax.random.split(jax.random.key(seed), 3)
    populations = draw_populations(jax.random.fold_in(keys[2], 71), 0)
    fluid = draw_fluid(jax.random.fold_in(keys[2], 71), 0)
    return dict(populations=populations, fluid=fluid)


VELOCITIES = ((0, 0, 0), (1, 0, 0), (-1, 0, 0), (0, 1, 0), (0, -1, 0), (0, 0, 1), (0, 0, -1),
              (1, 1, 0), (-1, -1, 0), (1, -1, 0), (-1, 1, 0), (1, 0, 1), (-1, 0, -1), (1, 0, -1),
              (-1, 0, 1), (0, 1, 1), (0, -1, -1), (0, 1, -1), (0, -1, 1))
WEIGHTS = (1.0 / 3.0,) + (1.0 / 18.0,) * 6 + (1.0 / 36.0,) * 12
OPPOSITE = (0, 2, 1, 4, 3, 6, 5, 8, 7, 10, 9, 12, 11, 14, 13, 16, 15, 18, 17)
relax_rate = 1.0 / 0.6
velocity_scale = 0.002
spread_side = 0.25
spread_middle = 0.5


def moments(current):
    density = jnp.sum(current, axis=0)
    speeds = []
    for component in range(3):
        total = jnp.zeros_like(density)
        for channel in range(19):
            factor = VELOCITIES[channel][component]
            if factor == 1:
                total = total + current[channel]
            elif factor == -1:
                total = total - current[channel]
        speeds.append(total / density)
    return density, speeds[0], speeds[1], speeds[2]


def collide(current):
    density, speed_x, speed_y, speed_z = moments(current)
    square = speed_x * speed_x + speed_y * speed_y + speed_z * speed_z
    relaxed = []
    for channel in range(19):
        along_x, along_y, along_z = VELOCITIES[channel]
        projected = along_x * speed_x + along_y * speed_y + along_z * speed_z
        balance = WEIGHTS[channel] * density * (1.0 + 3.0 * projected + 4.5 * projected * projected - 1.5 * square)
        relaxed.append(current[channel] - relax_rate * (current[channel] - balance))
    return jnp.stack(relaxed)


def propagate(padded, walls, relaxed):
    size_x, size_y, size_z = relaxed.shape[1], relaxed.shape[2], relaxed.shape[3]
    moved = []
    for channel in range(19):
        along_x, along_y, along_z = VELOCITIES[channel]
        start_x, start_y, start_z = 1 - along_x, 1 - along_y, 1 - along_z
        source = padded[channel, start_x:start_x + size_x, start_y:start_y + size_y, start_z:start_z + size_z]
        open_site = walls[start_x:start_x + size_x, start_y:start_y + size_y, start_z:start_z + size_z]
        moved.append(jnp.where(open_site > 0, source, relaxed[OPPOSITE[channel]]))
    return jnp.stack(moved)


def voxel_sums(current, fluid):
    density, speed_x, speed_y, speed_z = moments(current)
    fluid_float = fluid.astype(jnp.float32)
    stacked = jnp.stack([fluid_float * speed_x, fluid_float * speed_y, fluid_float * speed_z, fluid_float])
    size_x, size_y, size_z = fluid.shape
    return stacked.reshape(4, size_x // 4, 4, size_y // 4, 4, size_z // 4, 4).sum(axis=(2, 4, 6))


def trim(extended, dimension):
    length = extended.shape[dimension] - 2
    return (spread_side * lax.slice_in_dim(extended, 0, length, axis=dimension)
            + spread_middle * lax.slice_in_dim(extended, 1, length + 1, axis=dimension)
            + spread_side * lax.slice_in_dim(extended, 2, length + 2, axis=dimension))


def spread_axis(values, dimension):
    widths = [(1, 1) if other == dimension else (0, 0) for other in range(values.ndim)]
    return trim(jnp.pad(values, widths), dimension)


def reference(populations, fluid):
    walls = jnp.pad(fluid, 1)
    current = populations
    for sweep_index in range(STEPS):
        relaxed = collide(current)
        padded = jnp.pad(relaxed, ((0, 0), (1, 1), (1, 1), (1, 1)))
        current = propagate(padded, walls, relaxed)
    sums = voxel_sums(current, fluid)
    blurred = spread_axis(spread_axis(spread_axis(sums, 1), 2), 3)
    velocity_image = blurred[:3] / jnp.maximum(blurred[3], 1.0) / velocity_scale
    magnitude = blurred[3] / 64.0
    return velocity_image, magnitude
```

```python
import functools

import jax
import jax.numpy as jnp
from jax import lax
from jax.experimental import pallas as pl
from jax.experimental.pallas import tpu as pltpu
from jax.sharding import PartitionSpec as P

MESH = pl.DeviceIdType.MESH

VELOCITIES = (
    (0, 0, 0),
    (1, 0, 0),
    (-1, 0, 0),
    (0, 1, 0),
    (0, -1, 0),
    (0, 0, 1),
    (0, 0, -1),
    (1, 1, 0),
    (-1, -1, 0),
    (1, -1, 0),
    (-1, 1, 0),
    (1, 0, 1),
    (-1, 0, -1),
    (1, 0, -1),
    (-1, 0, 1),
    (0, 1, 1),
    (0, -1, -1),
    (0, 1, -1),
    (0, -1, 1),
)
OPPOSITE = (0, 2, 1, 4, 3, 6, 5, 8, 7, 10, 9, 12, 11, 14, 13, 16, 15, 18, 17)
ORDER = (9, 1, 11, 13, 7, 3, 15, 17, 10, 2, 14, 12, 8, 4, 18, 16, 0, 5, 6)
SLOT = tuple(ORDER.index(channel) for channel in range(19))
relax_rate = 1.0 / 0.6
velocity_scale = 0.002

NX, NY, NZ = 8, 32, 128
TOP = 8
LAST = TOP + NY - 1
TILES = NY // 8


def moments(f):
    s = [f[i] + f[i + 1] for i in range(1, 19, 2)]
    d = [f[i] - f[i + 1] for i in range(1, 19, 2)]
    rho = (f[0] + s[8]) + ((s[0] + s[1]) + (s[2] + s[3])) + ((s[4] + s[5]) + (s[6] + s[7]))
    mx = d[0] + (d[3] + d[4]) + (d[5] + d[6])
    my = d[1] + (d[3] - d[4]) + (d[7] + d[8])
    mz = d[2] + (d[5] - d[6]) + (d[7] - d[8])
    return rho, mx, my, mz


def collide(f):
    rho, mx, my, mz = moments(f)
    inverse = 1.0 / rho
    ux, uy, uz = mx * inverse, my * inverse, mz * inverse
    base = rho - 1.5 * (mx * ux + my * uy + mz * uz)
    keep = 1.0 - relax_rate
    relaxed = [keep * f[0] + (relax_rate / 3.0) * base]
    vx, vy, vz = 1.5 * ux, 1.5 * uy, 1.5 * uz
    near = (relax_rate / 18.0) * base
    far = (relax_rate / 36.0) * base
    ax, ay, az = (relax_rate / 6.0) * mx, (relax_rate / 6.0) * my, (relax_rate / 6.0) * mz
    bx, by, bz = 0.5 * ax, 0.5 * ay, 0.5 * az
    for channel, level, flow, speed in (
        (1, near, ax, vx),
        (3, near, ay, vy),
        (5, near, az, vz),
        (7, far, bx + by, vx + vy),
        (9, far, bx - by, vx - vy),
        (11, far, bx + bz, vx + vz),
        (13, far, bx - bz, vx - vz),
        (15, far, by + bz, vy + vz),
        (17, far, by - bz, vy - vz),
    ):
        even = level + flow * speed
        relaxed.append(keep * f[channel] + (even + flow))
        relaxed.append(keep * f[channel + 1] + (even - flow))
    return relaxed


def pulled(held, walls, x, tile):
    f = []
    for channel in range(19):
        cx, cy, cz = VELOCITIES[channel]
        rows = pl.ds(TOP + 8 * tile, 8)
        if channel == 0:
            f.append(held[SLOT[0], x + 1, rows, :])
            continue
        from_rows = pl.ds(TOP + 8 * tile - cy, 8)
        source = held[SLOT[channel], x + 1 - cx, from_rows, :]
        if cz:
            source = pltpu.roll(source, cz % NZ, 1)
        open_site = walls[cz % 3, x + 1 - cx, from_rows, :]
        f.append(jnp.where(open_site > 0, source, held[SLOT[OPPOSITE[channel]], x + 1, rows, :]))
    return f


def kernel(
    gx_size,
    gy_size,
    populations,
    fluid,
    velocity_ref,
    magnitude_ref,
    start,
    first,
    second,
    walls,
    sums,
    zmat,
    ymat,
    table,
    beside,
    mixed,
    gathered,
    final,
    load_sem,
    fluid_sem,
    flag_send,
    flag_recv,
    halo_send,
    halo_recv,
    side_send,
    side_recv,
    all_send,
    all_recv,
):
    gx, gy = lax.axis_index("gx"), lax.axis_index("gy")
    right, left = lax.rem(gx + 1, gx_size), lax.rem(gx + gx_size - 1, gx_size)
    above, below = lax.rem(gy + 1, gy_size), lax.rem(gy + gy_size - 1, gy_size)

    fluid_copy = pltpu.make_async_copy(fluid, walls.at[0, pl.ds(1, NX), pl.ds(TOP, NY), :], fluid_sem)
    fluid_copy.start()

    def load(x):
        return pltpu.make_async_copy(populations.at[:, x], start.at[:, x], load_sem.at[x])

    load_order = (7, 0, 1, 2, 3, 4, 5, 6)
    for x in load_order:
        load(x).start()

    barrier = pltpu.get_barrier_semaphore()
    greeted = [(a, b) for a in (left, gx, right) for b in (below, gy, above) if not (a is gx and b is gy)]
    for target in greeted:
        pl.semaphore_signal(barrier, inc=1, device_id=target, device_id_type=MESH)

    def greet(step, carry):
        pl.semaphore_signal(
            barrier, inc=1, device_id=(gx, lax.rem(gy + step, gy_size)), device_id_type=MESH
        )
        return carry

    lax.fori_loop(2, gy_size - 1, greet, 0)

    def lane_walls(slab, rows):
        flags = walls[0, slab, rows, :]
        lane = lax.broadcasted_iota(jnp.int32, flags.shape, flags.ndim - 1)
        walls[1, slab, rows, :] = jnp.where(lane == 0, 0, pltpu.roll(flags, 1, flags.ndim - 1))
        walls[2, slab, rows, :] = jnp.where(lane == NZ - 1, 0, pltpu.roll(flags, NZ - 1, flags.ndim - 1))

    row = lax.broadcasted_iota(jnp.int32, (32, NZ), 0)
    lane = lax.broadcasted_iota(jnp.int32, (32, NZ), 1)
    distance = jnp.abs(2 * (row % 16) + row // 16 - lane // 4)
    zmat[...] = jnp.where(distance == 0, 0.5, jnp.where(distance == 1, 0.25, 0.0)).astype(jnp.float32)

    def y_rows(step, carry):
        at = pl.multiple_of(8 * step, 8)
        row = lax.broadcasted_iota(jnp.int32, (8, 128), 0) + at
        lane = lax.broadcasted_iota(jnp.int32, (8, 128), 1)
        for z in range(2):
            hit = (row // 32 == 7 - lane // 16) & ((row % 32) // 4 == lane % 8) & ((lane // 8) % 2 == 1 - z)
            ymat[z, pl.ds(at, 8), :] = jnp.where(hit, 1.0, 0.0).astype(jnp.float32)
        return carry

    lax.fori_loop(0, 32, y_rows, 0)
    sums[...] = jnp.zeros(sums.shape, jnp.float32)

    fluid_copy.wait()

    def wall_slab(slab, carry):
        for tile in range(TILES):
            lane_walls(slab, pl.ds(TOP + 8 * tile, 8))
        return carry

    lax.fori_loop(1, NX + 1, wall_slab, 0)

    pl.semaphore_wait(barrier, 8 + gy_size - 3)

    def remote(buffer, source, target, send, recv, device):
        return pltpu.make_async_remote_copy(
            src_ref=buffer.at[source],
            dst_ref=buffer.at[target],
            send_sem=send,
            recv_sem=recv,
            device_id=device,
            device_id_type=MESH,
        )

    inner, block = pl.ds(1, NX), pl.ds(TOP, NY)
    low, high = pl.ds(TOP - 1, 1), pl.ds(LAST + 1, 1)
    bottom, top = pl.ds(TOP, 1), pl.ds(LAST, 1)

    def sides():
        x_faces = [
            (pl.ds(0, 5), (NX, block), (0, block), (right, gy)),
            (pl.ds(8, 5), (1, block), (NX + 1, block), (left, gy)),
            (pl.ds(4, 1), (NX, top), (0, low), (right, above)),
            (pl.ds(0, 1), (NX, bottom), (0, high), (right, below)),
            (pl.ds(8, 1), (1, top), (NX + 1, low), (left, above)),
            (pl.ds(12, 1), (1, bottom), (NX + 1, high), (left, below)),
        ]
        y_faces = [
            (pl.ds(4, 5), (inner, top), (inner, low), (gx, above)),
            (pl.ds(12, 4), (inner, bottom), (inner, high), (gx, below)),
            (pl.ds(0, 1), (inner, bottom), (inner, high), (gx, below)),
        ]
        return x_faces, y_faces

    x_faces, y_faces = sides()
    flags = [
        remote(walls, (0, *s), (0, *t), flag_send.at[i], flag_recv.at[i], device)
        for i, (_, s, t, device) in enumerate(x_faces + y_faces[:2])
    ]
    for copy in flags:
        copy.start()

    def halo(buffer, which):
        copies = [
            remote(buffer, (slots, *s), (slots, *t), halo_send.at[which, i], halo_recv.at[which, i], device)
            for i, (slots, s, t, device) in enumerate(x_faces + y_faces)
        ]
        return copies[:6], copies[6:]

    first_x, first_y = halo(first, 0)
    second_x, second_y = halo(second, 1)

    def relax_tile(x, tile):
        rows = pl.ds(8 * tile, 8)
        relaxed = collide([start[channel, x, rows, :] for channel in range(19)])
        for channel in range(19):
            first[SLOT[channel], x + 1, pl.ds(TOP + 8 * tile, 8), :] = relaxed[channel]

    def step_tile(x, tile):
        relaxed = collide(pulled(first, walls, x, tile))
        for channel in range(19):
            second[SLOT[channel], x + 1, pl.ds(TOP + 8 * tile, 8), :] = relaxed[channel]

    def sum_tile(x, tile):
        rho, mx, my, mz = moments(pulled(second, walls, x, tile))
        here = walls[0, x + 1, pl.ds(TOP + 8 * tile, 8), :].astype(jnp.float32)
        scale = here / rho
        for component, value in enumerate((mx * scale, my * scale, mz * scale, here)):
            rows = pl.ds(pl.multiple_of(component * 64 + (x // 4) * 32 + 8 * tile, 8), 8)
            sums[rows, :] = sums[rows, :] + value

    def over_slabs(body, edge, tiles):
        def edge_slab(step, carry):
            for tile in tiles:
                body((NX - 1) * (1 - step), tile)
            return carry

        def inner_slab(x, carry):
            for tile in tiles:
                body(x, tile)
            return carry

        if edge:
            lax.fori_loop(0, 2, edge_slab, 0)
        else:
            lax.fori_loop(1, NX - 1, inner_slab, 0)

    every, outer, middle = range(TILES), (0, TILES - 1), range(1, TILES - 1)

    load(7).wait()
    load(0).wait()
    over_slabs(relax_tile, True, every)
    for copy in first_x:
        copy.start()
    for x in range(1, NX - 1):
        load(x).wait()
    over_slabs(relax_tile, False, outer)
    for copy in first_y:
        copy.start()
    over_slabs(relax_tile, False, middle)

    over_slabs(step_tile, False, middle)

    for copy in flags:
        copy.wait_recv()

    @pl.when(gx == 0)
    def _():
        walls[0, 0, pl.ds(TOP - 1, NY + 2), :] = jnp.zeros((NY + 2, NZ), jnp.int32)

    @pl.when(gx == gx_size - 1)
    def _():
        walls[0, NX + 1, pl.ds(TOP - 1, NY + 2), :] = jnp.zeros((NY + 2, NZ), jnp.int32)

    @pl.when(gy == 0)
    def _():
        walls[0, :, low, :] = jnp.zeros((NX + 2, 1, NZ), jnp.int32)

    @pl.when(gy == gy_size - 1)
    def _():
        walls[0, :, high, :] = jnp.zeros((NX + 2, 1, NZ), jnp.int32)

    for slab in (0, NX + 1):
        wall_slab(slab, 0)

    def wall_rows(slab, carry):
        lane_walls(slab, low)
        lane_walls(slab, high)
        return carry

    lax.fori_loop(0, NX + 2, wall_rows, 0)

    for copy in first_x + first_y:
        copy.wait_recv()
    over_slabs(step_tile, True, every)
    for copy in second_x:
        copy.start()
    over_slabs(step_tile, False, outer)
    for copy in second_y:
        copy.start()

    over_slabs(sum_tile, False, middle)
    for copy in second_x + second_y:
        copy.wait_recv()
    over_slabs(sum_tile, True, every)
    over_slabs(sum_tile, False, outer)

    exact = dict(preferred_element_type=jnp.float32, precision=lax.Precision.HIGHEST)
    blurred_z = lax.dot_general(zmat[...], sums[...], (((1,), (1,)), ((), ())), **exact)
    table[...] = jnp.dot(blurred_z[:16], ymat[0], **exact) + jnp.dot(blurred_z[16:], ymat[1], **exact)

    to_right = pltpu.make_async_remote_copy(
        src_ref=table,
        dst_ref=beside.at[0],
        send_sem=side_send.at[0],
        recv_sem=side_recv.at[0],
        device_id=(right, gy),
        device_id_type=MESH,
    )
    to_left = pltpu.make_async_remote_copy(
        src_ref=table,
        dst_ref=beside.at[1],
        send_sem=side_send.at[1],
        recv_sem=side_recv.at[1],
        device_id=(left, gy),
        device_id_type=MESH,
    )
    to_right.start()
    to_left.start()
    to_right.wait_recv()
    to_left.wait_recv()
    own = table[...]
    lane = lax.broadcasted_iota(jnp.int32, own.shape, 1)
    lower = (lane // 16) % 2 == 1
    has_left = jnp.where(gx > 0, 0.25, 0.0)
    has_right = jnp.where(gx < gx_size - 1, 0.25, 0.0)
    swapped = jnp.where(lower, pltpu.roll(own, 16, 1), pltpu.roll(own, 128 - 16, 1))
    outside = jnp.where(
        lower,
        has_left * pltpu.roll(beside[0], 16, 1),
        has_right * pltpu.roll(beside[1], 128 - 16, 1),
    )
    mixed[...] = pltpu.roll(0.5 * own + 0.25 * swapped + outside, lax.rem(8 * gy + 8, 128), 1)

    def exchange(step):
        partner = lax.rem(gy + step, gy_size)
        return pltpu.make_async_remote_copy(
            src_ref=mixed.at[pl.ds(partner, 1)],
            dst_ref=gathered.at[pl.ds(gy, 1)],
            send_sem=all_send,
            recv_sem=all_recv,
            device_id=(gx, partner),
            device_id_type=MESH,
        )

    def send(step, carry):
        exchange(step).start()
        return carry

    lax.fori_loop(1, gy_size, send, 0)
    gathered[pl.ds(gy, 1), :] = mixed[pl.ds(gy, 1), :]
    everyone = pltpu.make_async_remote_copy(
        src_ref=mixed.at[pl.ds(0, gy_size - 1)],
        dst_ref=gathered.at[pl.ds(0, gy_size - 1)],
        send_sem=all_send,
        recv_sem=all_recv,
        device_id=(gx, above),
        device_id_type=MESH,
    )
    everyone.wait_recv()

    lane = lax.broadcasted_iota(jnp.int32, (8, 128), 1)
    halves = [jnp.zeros((8, 128), jnp.float32) for _ in range(2)]
    for source in range(gy_size):
        spread = jnp.broadcast_to(gathered[pl.ds(source, 1), :], (8, 128))
        for half in range(2):
            turned = pltpu.roll(spread, 64 * half, 1, stride=8, stride_axis=0)
            halves[half] = jnp.where(lane // 8 == source, turned, halves[half])
    whole = jnp.concatenate(halves, axis=0)
    lane = lax.broadcasted_iota(jnp.int32, (16, 128), 1)
    before = jnp.where(lane == 0, 0.0, pltpu.roll(whole, 1, 1))
    after = jnp.where(lane == 127, 0.0, pltpu.roll(whole, 127, 1))
    final[...] = 0.5 * whole + 0.25 * (before + after)
    for x in range(2):
        fraction = final[pl.ds(12 + 2 * x, 2), :]
        divisor = jnp.maximum(fraction, 1.0)
        for component in range(3):
            velocity_ref[component, x] = final[pl.ds(4 * component + 2 * x, 2), :] / divisor / velocity_scale
        magnitude_ref[x] = fraction / 64.0

    for copy in flags + first_x + first_y + second_x + second_y + [to_right, to_left]:
        copy.wait_send()
    everyone.wait_send()


def local(gx_size, gy_size, populations, fluid):
    padded = (NX + 2, NY + 2 * TOP, NZ)
    vmem, dma = pltpu.VMEM, pltpu.SemaphoreType.DMA
    f32 = jnp.float32
    velocity, magnitude = pl.pallas_call(
        functools.partial(kernel, gx_size, gy_size),
        out_shape=(
            jax.ShapeDtypeStruct((3, 2, 2, 128), f32),
            jax.ShapeDtypeStruct((2, 2, 128), f32),
        ),
        in_specs=[pl.BlockSpec(memory_space=pl.ANY)] * 2,
        out_specs=(pl.BlockSpec(memory_space=pltpu.VMEM),) * 2,
        scratch_shapes=[
            vmem((19, NX, NY, NZ), f32),
            vmem((19, *padded), f32),
            vmem((19, *padded), f32),
            vmem((3, *padded), jnp.int32),
            vmem((256, 128), f32),
            vmem((32, 128), f32),
            vmem((2, 256, 128), f32),
            vmem((16, 128), f32),
            vmem((2, 16, 128), f32),
            vmem((16, 128), f32),
            vmem((16, 128), f32),
            vmem((16, 128), f32),
            dma((8,)),
            dma,
            dma((8,)),
            dma((8,)),
            dma((2, 9)),
            dma((2, 9)),
            dma((2,)),
            dma((2,)),
            dma,
            dma,
        ],
        compiler_params=pltpu.CompilerParams(
            collective_id=0, has_side_effects=True, vmem_limit_bytes=40 * 1024 * 1024
        ),
    )(populations, fluid)
    return jnp.swapaxes(velocity, 2, 3), jnp.swapaxes(magnitude, 1, 2)


def solution(mesh):
    return jax.shard_map(
        functools.partial(local, mesh.shape["gx"], mesh.shape["gy"]),
        mesh=mesh,
        in_specs=(P(None, "gx", "gy", None), P("gx", "gy", None)),
        out_specs=(P(None, "gx", None, "gy"), P("gx", None, "gy")),
        check_vma=False,
    )
```

```python
import functools

import jax
import jax.numpy as jnp
from jax import lax
from jax.experimental import pallas as pl
from jax.experimental.pallas import tpu as pltpu
from jax.sharding import PartitionSpec as P

MESH = pl.DeviceIdType.MESH

VELOCITIES = (
    (0, 0, 0),
    (1, 0, 0),
    (-1, 0, 0),
    (0, 1, 0),
    (0, -1, 0),
    (0, 0, 1),
    (0, 0, -1),
    (1, 1, 0),
    (-1, -1, 0),
    (1, -1, 0),
    (-1, 1, 0),
    (1, 0, 1),
    (-1, 0, -1),
    (1, 0, -1),
    (-1, 0, 1),
    (0, 1, 1),
    (0, -1, -1),
    (0, 1, -1),
    (0, -1, 1),
)
OPPOSITE = (0, 2, 1, 4, 3, 6, 5, 8, 7, 10, 9, 12, 11, 14, 13, 16, 15, 18, 17)
ORDER = (9, 1, 11, 13, 7, 3, 15, 17, 10, 2, 14, 12, 8, 4, 18, 16, 0, 5, 6)
SLOT = tuple(ORDER.index(channel) for channel in range(19))
relax_rate = 1.0 / 0.6
velocity_scale = 0.002

NX, NY, NZ = 8, 32, 128
TOP = 8
LAST = TOP + NY - 1
TILES = NY // 8


def moments(f):
    s = [f[i] + f[i + 1] for i in range(1, 19, 2)]
    d = [f[i] - f[i + 1] for i in range(1, 19, 2)]
    rho = (f[0] + s[8]) + ((s[0] + s[1]) + (s[2] + s[3])) + ((s[4] + s[5]) + (s[6] + s[7]))
    mx = d[0] + (d[3] + d[4]) + (d[5] + d[6])
    my = d[1] + (d[3] - d[4]) + (d[7] + d[8])
    mz = d[2] + (d[5] - d[6]) + (d[7] - d[8])
    return rho, mx, my, mz


def collide(f):
    rho, mx, my, mz = moments(f)
    inverse = 1.0 / rho
    ux, uy, uz = mx * inverse, my * inverse, mz * inverse
    base = rho - 1.5 * (mx * ux + my * uy + mz * uz)
    keep = 1.0 - relax_rate
    relaxed = [keep * f[0] + (relax_rate / 3.0) * base]
    vx, vy, vz = 1.5 * ux, 1.5 * uy, 1.5 * uz
    near = (relax_rate / 18.0) * base
    far = (relax_rate / 36.0) * base
    ax, ay, az = (relax_rate / 6.0) * mx, (relax_rate / 6.0) * my, (relax_rate / 6.0) * mz
    bx, by, bz = 0.5 * ax, 0.5 * ay, 0.5 * az
    for channel, level, flow, speed in (
        (1, near, ax, vx),
        (3, near, ay, vy),
        (5, near, az, vz),
        (7, far, bx + by, vx + vy),
        (9, far, bx - by, vx - vy),
        (11, far, bx + bz, vx + vz),
        (13, far, bx - bz, vx - vz),
        (15, far, by + bz, vy + vz),
        (17, far, by - bz, vy - vz),
    ):
        even = level + flow * speed
        relaxed.append(keep * f[channel] + (even + flow))
        relaxed.append(keep * f[channel + 1] + (even - flow))
    return relaxed


def pulled(held, walls, x, tile):
    f = []
    for channel in range(19):
        cx, cy, cz = VELOCITIES[channel]
        rows = pl.ds(TOP + 8 * tile, 8)
        if channel == 0:
            f.append(held[SLOT[0], x + 1, rows, :])
            continue
        from_rows = pl.ds(TOP + 8 * tile - cy, 8)
        source = held[SLOT[channel], x + 1 - cx, from_rows, :]
        if cz:
            source = pltpu.roll(source, cz % NZ, 1)
        open_site = walls[cz % 3, x + 1 - cx, from_rows, :]
        f.append(jnp.where(open_site > 0, source, held[SLOT[OPPOSITE[channel]], x + 1, rows, :]))
    return f


def kernel(
    gx_size,
    gy_size,
    populations,
    fluid,
    velocity_ref,
    magnitude_ref,
    start,
    first,
    second,
    walls,
    sums,
    zmat,
    ymat,
    table,
    gathered,
    mixed,
    final,
    load_sem,
    fluid_sem,
    flag_send,
    flag_recv,
    halo_send,
    halo_recv,
    all_send,
    all_recv,
):
    gx, gy = lax.axis_index("gx"), lax.axis_index("gy")
    has_left, has_right = gx > 0, gx < gx_size - 1
    has_below, has_above = gy > 0, gy < gy_size - 1

    def load(x):
        return pltpu.make_async_copy(populations.at[:, x], start.at[:, x], load_sem.at[x])

    load(7).start()
    load(0).start()
    fluid_copy = pltpu.make_async_copy(fluid, walls.at[0, pl.ds(1, NX), pl.ds(TOP, NY), :], fluid_sem)
    fluid_copy.start()
    for x in range(1, NX - 1):
        load(x).start()

    barrier = pltpu.get_barrier_semaphore()

    def greet(x, begin):
        def one(step, carry):
            target = (x, lax.rem(gy + step, gy_size))
            pl.semaphore_signal(barrier, inc=1, device_id=target, device_id_type=MESH)
            return carry

        lax.fori_loop(begin, gy_size, one, 0)

    greet(gx, 1)
    pl.when(has_left)(lambda: greet(gx - 1, 0))
    pl.when(has_right)(lambda: greet(gx + 1, 0))

    def lane_walls(slab, rows):
        flags = walls[0, slab, rows, :]
        lane = lax.broadcasted_iota(jnp.int32, flags.shape, flags.ndim - 1)
        walls[1, slab, rows, :] = jnp.where(lane == 0, 0, pltpu.roll(flags, 1, flags.ndim - 1))
        walls[2, slab, rows, :] = jnp.where(lane == NZ - 1, 0, pltpu.roll(flags, NZ - 1, flags.ndim - 1))

    def wall_slab(slab, carry):
        for tile in range(TILES):
            lane_walls(slab, pl.ds(TOP + 8 * tile, 8))
        return carry

    def wall_rows(slab, carry):
        lane_walls(slab, low)
        lane_walls(slab, high)
        return carry

    inner, block = pl.ds(1, NX), pl.ds(TOP, NY)
    low, high = pl.ds(TOP - 1, 1), pl.ds(LAST + 1, 1)
    bottom, top = pl.ds(TOP, 1), pl.ds(LAST, 1)

    x_sides = [
        (pl.ds(0, 5), (NX, block), (0, block), (1, 0), has_right, has_left),
        (pl.ds(8, 5), (1, block), (NX + 1, block), (-1, 0), has_left, has_right),
        (pl.ds(4, 1), (NX, top), (0, low), (1, 1), has_right & has_above, has_left & has_below),
        (pl.ds(0, 1), (NX, bottom), (0, high), (1, -1), has_right & has_below, has_left & has_above),
        (pl.ds(8, 1), (1, top), (NX + 1, low), (-1, 1), has_left & has_above, has_right & has_below),
        (pl.ds(12, 1), (1, bottom), (NX + 1, high), (-1, -1), has_left & has_below, has_right & has_above),
    ]
    y_sides = [
        (pl.ds(4, 5), (inner, top), (inner, low), (0, 1), has_above, has_below),
        (pl.ds(12, 4), (inner, bottom), (inner, high), (0, -1), has_below, has_above),
        (pl.ds(0, 1), (inner, bottom), (inner, high), (0, -1), has_below, has_above),
    ]

    class Sides:
        def __init__(self, buffer, sides, slots, send, recv, offset):
            self.copies = [
                (
                    pltpu.make_async_remote_copy(
                        src_ref=buffer.at[(channels if slots else 0, *source)],
                        dst_ref=buffer.at[(channels if slots else 0, *target)],
                        send_sem=send.at[offset + i],
                        recv_sem=recv.at[offset + i],
                        device_id=(gx + way[0], gy + way[1]),
                        device_id_type=MESH,
                    ),
                    sent,
                    arrives,
                )
                for i, (channels, source, target, way, sent, arrives) in enumerate(sides)
            ]

        def start(self):
            for copy, sent, _ in self.copies:
                pl.when(sent)(copy.start)

        def wait_recv(self):
            for copy, _, arrives in self.copies:
                pl.when(arrives)(copy.wait_recv)

        def wait_send(self):
            for copy, sent, _ in self.copies:
                pl.when(sent)(copy.wait_send)

    flags = Sides(walls, x_sides + y_sides[:2], False, flag_send, flag_recv, 0)
    first_x = Sides(first, x_sides, True, halo_send.at[0], halo_recv.at[0], 0)
    first_y = Sides(first, y_sides, True, halo_send.at[0], halo_recv.at[0], 6)
    second_x = Sides(second, x_sides, True, halo_send.at[1], halo_recv.at[1], 0)
    second_y = Sides(second, y_sides, True, halo_send.at[1], halo_recv.at[1], 6)

    def relax_tile(x, tile):
        rows = pl.ds(8 * tile, 8)
        relaxed = collide([start[channel, x, rows, :] for channel in range(19)])
        for channel in range(19):
            first[SLOT[channel], x + 1, pl.ds(TOP + 8 * tile, 8), :] = relaxed[channel]

    def step_tile(x, tile):
        relaxed = collide(pulled(first, walls, x, tile))
        for channel in range(19):
            second[SLOT[channel], x + 1, pl.ds(TOP + 8 * tile, 8), :] = relaxed[channel]

    def sum_tile(x, tile):
        rho, mx, my, mz = moments(pulled(second, walls, x, tile))
        here = walls[0, x + 1, pl.ds(TOP + 8 * tile, 8), :].astype(jnp.float32)
        scale = here / rho
        for component, value in enumerate((mx * scale, my * scale, mz * scale, here)):
            rows = pl.ds(pl.multiple_of(component * 64 + (x // 4) * 32 + 8 * tile, 8), 8)
            sums[rows, :] = sums[rows, :] + value

    def over_slabs(body, edge, tiles):
        def edge_slab(step, carry):
            for tile in tiles:
                body((NX - 1) * (1 - step), tile)
            return carry

        def inner_slab(x, carry):
            for tile in tiles:
                body(x, tile)
            return carry

        if edge:
            lax.fori_loop(0, 2, edge_slab, 0)
        else:
            lax.fori_loop(1, NX - 1, inner_slab, 0)

    every, outer, middle = range(TILES), (0, TILES - 1), range(1, TILES - 1)

    load(7).wait()
    load(0).wait()
    over_slabs(relax_tile, True, every)
    columns = has_left.astype(jnp.int32) + has_right.astype(jnp.int32)
    pl.semaphore_wait(barrier, gy_size - 1 + gy_size * columns)
    first_x.start()
    fluid_copy.wait()
    flags.start()
    for x in range(1, NX - 1):
        load(x).wait()
    over_slabs(relax_tile, False, outer)
    first_y.start()
    over_slabs(relax_tile, False, middle)

    @pl.when(gx == 0)
    def _():
        walls[0, 0, pl.ds(TOP - 1, NY + 2), :] = jnp.zeros((NY + 2, NZ), jnp.int32)
        gathered[1] = jnp.zeros((16, 128), jnp.float32)

    @pl.when(gx == gx_size - 1)
    def _():
        walls[0, NX + 1, pl.ds(TOP - 1, NY + 2), :] = jnp.zeros((NY + 2, NZ), jnp.int32)
        gathered[2] = jnp.zeros((16, 128), jnp.float32)

    lax.fori_loop(1, NX + 1, wall_slab, 0)
    over_slabs(step_tile, False, middle)

    sums[...] = jnp.zeros(sums.shape, jnp.float32)
    row = lax.broadcasted_iota(jnp.int32, (32, NZ), 0)
    lane = lax.broadcasted_iota(jnp.int32, (32, NZ), 1)
    distance = jnp.abs(2 * (row & 15) + (row >> 4) - (lane >> 2))
    zmat[...] = jnp.where(distance == 0, 0.5, jnp.where(distance == 1, 0.25, 0.0)).astype(jnp.float32)

    def y_rows(step, carry):
        at = pl.multiple_of(8 * step, 8)
        row = lax.broadcasted_iota(jnp.int32, (8, 256), 0) + at
        column = lax.broadcasted_iota(jnp.int32, (8, 256), 1)
        hit = (((row >> 3) & 7) == 7 - (column >> 5)) & ((row & 7) == ((column >> 2) & 7))
        ymat[pl.ds(at, 8), :] = jnp.where(hit, 1.0, 0.0).astype(jnp.float32)
        return carry

    lax.fori_loop(0, 16, y_rows, 0)

    flags.wait_recv()

    @pl.when(gy == 0)
    def _():
        walls[0, :, low, :] = jnp.zeros((NX + 2, 1, NZ), jnp.int32)

    @pl.when(gy == gy_size - 1)
    def _():
        walls[0, :, high, :] = jnp.zeros((NX + 2, 1, NZ), jnp.int32)

    for slab in (0, NX + 1):
        wall_slab(slab, 0)
    lax.fori_loop(0, NX + 2, wall_rows, 0)

    first_y.wait_recv()
    over_slabs(step_tile, False, outer)
    first_x.wait_recv()
    over_slabs(step_tile, True, every)
    second_x.start()
    second_y.start()

    over_slabs(sum_tile, False, middle)
    second_y.wait_recv()
    over_slabs(sum_tile, False, outer)
    second_x.wait_recv()
    over_slabs(sum_tile, True, every)

    exact = dict(preferred_element_type=jnp.float32, precision=lax.Precision.HIGHEST)
    over_y = jnp.dot(ymat[...], sums[...], **exact)
    over_z = lax.dot_general(zmat[...], over_y, (((1,), (1,)), ((), ())), **exact)
    lane = lax.broadcasted_iota(jnp.int32, (16, 128), 1)
    table[...] = jnp.where(lane >= 64, over_z[:16], over_z[16:])

    def exchange(place, x, partner):
        return pltpu.make_async_remote_copy(
            src_ref=table.at[pl.ds(partner, 1)],
            dst_ref=gathered.at[place, pl.ds(gy, 1)],
            send_sem=all_send.at[place],
            recv_sem=all_recv.at[place],
            device_id=(x, partner),
            device_id_type=MESH,
        )

    def send(place, x, begin, end):
        def one(step, carry):
            exchange(place, x, lax.rem(gy + step, gy_size)).start()
            return carry

        lax.fori_loop(begin, end, one, 0)

    far = (gy_size // 2 - 3, gy_size // 2 + 4)
    send(0, gx, *far)
    pl.when(has_left)(lambda: send(2, gx - 1, *far))
    pl.when(has_right)(lambda: send(1, gx + 1, *far))
    send(0, gx, far[1], gy_size)
    send(0, gx, 1, far[0])
    pl.when(has_left)(lambda: send(2, gx - 1, far[1], gy_size + far[0]))
    pl.when(has_right)(lambda: send(1, gx + 1, far[1], gy_size + far[0]))
    gathered[0, pl.ds(gy, 1), :] = table[pl.ds(gy, 1), :]

    def everyone(place, count):
        return pltpu.make_async_remote_copy(
            src_ref=table.at[pl.ds(0, count)],
            dst_ref=gathered.at[place, pl.ds(0, count)],
            send_sem=all_send.at[place],
            recv_sem=all_recv.at[place],
            device_id=(gx, lax.rem(gy + 1, gy_size)),
            device_id_type=MESH,
        )

    column, from_left, from_right = everyone(0, gy_size - 1), everyone(1, gy_size), everyone(2, gy_size)
    column.wait_recv()
    pl.when(has_left)(from_left.wait_recv)
    pl.when(has_right)(from_right.wait_recv)

    lower = (lane & 8) != 0
    own = gathered[0]
    beside = jnp.where(
        lower,
        pltpu.roll(own, 8, 1) + pltpu.roll(gathered[1], 8, 1),
        pltpu.roll(own, 120, 1) + pltpu.roll(gathered[2], 120, 1),
    )
    along_x = pltpu.roll(0.5 * own + 0.25 * beside, 8, 1)

    mixed[pl.ds(0, 8), :] = pltpu.roll(along_x[:8], 0, 1, stride=8, stride_axis=0)
    mixed[pl.ds(8, 8), :] = pltpu.roll(along_x[8:], 64, 1, stride=8, stride_axis=0)
    lane = lax.broadcasted_iota(jnp.int32, (8, 128), 1)
    halves = [jnp.zeros((8, 128), jnp.float32) for _ in range(2)]
    for source in range(gy_size):
        spread = jnp.broadcast_to(mixed[pl.ds(source, 1), :], (8, 128))
        for half in range(2):
            turned = pltpu.roll(spread, 64 * half, 1, stride=8, stride_axis=0)
            halves[half] = jnp.where(lane >> 3 == source, turned, halves[half])
    for half in range(2):
        whole = halves[half]
        before = jnp.where(lane == 0, 0.0, pltpu.roll(whole, 1, 1))
        after = jnp.where(lane == 127, 0.0, pltpu.roll(whole, 127, 1))
        final[pl.ds(8 * half, 8), :] = 0.5 * whole + 0.25 * (before + after)
    for x in range(2):
        for z in range(2):
            fraction = final[pl.ds(8 * z + 6 + x, 1), :]
            divisor = jnp.maximum(fraction, 1.0)
            for component in range(3):
                voxels = final[pl.ds(8 * z + 2 * component + x, 1), :]
                velocity_ref[component, x, pl.ds(z, 1), :] = voxels / divisor / velocity_scale
            magnitude_ref[x, pl.ds(z, 1), :] = fraction / 64.0

    for sides in (flags, first_x, first_y, second_x, second_y):
        sides.wait_send()
    column.wait_send()
    pl.when(has_left)(from_right.wait_send)
    pl.when(has_right)(from_left.wait_send)


def local(gx_size, gy_size, populations, fluid):
    padded = (NX + 2, NY + 2 * TOP, NZ)
    vmem, dma = pltpu.VMEM, pltpu.SemaphoreType.DMA
    f32 = jnp.float32
    velocity, magnitude = pl.pallas_call(
        functools.partial(kernel, gx_size, gy_size),
        out_shape=(
            jax.ShapeDtypeStruct((3, 2, 2, 128), f32),
            jax.ShapeDtypeStruct((2, 2, 128), f32),
        ),
        in_specs=[pl.BlockSpec(memory_space=pltpu.HBM)] * 2,
        out_specs=(pl.BlockSpec(memory_space=pltpu.VMEM),) * 2,
        scratch_shapes=[
            vmem((19, NX, NY, NZ), f32),
            vmem((19, *padded), f32),
            vmem((19, *padded), f32),
            vmem((3, *padded), jnp.int32),
            vmem((256, 128), f32),
            vmem((32, 128), f32),
            vmem((128, 256), f32),
            vmem((16, 128), f32),
            vmem((3, 16, 128), f32),
            vmem((16, 128), f32),
            vmem((16, 128), f32),
            dma((8,)),
            dma,
            dma((8,)),
            dma((8,)),
            dma((2, 9)),
            dma((2, 9)),
            dma((3,)),
            dma((3,)),
        ],
        compiler_params=pltpu.CompilerParams(
            collective_id=0, has_side_effects=True, vmem_limit_bytes=58 * 1024 * 1024
        ),
    )(populations, fluid)
    return jnp.swapaxes(velocity, 2, 3), jnp.swapaxes(magnitude, 1, 2)


def solution(mesh):
    return jax.shard_map(
        functools.partial(local, mesh.shape["gx"], mesh.shape["gy"]),
        mesh=mesh,
        in_specs=(P(None, "gx", "gy", None), P("gx", "gy", None)),
        out_specs=(P(None, "gx", None, "gy"), P("gx", None, "gy")),
        check_vma=False,
    )
```

```python
import functools

import jax
import jax.numpy as jnp
from jax import lax
from jax.experimental import pallas as pl
from jax.experimental.pallas import tpu as pltpu
from jax.sharding import PartitionSpec as P

MESH = pl.DeviceIdType.MESH

VELOCITIES = (
    (0, 0, 0),
    (1, 0, 0),
    (-1, 0, 0),
    (0, 1, 0),
    (0, -1, 0),
    (0, 0, 1),
    (0, 0, -1),
    (1, 1, 0),
    (-1, -1, 0),
    (1, -1, 0),
    (-1, 1, 0),
    (1, 0, 1),
    (-1, 0, -1),
    (1, 0, -1),
    (-1, 0, 1),
    (0, 1, 1),
    (0, -1, -1),
    (0, 1, -1),
    (0, -1, 1),
)
OPPOSITE = (0, 2, 1, 4, 3, 6, 5, 8, 7, 10, 9, 12, 11, 14, 13, 16, 15, 18, 17)
ORDER = (9, 1, 11, 13, 7, 3, 15, 17, 10, 2, 14, 12, 8, 4, 18, 16, 0, 5, 6)
SLOT = tuple(ORDER.index(channel) for channel in range(19))
relax_rate = 1.0 / 0.6
velocity_scale = 0.002

NX, NY, NZ = 8, 32, 128
TOP = 8
LAST = TOP + NY - 1
TILES = NY // 8


def moments(f):
    s = [f[i] + f[i + 1] for i in range(1, 19, 2)]
    d = [f[i] - f[i + 1] for i in range(1, 19, 2)]
    rho = (f[0] + s[8]) + ((s[0] + s[1]) + (s[2] + s[3])) + ((s[4] + s[5]) + (s[6] + s[7]))
    mx = d[0] + (d[3] + d[4]) + (d[5] + d[6])
    my = d[1] + (d[3] - d[4]) + (d[7] + d[8])
    mz = d[2] + (d[5] - d[6]) + (d[7] - d[8])
    return rho, mx, my, mz


def collide(f):
    rho, mx, my, mz = moments(f)
    inverse = 1.0 / rho
    ux, uy, uz = mx * inverse, my * inverse, mz * inverse
    base = rho - 1.5 * (mx * ux + my * uy + mz * uz)
    keep = 1.0 - relax_rate
    relaxed = [keep * f[0] + (relax_rate / 3.0) * base]
    vx, vy, vz = 1.5 * ux, 1.5 * uy, 1.5 * uz
    near = (relax_rate / 18.0) * base
    far = (relax_rate / 36.0) * base
    ax, ay, az = (relax_rate / 6.0) * mx, (relax_rate / 6.0) * my, (relax_rate / 6.0) * mz
    bx, by, bz = 0.5 * ax, 0.5 * ay, 0.5 * az
    for channel, level, flow, speed in (
        (1, near, ax, vx),
        (3, near, ay, vy),
        (5, near, az, vz),
        (7, far, bx + by, vx + vy),
        (9, far, bx - by, vx - vy),
        (11, far, bx + bz, vx + vz),
        (13, far, bx - bz, vx - vz),
        (15, far, by + bz, vy + vz),
        (17, far, by - bz, vy - vz),
    ):
        even = level + flow * speed
        relaxed.append(keep * f[channel] + (even + flow))
        relaxed.append(keep * f[channel + 1] + (even - flow))
    return relaxed


def pulled(held, walls, x, tile):
    f = []
    for channel in range(19):
        cx, cy, cz = VELOCITIES[channel]
        rows = pl.ds(TOP + 8 * tile, 8)
        if channel == 0:
            f.append(held[SLOT[0], x + 1, rows, :])
            continue
        from_rows = pl.ds(TOP + 8 * tile - cy, 8)
        source = held[SLOT[channel], x + 1 - cx, from_rows, :]
        if cz:
            source = pltpu.roll(source, cz % NZ, 1)
        open_site = walls[cz % 3, x + 1 - cx, from_rows, :]
        f.append(jnp.where(open_site > 0, source, held[SLOT[OPPOSITE[channel]], x + 1, rows, :]))
    return f


def kernel(
    gx_size,
    gy_size,
    populations,
    fluid,
    velocity_ref,
    magnitude_ref,
    start,
    first,
    second,
    walls,
    sums,
    zmat,
    ymat,
    table,
    gathered,
    mixed,
    final,
    ready,
    load_sem,
    fluid_sem,
    flag_send,
    flag_recv,
    halo_send,
    halo_recv,
    all_send,
    all_recv,
):
    gx, gy = lax.axis_index("gx"), lax.axis_index("gy")
    has_left, has_right = gx > 0, gx < gx_size - 1
    has_below, has_above = gy > 0, gy < gy_size - 1

    def load(x):
        return pltpu.make_async_copy(populations.at[:, x], start.at[:, x], load_sem.at[x])

    fluid_copy = pltpu.make_async_copy(fluid, walls.at[0, pl.ds(1, NX), pl.ds(TOP, NY), :], fluid_sem)
    load(7).start()
    load(0).start()
    fluid_copy.start()
    for x in range(1, NX - 1):
        load(x).start()

    def number(*conditions):
        return sum(condition.astype(jnp.int32) for condition in conditions)

    barrier = pltpu.get_barrier_semaphore()
    beside_x = ((-1, has_left), (0, None), (1, has_right))
    beside_y = ((-1, has_below), (0, None), (1, has_above))
    for dx, in_x in beside_x:
        for dy, in_y in beside_y:
            if dx == 0 and dy == 0:
                continue
            there = in_y if in_x is None else in_x if in_y is None else in_x & in_y

            @pl.when(there)
            def _():
                pl.semaphore_signal(barrier, inc=1, device_id=(gx + dx, gy + dy), device_id_type=MESH)

    def tell(stage):
        for way in (-(2**stage), 2**stage):

            @pl.when((gy + way >= 0) & (gy + way < gy_size))
            def _():
                pl.semaphore_signal(ready.at[stage], inc=1, device_id=(gx, gy + way), device_id_type=MESH)

    def hear(stage):
        pl.semaphore_wait(ready.at[stage], number(gy >= 2**stage, gy + 2**stage < gy_size))

    def lane_walls(slab, rows):
        flags = walls[0, slab, rows, :]
        lane = lax.broadcasted_iota(jnp.int32, flags.shape, flags.ndim - 1)
        walls[1, slab, rows, :] = jnp.where(lane == 0, 0, pltpu.roll(flags, 1, flags.ndim - 1))
        walls[2, slab, rows, :] = jnp.where(lane == NZ - 1, 0, pltpu.roll(flags, NZ - 1, flags.ndim - 1))

    def wall_slab(slab, carry):
        for tile in range(TILES):
            lane_walls(slab, pl.ds(TOP + 8 * tile, 8))
        return carry

    inner, block = pl.ds(1, NX), pl.ds(TOP, NY)
    low, high = pl.ds(TOP - 1, 1), pl.ds(LAST + 1, 1)
    bottom, top = pl.ds(TOP, 1), pl.ds(LAST, 1)

    x_sides = [
        (pl.ds(0, 5), (NX, block), (0, block), (1, 0), has_right, has_left),
        (pl.ds(8, 5), (1, block), (NX + 1, block), (-1, 0), has_left, has_right),
        (pl.ds(4, 1), (NX, top), (0, low), (1, 1), has_right & has_above, has_left & has_below),
        (pl.ds(0, 1), (NX, bottom), (0, high), (1, -1), has_right & has_below, has_left & has_above),
        (pl.ds(8, 1), (1, top), (NX + 1, low), (-1, 1), has_left & has_above, has_right & has_below),
        (pl.ds(12, 1), (1, bottom), (NX + 1, high), (-1, -1), has_left & has_below, has_right & has_above),
    ]
    y_sides = [
        (pl.ds(4, 5), (inner, top), (inner, low), (0, 1), has_above, has_below),
        (pl.ds(12, 4), (inner, bottom), (inner, high), (0, -1), has_below, has_above),
        (pl.ds(0, 1), (inner, bottom), (inner, high), (0, -1), has_below, has_above),
    ]

    class Sides:
        def __init__(self, buffer, sides, slots, send, recv, offset):
            self.copies = [
                (
                    pltpu.make_async_remote_copy(
                        src_ref=buffer.at[(channels if slots else 0, *source)],
                        dst_ref=buffer.at[(channels if slots else 0, *target)],
                        send_sem=send.at[offset + i],
                        recv_sem=recv.at[offset + i],
                        device_id=(gx + way[0], gy + way[1]),
                        device_id_type=MESH,
                    ),
                    sent,
                    arrives,
                )
                for i, (channels, source, target, way, sent, arrives) in enumerate(sides)
            ]

        def start(self, begin=0, end=None):
            for copy, sent, _ in self.copies[begin:end]:
                pl.when(sent)(copy.start)

        def wait_recv(self):
            for copy, _, arrives in self.copies:
                pl.when(arrives)(copy.wait_recv)

        def wait_send(self):
            for copy, sent, _ in self.copies:
                pl.when(sent)(copy.wait_send)

    flags = Sides(walls, x_sides + y_sides[:2], False, flag_send, flag_recv, 0)
    first_x = Sides(first, x_sides, True, halo_send.at[0], halo_recv.at[0], 0)
    first_y = Sides(first, y_sides, True, halo_send.at[0], halo_recv.at[0], 6)
    second_x = Sides(second, x_sides, True, halo_send.at[1], halo_recv.at[1], 0)
    second_y = Sides(second, y_sides, True, halo_send.at[1], halo_recv.at[1], 6)

    def relax_tile(x, tile):
        rows = pl.ds(8 * tile, 8)
        relaxed = collide([start[channel, x, rows, :] for channel in range(19)])
        for channel in range(19):
            first[SLOT[channel], x + 1, pl.ds(TOP + 8 * tile, 8), :] = relaxed[channel]

    def step_tile(x, tile):
        relaxed = collide(pulled(first, walls, x, tile))
        for channel in range(19):
            second[SLOT[channel], x + 1, pl.ds(TOP + 8 * tile, 8), :] = relaxed[channel]

    def sum_tile(x, tile):
        rho, mx, my, mz = moments(pulled(second, walls, x, tile))
        here = walls[0, x + 1, pl.ds(TOP + 8 * tile, 8), :].astype(jnp.float32)
        scale = here / rho
        for component, value in enumerate((mx * scale, my * scale, mz * scale, here)):
            rows = pl.ds(pl.multiple_of(component * 64 + (x // 4) * 32 + 8 * tile, 8), 8)
            sums[rows, :] = sums[rows, :] + value

    def over_slabs(body, edge, tiles):
        def edge_slab(step, carry):
            for tile in tiles:
                body((NX - 1) * (1 - step), tile)
            return carry

        def inner_slab(x, carry):
            for tile in tiles:
                body(x, tile)
            return carry

        if edge:
            lax.fori_loop(0, 2, edge_slab, 0)
        else:
            lax.fori_loop(1, NX - 1, inner_slab, 0)

    every, outer, middle = range(TILES), (0, TILES - 1), range(1, TILES - 1)

    load(7).wait()
    load(0).wait()
    over_slabs(relax_tile, True, every)
    fluid_copy.wait()
    pl.semaphore_wait(barrier, (1 + number(has_left, has_right)) * (1 + number(has_below, has_above)) - 1)
    flags.start(0, 2)
    first_x.start(0, 2)
    flags.start(2)
    first_x.start(2)
    tell(0)
    for x in range(1, NX - 1):
        load(x).wait()
    over_slabs(relax_tile, False, outer)
    first_y.start()
    over_slabs(relax_tile, False, middle)
    hear(0)
    tell(1)

    @pl.when(gx == 0)
    def _():
        walls[0, 0, pl.ds(TOP - 1, NY + 2), :] = jnp.zeros((NY + 2, NZ), jnp.int32)
        gathered[1] = jnp.zeros((16, 128), jnp.float32)

    @pl.when(gx == gx_size - 1)
    def _():
        walls[0, NX + 1, pl.ds(TOP - 1, NY + 2), :] = jnp.zeros((NY + 2, NZ), jnp.int32)
        gathered[2] = jnp.zeros((16, 128), jnp.float32)

    lax.fori_loop(1, NX + 1, wall_slab, 0)
    over_slabs(step_tile, False, middle)
    hear(1)
    tell(2)

    sums[...] = jnp.zeros(sums.shape, jnp.float32)
    row = lax.broadcasted_iota(jnp.int32, (32, NZ), 0)
    lane = lax.broadcasted_iota(jnp.int32, (32, NZ), 1)
    distance = jnp.abs(2 * (row & 15) + (row >> 4) - (lane >> 2))
    zmat[...] = jnp.where(distance == 0, 0.5, jnp.where(distance == 1, 0.25, 0.0)).astype(jnp.float32)

    def y_rows(step, carry):
        at = pl.multiple_of(8 * step, 8)
        row = lax.broadcasted_iota(jnp.int32, (8, 256), 0) + at
        column = lax.broadcasted_iota(jnp.int32, (8, 256), 1)
        hit = (((row >> 3) & 7) == 7 - (column >> 5)) & ((row & 7) == ((column >> 2) & 7))
        ymat[pl.ds(at, 8), :] = jnp.where(hit, 1.0, 0.0).astype(jnp.float32)
        return carry

    lax.fori_loop(0, 16, y_rows, 0)

    flags.wait_recv()

    @pl.when(gy == 0)
    def _():
        walls[0, :, low, :] = jnp.zeros((NX + 2, 1, NZ), jnp.int32)

    @pl.when(gy == gy_size - 1)
    def _():
        walls[0, :, high, :] = jnp.zeros((NX + 2, 1, NZ), jnp.int32)

    for slab in (0, NX + 1):
        wall_slab(slab, 0)
    for row in (TOP - 1, LAST + 1):
        lane_walls(inner, row)

    first_y.wait_recv()
    over_slabs(step_tile, False, outer)
    first_x.wait_recv()
    over_slabs(step_tile, True, every)
    second_x.start()
    second_y.start()
    hear(2)
    tell(3)

    over_slabs(sum_tile, False, middle)
    second_y.wait_recv()
    over_slabs(sum_tile, False, outer)
    second_x.wait_recv()
    over_slabs(sum_tile, True, every)

    def parts(value):
        upper = value.astype(jnp.bfloat16)
        return upper, (value - upper.astype(jnp.float32)).astype(jnp.bfloat16)

    weights = ymat[...].astype(jnp.bfloat16)
    over_y = sum(jnp.dot(weights, part, preferred_element_type=jnp.float32) for part in parts(sums[...]))
    weights = zmat[...].astype(jnp.bfloat16)
    over_z = sum(
        lax.dot_general(weights, part, (((1,), (1,)), ((), ())), preferred_element_type=jnp.float32)
        for part in parts(over_y)
    )
    lane = lax.broadcasted_iota(jnp.int32, (16, 128), 1)
    table[...] = jnp.where(lane >= 64, over_z[:16], over_z[16:])

    hear(3)

    def exchange(place, x, partner):
        return pltpu.make_async_remote_copy(
            src_ref=table.at[pl.ds(partner, 1)],
            dst_ref=gathered.at[place, pl.ds(gy, 1)],
            send_sem=all_send.at[place],
            recv_sem=all_recv.at[place],
            device_id=(x, partner),
            device_id_type=MESH,
        )

    def send(place, x, begin, end):
        def one(step, carry):
            exchange(place, x, lax.rem(gy + step, gy_size)).start()
            return carry

        lax.fori_loop(begin, end, one, 0)

    far = (gy_size // 2 - 3, gy_size // 2 + 4)
    send(0, gx, *far)
    pl.when(has_left)(lambda: send(2, gx - 1, *far))
    pl.when(has_right)(lambda: send(1, gx + 1, *far))
    send(0, gx, far[1], gy_size)
    send(0, gx, 1, far[0])
    pl.when(has_left)(lambda: send(2, gx - 1, far[1], gy_size + far[0]))
    pl.when(has_right)(lambda: send(1, gx + 1, far[1], gy_size + far[0]))
    gathered[0, pl.ds(gy, 1), :] = table[pl.ds(gy, 1), :]

    def everyone(place, count):
        return pltpu.make_async_remote_copy(
            src_ref=table.at[pl.ds(0, count)],
            dst_ref=gathered.at[place, pl.ds(0, count)],
            send_sem=all_send.at[place],
            recv_sem=all_recv.at[place],
            device_id=(gx, lax.rem(gy + 1, gy_size)),
            device_id_type=MESH,
        )

    column, from_left, from_right = everyone(0, gy_size - 1), everyone(1, gy_size), everyone(2, gy_size)
    column.wait_recv()
    pl.when(has_left)(from_left.wait_recv)
    pl.when(has_right)(from_right.wait_recv)

    lower = (lane & 8) != 0
    own = gathered[0]
    beside = jnp.where(
        lower,
        pltpu.roll(own, 8, 1) + pltpu.roll(gathered[1], 8, 1),
        pltpu.roll(own, 120, 1) + pltpu.roll(gathered[2], 120, 1),
    )
    along_x = pltpu.roll(0.5 * own + 0.25 * beside, 8, 1)

    mixed[pl.ds(0, 8), :] = pltpu.roll(along_x[:8], 0, 1, stride=8, stride_axis=0)
    mixed[pl.ds(8, 8), :] = pltpu.roll(along_x[8:], 64, 1, stride=8, stride_axis=0)
    lane = lax.broadcasted_iota(jnp.int32, (8, 128), 1)
    halves = [jnp.zeros((8, 128), jnp.float32) for _ in range(2)]
    for source in range(gy_size):
        spread = jnp.broadcast_to(mixed[pl.ds(source, 1), :], (8, 128))
        for half in range(2):
            turned = pltpu.roll(spread, 64 * half, 1, stride=8, stride_axis=0)
            halves[half] = jnp.where(lane >> 3 == source, turned, halves[half])
    for half in range(2):
        whole = halves[half]
        before = jnp.where(lane == 0, 0.0, pltpu.roll(whole, 1, 1))
        after = jnp.where(lane == 127, 0.0, pltpu.roll(whole, 127, 1))
        final[pl.ds(8 * half, 8), :] = 0.5 * whole + 0.25 * (before + after)
    for x in range(2):
        for z in range(2):
            fraction = final[pl.ds(8 * z + 6 + x, 1), :]
            divisor = jnp.maximum(fraction, 1.0)
            for component in range(3):
                voxels = final[pl.ds(8 * z + 2 * component + x, 1), :]
                velocity_ref[component, x, pl.ds(z, 1), :] = voxels / divisor / velocity_scale
            magnitude_ref[x, pl.ds(z, 1), :] = fraction / 64.0

    for sides in (flags, first_x, first_y, second_x, second_y):
        sides.wait_send()
    column.wait_send()
    pl.when(has_left)(from_right.wait_send)
    pl.when(has_right)(from_left.wait_send)


def local(gx_size, gy_size, populations, fluid):
    padded = (NX + 2, NY + 2 * TOP, NZ)
    vmem, dma = pltpu.VMEM, pltpu.SemaphoreType.DMA
    f32 = jnp.float32
    velocity, magnitude = pl.pallas_call(
        functools.partial(kernel, gx_size, gy_size),
        out_shape=(
            jax.ShapeDtypeStruct((3, 2, 2, 128), f32),
            jax.ShapeDtypeStruct((2, 2, 128), f32),
        ),
        in_specs=[pl.BlockSpec(memory_space=pltpu.HBM)] * 2,
        out_specs=(pl.BlockSpec(memory_space=pltpu.VMEM),) * 2,
        scratch_shapes=[
            vmem((19, NX, NY, NZ), f32),
            vmem((19, *padded), f32),
            vmem((19, *padded), f32),
            vmem((3, *padded), jnp.int32),
            vmem((256, 128), f32),
            vmem((32, 128), f32),
            vmem((128, 256), f32),
            vmem((16, 128), f32),
            vmem((3, 16, 128), f32),
            vmem((16, 128), f32),
            vmem((16, 128), f32),
            pltpu.SemaphoreType.REGULAR((4,)),
            dma((8,)),
            dma,
            dma((8,)),
            dma((8,)),
            dma((2, 9)),
            dma((2, 9)),
            dma((3,)),
            dma((3,)),
        ],
        compiler_params=pltpu.CompilerParams(
            collective_id=0, has_side_effects=True, vmem_limit_bytes=55200 * 1024
        ),
    )(populations, fluid)
    return jnp.swapaxes(velocity, 2, 3), jnp.swapaxes(magnitude, 1, 2)


def solution(mesh):
    return jax.shard_map(
        functools.partial(local, mesh.shape["gx"], mesh.shape["gy"]),
        mesh=mesh,
        in_specs=(P(None, "gx", "gy", None), P("gx", "gy", None)),
        out_specs=(P(None, "gx", None, "gy"), P("gx", None, "gy")),
        check_vma=False,
    )
```

```python
import functools

import jax
import jax.numpy as jnp
from jax import lax
from jax.experimental import pallas as pl
from jax.experimental.pallas import tpu as pltpu
from jax.sharding import PartitionSpec as P

MESH = pl.DeviceIdType.MESH

VELOCITIES = (
    (0, 0, 0),
    (1, 0, 0),
    (-1, 0, 0),
    (0, 1, 0),
    (0, -1, 0),
    (0, 0, 1),
    (0, 0, -1),
    (1, 1, 0),
    (-1, -1, 0),
    (1, -1, 0),
    (-1, 1, 0),
    (1, 0, 1),
    (-1, 0, -1),
    (1, 0, -1),
    (-1, 0, 1),
    (0, 1, 1),
    (0, -1, -1),
    (0, 1, -1),
    (0, -1, 1),
)
OPPOSITE = (0, 2, 1, 4, 3, 6, 5, 8, 7, 10, 9, 12, 11, 14, 13, 16, 15, 18, 17)
FLAG = -1
ORDER = (FLAG, 9, 1, 11, 13, 7, FLAG, 3, 15, 17, FLAG, 10, 2, 14, 12, 8, FLAG, 4, 18, 16, 0, 5, 6)
SLOT = tuple(ORDER.index(channel) for channel in range(19))
relax_rate = 1.0 / 0.6
velocity_scale = 0.002

NX, NY, NZ = 8, 32, 128
TOP = 8
LAST = TOP + NY - 1
TILES = NY // 8


def moments(f):
    s = [f[i] + f[i + 1] for i in range(1, 19, 2)]
    d = [f[i] - f[i + 1] for i in range(1, 19, 2)]
    rho = (f[0] + s[8]) + ((s[0] + s[1]) + (s[2] + s[3])) + ((s[4] + s[5]) + (s[6] + s[7]))
    mx = d[0] + (d[3] + d[4]) + (d[5] + d[6])
    my = d[1] + (d[3] - d[4]) + (d[7] + d[8])
    mz = d[2] + (d[5] - d[6]) + (d[7] - d[8])
    return rho, mx, my, mz


def collide(f):
    rho, mx, my, mz = moments(f)
    inverse = 1.0 / rho
    ux, uy, uz = mx * inverse, my * inverse, mz * inverse
    base = rho - 1.5 * (mx * ux + my * uy + mz * uz)
    keep = 1.0 - relax_rate
    relaxed = [keep * f[0] + (relax_rate / 3.0) * base]
    vx, vy, vz = 1.5 * ux, 1.5 * uy, 1.5 * uz
    near = (relax_rate / 18.0) * base
    far = (relax_rate / 36.0) * base
    ax, ay, az = (relax_rate / 6.0) * mx, (relax_rate / 6.0) * my, (relax_rate / 6.0) * mz
    bx, by, bz = 0.5 * ax, 0.5 * ay, 0.5 * az
    for channel, level, flow, speed in (
        (1, near, ax, vx),
        (3, near, ay, vy),
        (5, near, az, vz),
        (7, far, bx + by, vx + vy),
        (9, far, bx - by, vx - vy),
        (11, far, bx + bz, vx + vz),
        (13, far, bx - bz, vx - vz),
        (15, far, by + bz, vy + vz),
        (17, far, by - bz, vy - vz),
    ):
        even = level + flow * speed
        relaxed.append(keep * f[channel] + (even + flow))
        relaxed.append(keep * f[channel + 1] + (even - flow))
    return relaxed


def pulled(held, walls, x, tile):
    f = []
    for channel in range(19):
        cx, cy, cz = VELOCITIES[channel]
        rows = pl.ds(TOP + 8 * tile, 8)
        if channel == 0:
            f.append(held[SLOT[0], x + 1, rows, :])
            continue
        from_rows = pl.ds(TOP + 8 * tile - cy, 8)
        source = held[SLOT[channel], x + 1 - cx, from_rows, :]
        if cz:
            source = pltpu.roll(source, cz % NZ, 1)
        open_site = walls[cz % 3, x + 1 - cx, from_rows, :]
        f.append(jnp.where(open_site > 0, source, held[SLOT[OPPOSITE[channel]], x + 1, rows, :]))
    return f


def kernel(
    gx_size,
    gy_size,
    populations,
    fluid,
    final,
    start,
    solid,
    first,
    second,
    walls,
    sums,
    zmat,
    ymat,
    table,
    gathered,
    mixed,
    ready,
    load_sem,
    fluid_sem,
    halo_send,
    halo_recv,
    all_send,
    all_recv,
):
    gx, gy = lax.axis_index("gx"), lax.axis_index("gy")
    f32 = jnp.float32
    has_left, has_right = gx > 0, gx < gx_size - 1
    has_below, has_above = gy > 0, gy < gy_size - 1

    def load(x):
        return pltpu.make_async_copy(populations.at[:, x], start.at[:, x], load_sem.at[x])

    fluid_copy = pltpu.make_async_copy(fluid, solid, fluid_sem)
    load(7).start()
    load(0).start()
    fluid_copy.start()
    for x in range(1, NX - 1):
        load(x).start()

    def number(*conditions):
        return sum(condition.astype(jnp.int32) for condition in conditions)

    barrier = pltpu.get_barrier_semaphore()
    beside_x = ((-1, has_left), (0, None), (1, has_right))
    beside_y = ((-1, has_below), (0, None), (1, has_above))
    for dx, in_x in beside_x:
        for dy, in_y in beside_y:
            if dx == 0 and dy == 0:
                continue
            there = in_y if in_x is None else in_x if in_y is None else in_x & in_y

            @pl.when(there)
            def _():
                pl.semaphore_signal(barrier, inc=1, device_id=(gx + dx, gy + dy), device_id_type=MESH)

    def tell(stage):
        for way in (-(2**stage), 2**stage):

            @pl.when((gy + way >= 0) & (gy + way < gy_size))
            def _():
                pl.semaphore_signal(ready.at[stage], inc=1, device_id=(gx, gy + way), device_id_type=MESH)

    def hear(stage):
        pl.semaphore_wait(ready.at[stage], number(gy >= 2**stage, gy + 2**stage < gy_size))

    def lane_walls(slab, rows):
        flags = walls[0, slab, rows, :]
        lane = lax.broadcasted_iota(jnp.int32, flags.shape, flags.ndim - 1)
        walls[1, slab, rows, :] = jnp.where(lane == 0, 0.0, pltpu.roll(flags, 1, flags.ndim - 1))
        walls[2, slab, rows, :] = jnp.where(lane == NZ - 1, 0.0, pltpu.roll(flags, NZ - 1, flags.ndim - 1))

    def inner_walls(x, carry):
        for tile in range(TILES):
            rows = pl.ds(TOP + 8 * tile, 8)
            walls[0, x + 1, rows, :] = solid[x, pl.ds(8 * tile, 8), :].astype(jnp.float32)
            lane_walls(x + 1, rows)
        return carry

    def face_flags(x, carry):
        upper = solid[x, pl.ds(NY - 8, 8), :].astype(jnp.float32)
        lower = solid[x, pl.ds(0, 8), :].astype(jnp.float32)
        for slot in (6, 10):
            first[slot, x + 1, pl.ds(TOP + NY - 8, 8), :] = upper
            second[slot, x + 1, pl.ds(TOP + NY - 8, 8), :] = upper
        first[16, x + 1, pl.ds(TOP, 8), :] = lower
        second[16, x + 1, pl.ds(TOP, 8), :] = lower
        return carry

    inner, block = pl.ds(1, NX), pl.ds(TOP, NY)
    low, high = pl.ds(TOP - 1, 1), pl.ds(LAST + 1, 1)
    bottom, top = pl.ds(TOP, 1), pl.ds(LAST, 1)

    def x_sides(flags):
        return [
            (pl.ds(5, 1 + flags), (NX, top), (0, low), (1, 1), has_right & has_above, has_left & has_below),
            (pl.ds(1 - flags, 1 + flags), (NX, bottom), (0, high), (1, -1), has_right & has_below, has_left & has_above),
            (pl.ds(11 - flags, 1 + flags), (1, top), (NX + 1, low), (-1, 1), has_left & has_above, has_right & has_below),
            (pl.ds(15, 1 + flags), (1, bottom), (NX + 1, high), (-1, -1), has_left & has_below, has_right & has_above),
            (pl.ds(1, 5 + flags), (NX, block), (0, block), (1, 0), has_right, has_left),
            (pl.ds(11, 5 + flags), (1, block), (NX + 1, block), (-1, 0), has_left, has_right),
        ]

    y_sides = [
        (pl.ds(5, 7), (inner, top), (inner, low), (0, 1), has_above, has_below),
        (pl.ds(15, 5), (inner, bottom), (inner, high), (0, -1), has_below, has_above),
        (pl.ds(1, 1), (inner, bottom), (inner, high), (0, -1), has_below, has_above),
    ]

    class Sides:
        def __init__(self, buffer, sides, send, recv, offset):
            self.copies = [
                (
                    pltpu.make_async_remote_copy(
                        src_ref=buffer.at[(channels, *source)],
                        dst_ref=buffer.at[(channels, *target)],
                        send_sem=send.at[offset + i],
                        recv_sem=recv.at[offset + i],
                        device_id=(gx + way[0], gy + way[1]),
                        device_id_type=MESH,
                    ),
                    sent,
                    arrives,
                )
                for i, (channels, source, target, way, sent, arrives) in enumerate(sides)
            ]

        def start(self):
            for copy, sent, _ in self.copies:
                pl.when(sent)(copy.start)

        def wait_recv(self):
            for copy, _, arrives in self.copies:
                pl.when(arrives)(copy.wait_recv)

        def wait_send(self):
            for copy, sent, _ in self.copies:
                pl.when(sent)(copy.wait_send)

    first_x = Sides(first, x_sides(1), halo_send.at[0], halo_recv.at[0], 0)
    first_y = Sides(first, y_sides, halo_send.at[0], halo_recv.at[0], 6)
    second_x = Sides(second, x_sides(0), halo_send.at[1], halo_recv.at[1], 0)
    second_y = Sides(second, y_sides, halo_send.at[1], halo_recv.at[1], 6)

    def relax_tile(x, tile):
        rows = pl.ds(8 * tile, 8)
        relaxed = collide([start[channel, x, rows, :] for channel in range(19)])
        for channel in range(19):
            first[SLOT[channel], x + 1, pl.ds(TOP + 8 * tile, 8), :] = relaxed[channel]

    def step_tile(x, tile):
        relaxed = collide(pulled(first, walls, x, tile))
        for channel in range(19):
            second[SLOT[channel], x + 1, pl.ds(TOP + 8 * tile, 8), :] = relaxed[channel]

    def sum_tile(x, tile):
        rho, mx, my, mz = moments(pulled(second, walls, x, tile))
        here = walls[0, x + 1, pl.ds(TOP + 8 * tile, 8), :]
        scale = here / rho
        for component, value in enumerate((mx * scale, my * scale, mz * scale, here)):
            rows = pl.ds(pl.multiple_of(component * 64 + (x // 4) * 32 + 8 * tile, 8), 8)
            sums[rows, :] = sums[rows, :] + value

    def over_slabs(body, edge, tiles):
        def edge_slab(step, carry):
            for tile in tiles:
                body((NX - 1) * (1 - step), tile)
            return carry

        def inner_slab(x, carry):
            for tile in tiles:
                body(x, tile)
            return carry

        if edge:
            lax.fori_loop(0, 2, edge_slab, 0)
        else:
            lax.fori_loop(1, NX - 1, inner_slab, 0)

    every, outer, middle = range(TILES), (0, TILES - 1), range(1, TILES - 1)

    sums[...] = jnp.zeros(sums.shape, jnp.float32)
    row = lax.broadcasted_iota(jnp.int32, (32, NZ), 0)
    lane = lax.broadcasted_iota(jnp.int32, (32, NZ), 1)
    distance = jnp.abs(2 * (row & 15) + (row >> 4) - (lane >> 2))
    zmat[...] = jnp.where(distance == 0, 0.5, jnp.where(distance == 1, 0.25, 0.0)).astype(jnp.float32)

    def y_rows(step, carry):
        at = pl.multiple_of(8 * step, 8)
        row = lax.broadcasted_iota(jnp.int32, (8, 256), 0) + at
        column = lax.broadcasted_iota(jnp.int32, (8, 256), 1)
        hit = (((row >> 3) & 7) == 7 - (column >> 5)) & ((row & 7) == ((column >> 2) & 7))
        ymat[pl.ds(at, 8), :] = jnp.where(hit, 1.0, 0.0).astype(jnp.float32)
        return carry

    lax.fori_loop(0, 16, y_rows, 0)

    @pl.when(gx == 0)
    def _():
        first[6, 0, pl.ds(TOP, NY), :] = jnp.zeros((NY, NZ), f32)
        first[6, 0, low, :] = jnp.zeros((1, NZ), f32)
        first[0, 0, high, :] = jnp.zeros((1, NZ), f32)
        gathered[1] = jnp.zeros((16, 128), f32)

    @pl.when(gx == gx_size - 1)
    def _():
        first[16, NX + 1, pl.ds(TOP, NY), :] = jnp.zeros((NY, NZ), f32)
        first[10, NX + 1, low, :] = jnp.zeros((1, NZ), f32)
        first[16, NX + 1, high, :] = jnp.zeros((1, NZ), f32)
        gathered[2] = jnp.zeros((16, 128), f32)

    @pl.when(gy == 0)
    def _():
        first[6, inner, TOP - 1, :] = jnp.zeros((NX, NZ), f32)
        first[6, 0, low, :] = jnp.zeros((1, NZ), f32)
        first[10, NX + 1, low, :] = jnp.zeros((1, NZ), f32)

    @pl.when(gy == gy_size - 1)
    def _():
        first[16, inner, LAST + 1, :] = jnp.zeros((NX, NZ), f32)
        first[0, 0, high, :] = jnp.zeros((1, NZ), f32)
        first[16, NX + 1, high, :] = jnp.zeros((1, NZ), f32)

    load(7).wait()
    load(0).wait()
    over_slabs(relax_tile, True, every)
    fluid_copy.wait()
    lax.fori_loop(0, NX, face_flags, 0)
    for tile in range(TILES):
        rows, own = pl.ds(TOP + 8 * tile, 8), pl.ds(8 * tile, 8)
        first[6, NX, rows, :] = solid[NX - 1, own, :].astype(f32)
        first[16, 1, rows, :] = solid[0, own, :].astype(f32)
    first[0, NX, pl.ds(TOP, 8), :] = solid[NX - 1, pl.ds(0, 8), :].astype(f32)
    for x in range(1, NX - 1):
        load(x).wait()
    over_slabs(relax_tile, False, outer)
    over_slabs(relax_tile, False, middle)
    pl.semaphore_wait(barrier, (1 + number(has_left, has_right)) * (1 + number(has_below, has_above)) - 1)
    first_x.start()
    first_y.start()
    tell(0)

    lax.fori_loop(0, NX, inner_walls, 0)
    over_slabs(step_tile, False, middle)
    hear(0)
    tell(1)

    first_y.wait_recv()
    for slot, row in ((6, TOP - 1), (16, LAST + 1)):
        walls[0, inner, row, :] = first[slot, inner, row, :]
        lane_walls(inner, row)
    over_slabs(step_tile, False, outer)
    hear(1)
    tell(2)
    first_x.wait_recv()
    for slot, slab in ((6, 0), (16, NX + 1)):
        for tile in range(TILES):
            rows = pl.ds(TOP + 8 * tile, 8)
            walls[0, slab, rows, :] = first[slot, slab, rows, :]
            lane_walls(slab, rows)
    for slot, slab, row in ((6, 0, low), (0, 0, high), (10, NX + 1, low), (16, NX + 1, high)):
        walls[0, slab, row, :] = first[slot, slab, row, :]
    over_slabs(step_tile, True, every)
    second_x.start()
    second_y.start()
    hear(2)
    tell(3)

    over_slabs(sum_tile, False, middle)
    for sides in (first_x, first_y):
        sides.wait_send()
    second_y.wait_recv()
    over_slabs(sum_tile, False, outer)
    second_x.wait_recv()
    over_slabs(sum_tile, True, every)

    def parts(value):
        upper = value.astype(jnp.bfloat16)
        return upper, (value - upper.astype(jnp.float32)).astype(jnp.bfloat16)

    weights = ymat[...].astype(jnp.bfloat16)
    over_y = sum(jnp.dot(weights, part, preferred_element_type=jnp.float32) for part in parts(sums[...]))
    weights = zmat[...].astype(jnp.bfloat16)
    over_z = sum(
        lax.dot_general(weights, part, (((1,), (1,)), ((), ())), preferred_element_type=jnp.float32)
        for part in parts(over_y)
    )
    lane = lax.broadcasted_iota(jnp.int32, (16, 128), 1)
    table[...] = jnp.where(lane >= 64, over_z[:16], over_z[16:])

    hear(3)

    def exchange(place, x, partner):
        return pltpu.make_async_remote_copy(
            src_ref=table.at[pl.ds(partner, 1)],
            dst_ref=gathered.at[place, pl.ds(gy, 1)],
            send_sem=all_send.at[place],
            recv_sem=all_recv.at[place],
            device_id=(x, partner),
            device_id_type=MESH,
        )

    def send(place, x, begin, end):
        for step in range(begin, end):
            exchange(place, x, lax.rem(gy + step, gy_size)).start()

    far = (gy_size // 2 - 3, gy_size // 2 + 4)
    send(0, gx, *far)
    pl.when(has_left)(lambda: send(2, gx - 1, *far))
    pl.when(has_right)(lambda: send(1, gx + 1, *far))
    send(0, gx, far[1], gy_size)
    send(0, gx, 1, far[0])
    pl.when(has_left)(lambda: send(2, gx - 1, far[1], gy_size + far[0]))
    pl.when(has_right)(lambda: send(1, gx + 1, far[1], gy_size + far[0]))
    gathered[0, pl.ds(gy, 1), :] = table[pl.ds(gy, 1), :]

    def everyone(place, count):
        return pltpu.make_async_remote_copy(
            src_ref=table.at[pl.ds(0, count)],
            dst_ref=gathered.at[place, pl.ds(0, count)],
            send_sem=all_send.at[place],
            recv_sem=all_recv.at[place],
            device_id=(gx, lax.rem(gy + 1, gy_size)),
            device_id_type=MESH,
        )

    column, from_left, from_right = everyone(0, gy_size - 1), everyone(1, gy_size), everyone(2, gy_size)
    second_x.wait_send()
    second_y.wait_send()
    column.wait_send()
    pl.when(has_left)(from_right.wait_send)
    pl.when(has_right)(from_left.wait_send)
    column.wait_recv()
    pl.when(has_left)(from_left.wait_recv)
    pl.when(has_right)(from_right.wait_recv)

    lower = (lane & 8) != 0
    own = gathered[0]
    beside = jnp.where(
        lower,
        pltpu.roll(own, 8, 1) + pltpu.roll(gathered[1], 8, 1),
        pltpu.roll(own, 120, 1) + pltpu.roll(gathered[2], 120, 1),
    )
    along_x = pltpu.roll(0.5 * own + 0.25 * beside, 8, 1)

    mixed[pl.ds(0, 8), :] = pltpu.roll(along_x[:8], 0, 1, stride=8, stride_axis=0)
    mixed[pl.ds(8, 8), :] = pltpu.roll(along_x[8:], 64, 1, stride=8, stride_axis=0)
    lane = lax.broadcasted_iota(jnp.int32, (8, 128), 1)
    halves = [jnp.zeros((8, 128), jnp.float32) for _ in range(2)]
    for source in range(gy_size):
        spread = jnp.broadcast_to(mixed[pl.ds(source, 1), :], (8, 128))
        for half in range(2):
            turned = pltpu.roll(spread, 64 * half, 1, stride=8, stride_axis=0)
            halves[half] = jnp.where(lane >> 3 == source, turned, halves[half])
    for half in range(2):
        whole = halves[half]
        before = jnp.where(lane == 0, 0.0, pltpu.roll(whole, 1, 1))
        after = jnp.where(lane == 127, 0.0, pltpu.roll(whole, 127, 1))
        final[pl.ds(8 * half, 8), :] = 0.5 * whole + 0.25 * (before + after)


def finish(final, velocity_ref, magnitude_ref):
    for x in range(2):
        for z in range(2):
            fraction = final[pl.ds(8 * z + 6 + x, 1), :]
            divisor = jnp.maximum(fraction, 1.0)
            for component in range(3):
                voxels = final[pl.ds(8 * z + 2 * component + x, 1), :]
                velocity_ref[component, x, pl.ds(z, 1), :] = voxels / divisor / velocity_scale
            magnitude_ref[x, pl.ds(z, 1), :] = fraction / 64.0


def local(gx_size, gy_size, populations, fluid):
    padded = (NX + 2, NY + 2 * TOP, NZ)
    vmem, dma = pltpu.VMEM, pltpu.SemaphoreType.DMA
    f32 = jnp.float32
    blurred = pl.pallas_call(
        functools.partial(kernel, gx_size, gy_size),
        out_shape=jax.ShapeDtypeStruct((16, 128), f32),
        in_specs=[pl.BlockSpec(memory_space=pltpu.HBM)] * 2,
        out_specs=pl.BlockSpec(memory_space=pltpu.VMEM),
        scratch_shapes=[
            vmem((19, NX, NY, NZ), f32),
            vmem((NX, NY, NZ), jnp.int32),
            vmem((len(ORDER), *padded), f32),
            vmem((len(ORDER), *padded), f32),
            vmem((3, *padded), f32),
            vmem((256, 128), f32),
            vmem((32, 128), f32),
            vmem((128, 256), f32),
            vmem((16, 128), f32),
            vmem((3, 16, 128), f32),
            vmem((16, 128), f32),
            pltpu.SemaphoreType.REGULAR((4,)),
            dma((8,)),
            dma,
            dma((2, 9)),
            dma((2, 9)),
            dma((3,)),
            dma((3,)),
        ],
        compiler_params=pltpu.CompilerParams(
            collective_id=0, has_side_effects=True, vmem_limit_bytes=55200 * 1024
        ),
    )(populations, fluid)
    velocity, magnitude = pl.pallas_call(
        finish,
        out_shape=(
            jax.ShapeDtypeStruct((3, 2, 2, 128), f32),
            jax.ShapeDtypeStruct((2, 2, 128), f32),
        ),
        in_specs=[pl.BlockSpec(memory_space=pltpu.VMEM)],
        out_specs=(pl.BlockSpec(memory_space=pltpu.VMEM),) * 2,
        compiler_params=pltpu.CompilerParams(vmem_limit_bytes=1024 * 1024),
    )(blurred)
    return jnp.swapaxes(velocity, 2, 3), jnp.swapaxes(magnitude, 1, 2)


def solution(mesh):
    return jax.shard_map(
        functools.partial(local, mesh.shape["gx"], mesh.shape["gy"]),
        mesh=mesh,
        in_specs=(P(None, "gx", "gy", None), P("gx", "gy", None)),
        out_specs=(P(None, "gx", None, "gy"), P("gx", None, "gy")),
        check_vma=False,
    )
```

```python
import functools

import jax
import jax.numpy as jnp
from jax import lax
from jax.experimental import pallas as pl
from jax.experimental.pallas import tpu as pltpu
from jax.sharding import PartitionSpec as P

MESH = pl.DeviceIdType.MESH

VELOCITIES = (
    (0, 0, 0),
    (1, 0, 0),
    (-1, 0, 0),
    (0, 1, 0),
    (0, -1, 0),
    (0, 0, 1),
    (0, 0, -1),
    (1, 1, 0),
    (-1, -1, 0),
    (1, -1, 0),
    (-1, 1, 0),
    (1, 0, 1),
    (-1, 0, -1),
    (1, 0, -1),
    (-1, 0, 1),
    (0, 1, 1),
    (0, -1, -1),
    (0, 1, -1),
    (0, -1, 1),
)
OPPOSITE = (0, 2, 1, 4, 3, 6, 5, 8, 7, 10, 9, 12, 11, 14, 13, 16, 15, 18, 17)
FLAG = -1
ORDER = (FLAG, 9, 1, 11, 13, 7, FLAG, 3, 15, 17, FLAG, 10, 2, 14, 12, 8, FLAG, 4, 18, 16, 0, 5, 6)
SLOT = tuple(ORDER.index(channel) for channel in range(19))
relax_rate = 1.0 / 0.6
velocity_scale = 0.002

NX, NY, NZ = 8, 32, 128
TOP = 8
LAST = TOP + NY - 1
TILES = NY // 8


def moments(f):
    s = [f[i] + f[i + 1] for i in range(1, 19, 2)]
    d = [f[i] - f[i + 1] for i in range(1, 19, 2)]
    rho = (f[0] + s[8]) + ((s[0] + s[1]) + (s[2] + s[3])) + ((s[4] + s[5]) + (s[6] + s[7]))
    mx = d[0] + (d[3] + d[4]) + (d[5] + d[6])
    my = d[1] + (d[3] - d[4]) + (d[7] + d[8])
    mz = d[2] + (d[5] - d[6]) + (d[7] - d[8])
    return rho, mx, my, mz


def collide(f):
    rho, mx, my, mz = moments(f)
    inverse = 1.0 / rho
    ux, uy, uz = mx * inverse, my * inverse, mz * inverse
    base = rho - 1.5 * (mx * ux + my * uy + mz * uz)
    keep = 1.0 - relax_rate
    relaxed = [keep * f[0] + (relax_rate / 3.0) * base]
    vx, vy, vz = 1.5 * ux, 1.5 * uy, 1.5 * uz
    near = (relax_rate / 18.0) * base
    far = (relax_rate / 36.0) * base
    ax, ay, az = (relax_rate / 6.0) * mx, (relax_rate / 6.0) * my, (relax_rate / 6.0) * mz
    bx, by, bz = 0.5 * ax, 0.5 * ay, 0.5 * az
    for channel, level, flow, speed in (
        (1, near, ax, vx),
        (3, near, ay, vy),
        (5, near, az, vz),
        (7, far, bx + by, vx + vy),
        (9, far, bx - by, vx - vy),
        (11, far, bx + bz, vx + vz),
        (13, far, bx - bz, vx - vz),
        (15, far, by + bz, vy + vz),
        (17, far, by - bz, vy - vz),
    ):
        even = level + flow * speed
        relaxed.append(keep * f[channel] + (even + flow))
        relaxed.append(keep * f[channel + 1] + (even - flow))
    return relaxed


def pulled(held, walls, x, tile):
    f = []
    for channel in range(19):
        cx, cy, cz = VELOCITIES[channel]
        rows = pl.ds(TOP + 8 * tile, 8)
        if channel == 0:
            f.append(held[SLOT[0], x + 1, rows, :])
            continue
        from_rows = pl.ds(TOP + 8 * tile - cy, 8)
        source = held[SLOT[channel], x + 1 - cx, from_rows, :]
        if cz:
            source = pltpu.roll(source, cz % NZ, 1)
        open_site = walls[cz % 3, x + 1 - cx, from_rows, :]
        f.append(jnp.where(open_site > 0, source, held[SLOT[OPPOSITE[channel]], x + 1, rows, :]))
    return f


def kernel(
    gx_size,
    gy_size,
    populations,
    fluid,
    final,
    start,
    solid,
    first,
    second,
    walls,
    sums,
    zmat,
    ymat,
    table,
    gathered,
    mixed,
    ready,
    load_sem,
    fluid_sem,
    halo_send,
    halo_recv,
    all_send,
    all_recv,
):
    gx, gy = lax.axis_index("gx"), lax.axis_index("gy")
    f32 = jnp.float32
    has_left, has_right = gx > 0, gx < gx_size - 1
    has_below, has_above = gy > 0, gy < gy_size - 1

    def number(*conditions):
        return sum(condition.astype(jnp.int32) for condition in conditions)

    barrier = pltpu.get_barrier_semaphore()
    beside_x = ((-1, has_left), (1, has_right), (0, None))
    beside_y = ((-1, has_below), (0, None), (1, has_above))
    for dx, in_x in beside_x:
        for dy, in_y in beside_y:
            if dx == 0 and dy == 0:
                continue
            there = in_y if in_x is None else in_x if in_y is None else in_x & in_y

            @pl.when(there)
            def _():
                pl.semaphore_signal(barrier, inc=1, device_id=(gx + dx, gy + dy), device_id_type=MESH)

    def load(x):
        return pltpu.make_async_copy(populations.at[:, x], start.at[:, x], load_sem.at[x])

    fluid_copy = pltpu.make_async_copy(fluid, solid, fluid_sem)
    load(7).start()
    load(0).start()
    fluid_copy.start()
    for x in range(1, NX - 1):
        load(x).start()

    def tell(stage):
        for way in (-(2**stage), 2**stage):

            @pl.when((gy + way >= 0) & (gy + way < gy_size))
            def _():
                pl.semaphore_signal(ready.at[stage], inc=1, device_id=(gx, gy + way), device_id_type=MESH)

    def hear(stage):
        pl.semaphore_wait(ready.at[stage], number(gy >= 2**stage, gy + 2**stage < gy_size))

    def lane_walls(slab, rows):
        flags = walls[0, slab, rows, :]
        lane = lax.broadcasted_iota(jnp.int32, flags.shape, flags.ndim - 1)
        walls[1, slab, rows, :] = jnp.where(lane == 0, 0.0, pltpu.roll(flags, 1, flags.ndim - 1))
        walls[2, slab, rows, :] = jnp.where(lane == NZ - 1, 0.0, pltpu.roll(flags, NZ - 1, flags.ndim - 1))

    def inner_walls(x, carry):
        for tile in range(TILES):
            rows = pl.ds(TOP + 8 * tile, 8)
            walls[0, x + 1, rows, :] = solid[x, pl.ds(8 * tile, 8), :].astype(jnp.float32)
            lane_walls(x + 1, rows)
        return carry

    def face_flags(x, carry):
        upper = solid[x, pl.ds(NY - 8, 8), :].astype(jnp.float32)
        lower = solid[x, pl.ds(0, 8), :].astype(jnp.float32)
        for slot in (6, 10):
            first[slot, x + 1, pl.ds(TOP + NY - 8, 8), :] = upper
            second[slot, x + 1, pl.ds(TOP + NY - 8, 8), :] = upper
        first[16, x + 1, pl.ds(TOP, 8), :] = lower
        second[16, x + 1, pl.ds(TOP, 8), :] = lower
        return carry

    inner, block = pl.ds(1, NX), pl.ds(TOP, NY)
    low, high = pl.ds(TOP - 1, 1), pl.ds(LAST + 1, 1)
    bottom, top = pl.ds(TOP, 1), pl.ds(LAST, 1)

    def x_sides(flags):
        return [
            (pl.ds(5, 1 + flags), (NX, top), (0, low), (1, 1), has_right & has_above, has_left & has_below),
            (pl.ds(1 - flags, 1 + flags), (NX, bottom), (0, high), (1, -1), has_right & has_below, has_left & has_above),
            (pl.ds(11 - flags, 1 + flags), (1, top), (NX + 1, low), (-1, 1), has_left & has_above, has_right & has_below),
            (pl.ds(15, 1 + flags), (1, bottom), (NX + 1, high), (-1, -1), has_left & has_below, has_right & has_above),
            (pl.ds(1, 5 + flags), (NX, block), (0, block), (1, 0), has_right, has_left),
            (pl.ds(11, 5 + flags), (1, block), (NX + 1, block), (-1, 0), has_left, has_right),
        ]

    y_sides = [
        (pl.ds(5, 7), (inner, top), (inner, low), (0, 1), has_above, has_below),
        (pl.ds(15, 5), (inner, bottom), (inner, high), (0, -1), has_below, has_above),
        (pl.ds(1, 1), (inner, bottom), (inner, high), (0, -1), has_below, has_above),
    ]

    class Sides:
        def __init__(self, buffer, sides, send, recv, offset):
            self.copies = [
                (
                    pltpu.make_async_remote_copy(
                        src_ref=buffer.at[(channels, *source)],
                        dst_ref=buffer.at[(channels, *target)],
                        send_sem=send.at[offset + i],
                        recv_sem=recv.at[offset + i],
                        device_id=(gx + way[0], gy + way[1]),
                        device_id_type=MESH,
                    ),
                    sent,
                    arrives,
                )
                for i, (channels, source, target, way, sent, arrives) in enumerate(sides)
            ]

        def start(self):
            for copy, sent, _ in self.copies:
                pl.when(sent)(copy.start)

        def wait_recv(self):
            for copy, _, arrives in self.copies:
                pl.when(arrives)(copy.wait_recv)

        def wait_send(self):
            for copy, sent, _ in self.copies:
                pl.when(sent)(copy.wait_send)

    first_x = Sides(first, x_sides(1), halo_send.at[0], halo_recv.at[0], 0)
    first_y = Sides(first, y_sides, halo_send.at[0], halo_recv.at[0], 6)
    second_x = Sides(second, x_sides(0), halo_send.at[1], halo_recv.at[1], 0)
    second_y = Sides(second, y_sides, halo_send.at[1], halo_recv.at[1], 6)

    def relax_tile(x, tile):
        rows = pl.ds(8 * tile, 8)
        relaxed = collide([start[channel, x, rows, :] for channel in range(19)])
        for channel in range(19):
            first[SLOT[channel], x + 1, pl.ds(TOP + 8 * tile, 8), :] = relaxed[channel]

    def step_tile(x, tile):
        relaxed = collide(pulled(first, walls, x, tile))
        for channel in range(19):
            second[SLOT[channel], x + 1, pl.ds(TOP + 8 * tile, 8), :] = relaxed[channel]

    def sum_tile(x, tile):
        rho, mx, my, mz = moments(pulled(second, walls, x, tile))
        here = walls[0, x + 1, pl.ds(TOP + 8 * tile, 8), :]
        scale = here / rho
        for component, value in enumerate((mx * scale, my * scale, mz * scale, here)):
            rows = pl.ds(pl.multiple_of(component * 64 + (x // 4) * 32 + 8 * tile, 8), 8)
            sums[rows, :] = sums[rows, :] + value

    def over_slabs(body, edge, tiles):
        def edge_slab(step, carry):
            for tile in tiles:
                body((NX - 1) * (1 - step), tile)
            return carry

        def inner_slab(x, carry):
            for tile in tiles:
                body(x, tile)
            return carry

        if edge:
            lax.fori_loop(0, 2, edge_slab, 0)
        else:
            lax.fori_loop(1, NX - 1, inner_slab, 0)

    every, outer, middle = range(TILES), (0, TILES - 1), range(1, TILES - 1)

    sums[...] = jnp.zeros(sums.shape, jnp.float32)
    row = lax.broadcasted_iota(jnp.int32, (32, NZ), 0)
    lane = lax.broadcasted_iota(jnp.int32, (32, NZ), 1)
    distance = jnp.abs(2 * (row & 15) + (row >> 4) - (lane >> 2))
    zmat[...] = jnp.where(distance == 0, 0.5, jnp.where(distance == 1, 0.25, 0.0)).astype(jnp.float32)

    turn = 8 * gy + 8

    def y_rows(step, carry):
        at = pl.multiple_of(8 * step, 8)
        row = (lax.broadcasted_iota(jnp.int32, (8, 256), 0) + (at - turn + 256)) & 127
        column = lax.broadcasted_iota(jnp.int32, (8, 256), 1)
        hit = (((row >> 4) & 3) == 3 - (column >> 6)) & ((row & 7) == ((column >> 2) & 7))
        same = ((row >> 3) & 1) != ((column >> 5) & 1)
        ymat[pl.ds(at, 8), :] = jnp.where(hit, jnp.where(same, 0.5, 0.25), 0.0)
        ymat[pl.ds(pl.multiple_of(at + 128, 8), 8), :] = jnp.where(hit & ~same, 0.25, 0.0)
        return carry

    lax.fori_loop(0, 16, y_rows, 0)

    @pl.when(gx == 0)
    def _():
        first[6, 0, pl.ds(TOP, NY), :] = jnp.zeros((NY, NZ), f32)
        first[6, 0, low, :] = jnp.zeros((1, NZ), f32)
        first[0, 0, high, :] = jnp.zeros((1, NZ), f32)
        gathered[1] = jnp.zeros((16, 128), f32)

    @pl.when(gx == gx_size - 1)
    def _():
        first[16, NX + 1, pl.ds(TOP, NY), :] = jnp.zeros((NY, NZ), f32)
        first[10, NX + 1, low, :] = jnp.zeros((1, NZ), f32)
        first[16, NX + 1, high, :] = jnp.zeros((1, NZ), f32)
        gathered[2] = jnp.zeros((16, 128), f32)

    @pl.when(gy == 0)
    def _():
        first[6, inner, TOP - 1, :] = jnp.zeros((NX, NZ), f32)
        first[6, 0, low, :] = jnp.zeros((1, NZ), f32)
        first[10, NX + 1, low, :] = jnp.zeros((1, NZ), f32)

    @pl.when(gy == gy_size - 1)
    def _():
        first[16, inner, LAST + 1, :] = jnp.zeros((NX, NZ), f32)
        first[0, 0, high, :] = jnp.zeros((1, NZ), f32)
        first[16, NX + 1, high, :] = jnp.zeros((1, NZ), f32)

    load(7).wait()
    load(0).wait()
    over_slabs(relax_tile, True, every)
    fluid_copy.wait()
    lax.fori_loop(0, NX, face_flags, 0)
    for tile in range(TILES):
        rows, own = pl.ds(TOP + 8 * tile, 8), pl.ds(8 * tile, 8)
        first[6, NX, rows, :] = solid[NX - 1, own, :].astype(f32)
        first[16, 1, rows, :] = solid[0, own, :].astype(f32)
    first[0, NX, pl.ds(TOP, 8), :] = solid[NX - 1, pl.ds(0, 8), :].astype(f32)
    for x in range(1, NX - 1):
        load(x).wait()
    over_slabs(relax_tile, False, outer)
    pl.semaphore_wait(barrier, (1 + number(has_left, has_right)) * (1 + number(has_below, has_above)) - 1)
    first_x.start()
    first_y.start()
    tell(0)

    over_slabs(relax_tile, False, middle)
    lax.fori_loop(0, NX, inner_walls, 0)
    over_slabs(step_tile, False, middle)
    hear(0)
    tell(1)

    first_y.wait_recv()
    for slot, row in ((6, TOP - 1), (16, LAST + 1)):
        walls[0, inner, row, :] = first[slot, inner, row, :]
        lane_walls(inner, row)
    over_slabs(step_tile, False, outer)
    hear(1)
    tell(2)
    first_x.wait_recv()
    for slot, slab in ((6, 0), (16, NX + 1)):
        for tile in range(TILES):
            rows = pl.ds(TOP + 8 * tile, 8)
            walls[0, slab, rows, :] = first[slot, slab, rows, :]
            lane_walls(slab, rows)
    for slot, slab, row in ((6, 0, low), (0, 0, high), (10, NX + 1, low), (16, NX + 1, high)):
        walls[0, slab, row, :] = first[slot, slab, row, :]
    over_slabs(step_tile, True, every)
    second_x.start()
    second_y.start()
    hear(2)
    tell(3)

    over_slabs(sum_tile, False, middle)
    for sides in (first_x, first_y):
        sides.wait_send()
    second_y.wait_recv()
    over_slabs(sum_tile, False, outer)
    second_x.wait_recv()
    over_slabs(sum_tile, True, every)

    def parts(value):
        upper = value.astype(jnp.bfloat16)
        return upper, (value - upper.astype(jnp.float32)).astype(jnp.bfloat16)

    weights = ymat[...].astype(jnp.bfloat16)
    over_y = sum(jnp.dot(weights, part, preferred_element_type=jnp.float32) for part in parts(sums[...]))
    weights = zmat[...].astype(jnp.bfloat16)
    over_z = sum(
        lax.dot_general(weights, part, (((1,), (1,)), ((), ())), preferred_element_type=jnp.float32)
        for part in parts(over_y)
    )
    lane = lax.broadcasted_iota(jnp.int32, (16, 128), 1)
    first_z = ((lane - turn + 256) & 64) != 0
    for part in range(2):
        lanes = slice(128 * part, 128 * part + 128)
        table[part] = jnp.where(first_z, over_z[:16, lanes], over_z[16:, lanes])
    hear(3)

    def exchange(place, x, partner):
        return pltpu.make_async_remote_copy(
            src_ref=table.at[min(place, 1), pl.ds(partner, 1)],
            dst_ref=gathered.at[place, pl.ds(gy, 1)],
            send_sem=all_send.at[place],
            recv_sem=all_recv.at[place],
            device_id=(x, partner),
            device_id_type=MESH,
        )

    def send(place, x, steps):
        for step in steps:
            exchange(place, x, lax.rem(gy + step, gy_size)).start()

    middle_step = gy_size // 2
    steps = sorted(range(gy_size), key=lambda step: abs(step - middle_step))
    for some in (steps[:7], steps[7:]):
        pl.when(has_left)(lambda: send(2, gx - 1, some))
        pl.when(has_right)(lambda: send(1, gx + 1, some))
        send(0, gx, [step for step in some if step])
    gathered[0, pl.ds(gy, 1), :] = table[0, pl.ds(gy, 1), :]

    def everyone(place, count):
        return pltpu.make_async_remote_copy(
            src_ref=table.at[min(place, 1), pl.ds(0, count)],
            dst_ref=gathered.at[place, pl.ds(0, count)],
            send_sem=all_send.at[place],
            recv_sem=all_recv.at[place],
            device_id=(gx, lax.rem(gy + 1, gy_size)),
            device_id_type=MESH,
        )

    column, from_left, from_right = everyone(0, gy_size - 1), everyone(1, gy_size), everyone(2, gy_size)
    second_x.wait_send()
    second_y.wait_send()
    column.wait_send()
    pl.when(has_left)(from_right.wait_send)
    pl.when(has_right)(from_left.wait_send)
    column.wait_recv()
    pl.when(has_left)(from_left.wait_recv)
    pl.when(has_right)(from_right.wait_recv)

    row = lax.broadcasted_iota(jnp.int32, (16, 128), 0)
    lower = (((lane >> 3) - row) & 1) == 0
    mixed[...] = gathered[0] + jnp.where(lower, gathered[1], gathered[2])

    lane = lax.broadcasted_iota(jnp.int32, (8, 128), 1)
    halves = [jnp.zeros((8, 128), jnp.float32) for _ in range(2)]
    for source in range(gy_size):
        spread = jnp.broadcast_to(mixed[pl.ds(source, 1), :], (8, 128))
        for half in range(2):
            turned = pltpu.roll(spread, 64 * half, 1, stride=8, stride_axis=0)
            halves[half] = jnp.where(lane >> 3 == source, turned, halves[half])
    for half in range(2):
        whole = halves[half]
        before = jnp.where(lane == 0, 0.0, pltpu.roll(whole, 1, 1))
        after = jnp.where(lane == 127, 0.0, pltpu.roll(whole, 127, 1))
        final[pl.ds(8 * half, 8), :] = 0.5 * whole + 0.25 * (before + after)


def finish(final, velocity_ref, magnitude_ref):
    for x in range(2):
        for z in range(2):
            fraction = final[pl.ds(8 * z + 6 + x, 1), :]
            divisor = jnp.maximum(fraction, 1.0)
            for component in range(3):
                voxels = final[pl.ds(8 * z + 2 * component + x, 1), :]
                velocity_ref[component, x, pl.ds(z, 1), :] = voxels / divisor / velocity_scale
            magnitude_ref[x, pl.ds(z, 1), :] = fraction / 64.0


def local(gx_size, gy_size, populations, fluid):
    padded = (NX + 2, NY + 2 * TOP, NZ)
    vmem, dma = pltpu.VMEM, pltpu.SemaphoreType.DMA
    f32 = jnp.float32
    blurred = pl.pallas_call(
        functools.partial(kernel, gx_size, gy_size),
        out_shape=jax.ShapeDtypeStruct((16, 128), f32),
        in_specs=[pl.BlockSpec(memory_space=pltpu.HBM)] * 2,
        out_specs=pl.BlockSpec(memory_space=pltpu.VMEM),
        scratch_shapes=[
            vmem((19, NX, NY, NZ), f32),
            vmem((NX, NY, NZ), jnp.int32),
            vmem((len(ORDER), *padded), f32),
            vmem((len(ORDER), *padded), f32),
            vmem((3, *padded), f32),
            vmem((256, 128), f32),
            vmem((32, 128), f32),
            vmem((256, 256), f32),
            vmem((2, 16, 128), f32),
            vmem((3, 16, 128), f32),
            vmem((16, 128), f32),
            pltpu.SemaphoreType.REGULAR((4,)),
            dma((8,)),
            dma,
            dma((2, 9)),
            dma((2, 9)),
            dma((3,)),
            dma((3,)),
        ],
        compiler_params=pltpu.CompilerParams(
            collective_id=0, has_side_effects=True, vmem_limit_bytes=55200 * 1024
        ),
    )(populations, fluid)
    velocity, magnitude = pl.pallas_call(
        finish,
        out_shape=(
            jax.ShapeDtypeStruct((3, 2, 2, 128), f32),
            jax.ShapeDtypeStruct((2, 2, 128), f32),
        ),
        in_specs=[pl.BlockSpec(memory_space=pltpu.VMEM)],
        out_specs=(pl.BlockSpec(memory_space=pltpu.VMEM),) * 2,
        compiler_params=pltpu.CompilerParams(vmem_limit_bytes=1024 * 1024),
    )(blurred)
    return jnp.swapaxes(velocity, 2, 3), jnp.swapaxes(magnitude, 1, 2)


def solution(mesh):
    return jax.shard_map(
        functools.partial(local, mesh.shape["gx"], mesh.shape["gy"]),
        mesh=mesh,
        in_specs=(P(None, "gx", "gy", None), P("gx", "gy", None)),
        out_specs=(P(None, "gx", None, "gy"), P("gx", None, "gy")),
        check_vma=False,
    )
```

```python
import functools

import jax
import jax.numpy as jnp
from jax import lax
from jax.experimental import pallas as pl
from jax.experimental.pallas import tpu as pltpu
from jax.sharding import PartitionSpec as P

MESH = pl.DeviceIdType.MESH

VELOCITIES = (
    (0, 0, 0),
    (1, 0, 0),
    (-1, 0, 0),
    (0, 1, 0),
    (0, -1, 0),
    (0, 0, 1),
    (0, 0, -1),
    (1, 1, 0),
    (-1, -1, 0),
    (1, -1, 0),
    (-1, 1, 0),
    (1, 0, 1),
    (-1, 0, -1),
    (1, 0, -1),
    (-1, 0, 1),
    (0, 1, 1),
    (0, -1, -1),
    (0, 1, -1),
    (0, -1, 1),
)
OPPOSITE = (0, 2, 1, 4, 3, 6, 5, 8, 7, 10, 9, 12, 11, 14, 13, 16, 15, 18, 17)
FLAG = -1
ORDER = (FLAG, 9, 1, 11, 13, 7, FLAG, 3, 15, 17, FLAG, 10, 2, 14, 12, 8, FLAG, 4, 18, 16, 0, 5, 6)
SLOT = tuple(ORDER.index(channel) for channel in range(19))
relax_rate = 1.0 / 0.6
velocity_scale = 0.002

NX, NY, NZ = 8, 32, 128
TOP = 8
LAST = TOP + NY - 1
TILES = NY // 8


def moments(f):
    s = [f[i] + f[i + 1] for i in range(1, 19, 2)]
    d = [f[i] - f[i + 1] for i in range(1, 19, 2)]
    rho = (f[0] + s[8]) + ((s[0] + s[1]) + (s[2] + s[3])) + ((s[4] + s[5]) + (s[6] + s[7]))
    mx = d[0] + (d[3] + d[4]) + (d[5] + d[6])
    my = d[1] + (d[3] - d[4]) + (d[7] + d[8])
    mz = d[2] + (d[5] - d[6]) + (d[7] - d[8])
    return rho, mx, my, mz


def collide(f):
    rho, mx, my, mz = moments(f)
    inverse = 1.0 / rho
    ux, uy, uz = mx * inverse, my * inverse, mz * inverse
    base = rho - 1.5 * (mx * ux + my * uy + mz * uz)
    keep = 1.0 - relax_rate
    relaxed = [keep * f[0] + (relax_rate / 3.0) * base]
    vx, vy, vz = 1.5 * ux, 1.5 * uy, 1.5 * uz
    near = (relax_rate / 18.0) * base
    far = (relax_rate / 36.0) * base
    ax, ay, az = (relax_rate / 6.0) * mx, (relax_rate / 6.0) * my, (relax_rate / 6.0) * mz
    bx, by, bz = 0.5 * ax, 0.5 * ay, 0.5 * az
    for channel, level, flow, speed in (
        (1, near, ax, vx),
        (3, near, ay, vy),
        (5, near, az, vz),
        (7, far, bx + by, vx + vy),
        (9, far, bx - by, vx - vy),
        (11, far, bx + bz, vx + vz),
        (13, far, bx - bz, vx - vz),
        (15, far, by + bz, vy + vz),
        (17, far, by - bz, vy - vz),
    ):
        even = level + flow * speed
        relaxed.append(keep * f[channel] + (even + flow))
        relaxed.append(keep * f[channel + 1] + (even - flow))
    return relaxed


def pulled(held, walls, x, tile):
    f = []
    for channel in range(19):
        cx, cy, cz = VELOCITIES[channel]
        rows = pl.ds(TOP + 8 * tile, 8)
        if channel == 0:
            f.append(held[SLOT[0], x + 1, rows, :])
            continue
        from_rows = pl.ds(TOP + 8 * tile - cy, 8)
        source = held[SLOT[channel], x + 1 - cx, from_rows, :]
        if cz:
            source = pltpu.roll(source, cz % NZ, 1)
        open_site = walls[cz % 3, x + 1 - cx, from_rows, :]
        f.append(jnp.where(open_site > 0, source, held[SLOT[OPPOSITE[channel]], x + 1, rows, :]))
    return f


def kernel(
    gx_size,
    gy_size,
    populations,
    fluid,
    final,
    start,
    solid,
    first,
    second,
    walls,
    sums,
    zmat,
    ymat,
    table,
    gathered,
    mixed,
    ready,
    load_sem,
    fluid_sem,
    halo_send,
    halo_recv,
    all_send,
    all_recv,
):
    gx, gy = lax.axis_index("gx"), lax.axis_index("gy")
    f32 = jnp.float32
    has_left, has_right = gx > 0, gx < gx_size - 1
    has_below, has_above = gy > 0, gy < gy_size - 1

    def number(*conditions):
        return sum(condition.astype(jnp.int32) for condition in conditions)

    barrier = pltpu.get_barrier_semaphore()
    beside_x = ((-1, has_left), (1, has_right), (0, None))
    beside_y = ((-1, has_below), (0, None), (1, has_above))
    for dx, in_x in beside_x:
        for dy, in_y in beside_y:
            if dx == 0 and dy == 0:
                continue
            there = in_y if in_x is None else in_x if in_y is None else in_x & in_y

            @pl.when(there)
            def _():
                pl.semaphore_signal(barrier, inc=1, device_id=(gx + dx, gy + dy), device_id_type=MESH)

    def load(x):
        return pltpu.make_async_copy(populations.at[:, x], start.at[:, x], load_sem.at[x])

    fluid_copy = pltpu.make_async_copy(fluid, solid, fluid_sem)
    load(7).start()
    load(0).start()
    fluid_copy.start()
    for x in range(1, NX - 1):
        load(x).start()

    def tell(stage):
        for way in (-(2**stage), 2**stage):

            @pl.when((gy + way >= 0) & (gy + way < gy_size))
            def _():
                pl.semaphore_signal(ready.at[stage], inc=1, device_id=(gx, gy + way), device_id_type=MESH)

    def hear(stage):
        pl.semaphore_wait(ready.at[stage], number(gy >= 2**stage, gy + 2**stage < gy_size))

    def lane_walls(slab, rows):
        flags = walls[0, slab, rows, :]
        lane = lax.broadcasted_iota(jnp.int32, flags.shape, flags.ndim - 1)
        walls[1, slab, rows, :] = jnp.where(lane == 0, 0.0, pltpu.roll(flags, 1, flags.ndim - 1))
        walls[2, slab, rows, :] = jnp.where(lane == NZ - 1, 0.0, pltpu.roll(flags, NZ - 1, flags.ndim - 1))

    def inner_walls(x, carry):
        for tile in range(TILES):
            rows = pl.ds(TOP + 8 * tile, 8)
            walls[0, x + 1, rows, :] = solid[x, pl.ds(8 * tile, 8), :].astype(jnp.float32)
            lane_walls(x + 1, rows)
        return carry

    def face_flags(x, carry):
        upper = solid[x, pl.ds(NY - 8, 8), :].astype(jnp.float32)
        lower = solid[x, pl.ds(0, 8), :].astype(jnp.float32)
        for slot in (6, 10):
            first[slot, x + 1, pl.ds(TOP + NY - 8, 8), :] = upper
            second[slot, x + 1, pl.ds(TOP + NY - 8, 8), :] = upper
        first[16, x + 1, pl.ds(TOP, 8), :] = lower
        second[16, x + 1, pl.ds(TOP, 8), :] = lower
        return carry

    inner, block = pl.ds(1, NX), pl.ds(TOP, NY)
    low, high = pl.ds(TOP - 1, 1), pl.ds(LAST + 1, 1)
    bottom, top = pl.ds(TOP, 1), pl.ds(LAST, 1)

    def x_sides(flags, cut):
        sides = []
        for start_row, count in ((TOP, cut), (TOP + cut, NY - cut)):
            rows = pl.ds(start_row, count)
            sides += [
                (pl.ds(1, 5 + flags), (NX, rows), (0, rows), (1, 0), has_right, has_left),
                (pl.ds(11, 5 + flags), (1, rows), (NX + 1, rows), (-1, 0), has_left, has_right),
            ]
        below_corners = [
            (pl.ds(1 - flags, 1 + flags), (NX, bottom), (0, high), (1, -1), has_right & has_below, has_left & has_above),
            (pl.ds(15, 1 + flags), (1, bottom), (NX + 1, high), (-1, -1), has_left & has_below, has_right & has_above),
        ]
        above_corners = [
            (pl.ds(5, 1 + flags), (NX, top), (0, low), (1, 1), has_right & has_above, has_left & has_below),
            (pl.ds(11 - flags, 1 + flags), (1, top), (NX + 1, low), (-1, 1), has_left & has_above, has_right & has_below),
        ]
        return below_corners + sides[:2] + above_corners + sides[2:]

    y_sides = [
        (pl.ds(5, 7), (inner, top), (inner, low), (0, 1), has_above, has_below),
        (pl.ds(15, 5), (inner, bottom), (inner, high), (0, -1), has_below, has_above),
        (pl.ds(1, 1), (inner, bottom), (inner, high), (0, -1), has_below, has_above),
    ]

    class Sides:
        def __init__(self, buffer, sides, send, recv, offset):
            self.copies = [
                (
                    pltpu.make_async_remote_copy(
                        src_ref=buffer.at[(channels, *source)],
                        dst_ref=buffer.at[(channels, *target)],
                        send_sem=send.at[offset + i],
                        recv_sem=recv.at[offset + i],
                        device_id=(gx + way[0], gy + way[1]),
                        device_id_type=MESH,
                    ),
                    sent,
                    arrives,
                )
                for i, (channels, source, target, way, sent, arrives) in enumerate(sides)
            ]

        def start(self, *which):
            for i in which or range(len(self.copies)):
                copy, sent, _ = self.copies[i]
                pl.when(sent)(copy.start)

        def wait_recv(self, *which):
            for i in which or range(len(self.copies)):
                copy, _, arrives = self.copies[i]
                pl.when(arrives)(copy.wait_recv)

        def wait_send(self):
            for copy, sent, _ in self.copies:
                pl.when(sent)(copy.wait_send)

    first_x = Sides(first, x_sides(1, 17), halo_send.at[0], halo_recv.at[0], 0)
    first_y = Sides(first, y_sides, halo_send.at[0], halo_recv.at[0], 8)
    second_x = Sides(second, x_sides(0, 16), halo_send.at[1], halo_recv.at[1], 0)
    second_y = Sides(second, y_sides, halo_send.at[1], halo_recv.at[1], 8)

    def relax_tile(x, tile):
        rows = pl.ds(8 * tile, 8)
        relaxed = collide([start[channel, x, rows, :] for channel in range(19)])
        for channel in range(19):
            first[SLOT[channel], x + 1, pl.ds(TOP + 8 * tile, 8), :] = relaxed[channel]

    def step_tile(x, tile):
        relaxed = collide(pulled(first, walls, x, tile))
        for channel in range(19):
            second[SLOT[channel], x + 1, pl.ds(TOP + 8 * tile, 8), :] = relaxed[channel]

    def sum_tile(x, tile):
        rho, mx, my, mz = moments(pulled(second, walls, x, tile))
        here = walls[0, x + 1, pl.ds(TOP + 8 * tile, 8), :]
        scale = here / rho
        for component, value in enumerate((mx * scale, my * scale, mz * scale, here)):
            rows = pl.ds(pl.multiple_of(component * 64 + (x // 4) * 32 + 8 * tile, 8), 8)
            sums[rows, :] = sums[rows, :] + value

    def over_slabs(body, edge, tiles):
        def inner_slab(x, carry):
            for tile in tiles:
                body(x, tile)
            return carry

        if edge:
            for tile in tiles:
                for x in (NX - 1, 0):
                    body(x, tile)
        else:
            lax.fori_loop(1, NX - 1, inner_slab, 0)

    every, outer, middle = range(TILES), (0, TILES - 1), range(1, TILES - 1)

    sums[...] = jnp.zeros(sums.shape, jnp.float32)
    row = lax.broadcasted_iota(jnp.int32, (32, NZ), 0)
    lane = lax.broadcasted_iota(jnp.int32, (32, NZ), 1)
    distance = jnp.abs(2 * (row & 15) + (row >> 4) - (lane >> 2))
    zmat[...] = jnp.where(distance == 0, 0.5, jnp.where(distance == 1, 0.25, 0.0)).astype(jnp.float32)

    turn = 8 * gy + 8

    def y_rows(step, carry):
        at = pl.multiple_of(8 * step, 8)
        row = (lax.broadcasted_iota(jnp.int32, (8, 256), 0) + (at - turn + 256)) & 127
        column = lax.broadcasted_iota(jnp.int32, (8, 256), 1)
        hit = (((row >> 4) & 3) == 3 - (column >> 6)) & ((row & 7) == ((column >> 2) & 7))
        same = ((row >> 3) & 1) != ((column >> 5) & 1)
        ymat[pl.ds(at, 8), :] = jnp.where(hit, jnp.where(same, 0.5, 0.25), 0.0)
        ymat[pl.ds(pl.multiple_of(at + 128, 8), 8), :] = jnp.where(hit & ~same, 0.25, 0.0)
        return carry

    lax.fori_loop(0, 16, y_rows, 0)

    @pl.when(gx == 0)
    def _():
        first[6, 0, pl.ds(TOP, NY), :] = jnp.zeros((NY, NZ), f32)
        first[6, 0, low, :] = jnp.zeros((1, NZ), f32)
        first[0, 0, high, :] = jnp.zeros((1, NZ), f32)
        gathered[1] = jnp.zeros((16, 128), f32)

    @pl.when(gx == gx_size - 1)
    def _():
        first[16, NX + 1, pl.ds(TOP, NY), :] = jnp.zeros((NY, NZ), f32)
        first[10, NX + 1, low, :] = jnp.zeros((1, NZ), f32)
        first[16, NX + 1, high, :] = jnp.zeros((1, NZ), f32)
        gathered[2] = jnp.zeros((16, 128), f32)

    @pl.when(gy == 0)
    def _():
        first[6, inner, TOP - 1, :] = jnp.zeros((NX, NZ), f32)
        first[6, 0, low, :] = jnp.zeros((1, NZ), f32)
        first[10, NX + 1, low, :] = jnp.zeros((1, NZ), f32)

    @pl.when(gy == gy_size - 1)
    def _():
        first[16, inner, LAST + 1, :] = jnp.zeros((NX, NZ), f32)
        first[0, 0, high, :] = jnp.zeros((1, NZ), f32)
        first[16, NX + 1, high, :] = jnp.zeros((1, NZ), f32)

    load(7).wait()
    load(0).wait()
    over_slabs(relax_tile, True, every)
    fluid_copy.wait()
    lax.fori_loop(0, NX, face_flags, 0)
    for tile in range(TILES):
        rows, own = pl.ds(TOP + 8 * tile, 8), pl.ds(8 * tile, 8)
        first[6, NX, rows, :] = solid[NX - 1, own, :].astype(f32)
        first[16, 1, rows, :] = solid[0, own, :].astype(f32)
    first[0, NX, pl.ds(TOP, 8), :] = solid[NX - 1, pl.ds(0, 8), :].astype(f32)
    for x in range(1, NX - 1):
        load(x).wait()
    over_slabs(relax_tile, False, outer)
    pl.semaphore_wait(barrier, (1 + number(has_left, has_right)) * (1 + number(has_below, has_above)) - 1)
    first_x.start(0, 1, 4, 5, 2, 3, 6, 7)
    first_y.start()
    tell(0)

    over_slabs(relax_tile, False, middle)
    lax.fori_loop(0, NX, inner_walls, 0)
    over_slabs(step_tile, False, middle)
    hear(0)
    tell(1)

    first_y.wait_recv()
    for slot, row in ((6, TOP - 1), (16, LAST + 1)):
        walls[0, inner, row, :] = first[slot, inner, row, :]
        lane_walls(inner, row)
    over_slabs(step_tile, False, outer)
    hear(1)
    tell(2)
    first_x.wait_recv(2, 3, 4, 5)
    for slot, slab, row in ((6, 0, low), (10, NX + 1, low), (6, 0, pl.ds(TOP + 16, 1)), (16, NX + 1, pl.ds(TOP + 16, 1))):
        walls[0, slab, row, :] = first[slot, slab, row, :]

    def halo_walls(tiles):
        for slot, slab in ((6, 0), (16, NX + 1)):
            for tile in tiles:
                rows = pl.ds(TOP + 8 * tile, 8)
                walls[0, slab, rows, :] = first[slot, slab, rows, :]
                lane_walls(slab, rows)

    halo_walls((0, 1))
    over_slabs(step_tile, True, (0, 1))
    second_x.start(0, 1, 2, 3)
    first_x.wait_recv(0, 1, 6, 7)
    for slot, slab, row in ((0, 0, high), (16, NX + 1, high)):
        walls[0, slab, row, :] = first[slot, slab, row, :]
    halo_walls((2, 3))
    over_slabs(step_tile, True, (2, 3))
    second_x.start(4, 5, 6, 7)
    second_y.start()
    hear(2)
    tell(3)

    over_slabs(sum_tile, False, middle)
    for sides in (first_x, first_y):
        sides.wait_send()
    second_y.wait_recv()
    over_slabs(sum_tile, False, outer)
    second_x.wait_recv()
    over_slabs(sum_tile, True, every)

    def parts(value):
        upper = value.astype(jnp.bfloat16)
        return upper, (value - upper.astype(jnp.float32)).astype(jnp.bfloat16)

    weights = ymat[...].astype(jnp.bfloat16)
    over_y = sum(jnp.dot(weights, part, preferred_element_type=jnp.float32) for part in parts(sums[...]))
    weights = zmat[...].astype(jnp.bfloat16)
    over_z = sum(
        lax.dot_general(weights, part, (((1,), (1,)), ((), ())), preferred_element_type=jnp.float32)
        for part in parts(over_y)
    )
    lane = lax.broadcasted_iota(jnp.int32, (16, 128), 1)
    first_z = ((lane - turn + 256) & 64) != 0
    for part in range(2):
        lanes = slice(128 * part, 128 * part + 128)
        table[part] = jnp.where(first_z, over_z[:16, lanes], over_z[16:, lanes])
    hear(3)

    def exchange(place, x, partner):
        return pltpu.make_async_remote_copy(
            src_ref=table.at[min(place, 1), pl.ds(partner, 1)],
            dst_ref=gathered.at[place, pl.ds(gy, 1)],
            send_sem=all_send.at[place],
            recv_sem=all_recv.at[place],
            device_id=(x, partner),
            device_id_type=MESH,
        )

    def send(place, x, steps):
        for step in steps:
            exchange(place, x, lax.rem(gy + step, gy_size)).start()

    middle_step = gy_size // 2
    steps = sorted(range(gy_size), key=lambda step: abs(step - middle_step))
    for some in (steps[:7], steps[7:]):
        pl.when(has_left)(lambda: send(2, gx - 1, some))
        pl.when(has_right)(lambda: send(1, gx + 1, some))
        send(0, gx, [step for step in some if step])
    gathered[0, pl.ds(gy, 1), :] = table[0, pl.ds(gy, 1), :]

    def everyone(place, count):
        return pltpu.make_async_remote_copy(
            src_ref=table.at[min(place, 1), pl.ds(0, count)],
            dst_ref=gathered.at[place, pl.ds(0, count)],
            send_sem=all_send.at[place],
            recv_sem=all_recv.at[place],
            device_id=(gx, lax.rem(gy + 1, gy_size)),
            device_id_type=MESH,
        )

    column, from_left, from_right = everyone(0, gy_size - 1), everyone(1, gy_size), everyone(2, gy_size)
    second_x.wait_send()
    second_y.wait_send()
    column.wait_send()
    pl.when(has_left)(from_right.wait_send)
    pl.when(has_right)(from_left.wait_send)
    column.wait_recv()
    pl.when(has_left)(from_left.wait_recv)
    pl.when(has_right)(from_right.wait_recv)

    row = lax.broadcasted_iota(jnp.int32, (16, 128), 0)
    lower = (((lane >> 3) - row) & 1) == 0
    mixed[...] = gathered[0] + jnp.where(lower, gathered[1], gathered[2])

    lane = lax.broadcasted_iota(jnp.int32, (8, 128), 1)
    halves = [jnp.zeros((8, 128), jnp.float32) for _ in range(2)]
    for source in range(gy_size):
        spread = jnp.broadcast_to(mixed[pl.ds(source, 1), :], (8, 128))
        for half in range(2):
            turned = pltpu.roll(spread, 64 * half, 1, stride=8, stride_axis=0)
            halves[half] = jnp.where(lane >> 3 == source, turned, halves[half])
    for half in range(2):
        whole = halves[half]
        before = jnp.where(lane == 0, 0.0, pltpu.roll(whole, 1, 1))
        after = jnp.where(lane == 127, 0.0, pltpu.roll(whole, 127, 1))
        final[pl.ds(8 * half, 8), :] = 0.5 * whole + 0.25 * (before + after)


def finish(final, velocity_ref, magnitude_ref):
    for x in range(2):
        for z in range(2):
            fraction = final[pl.ds(8 * z + 6 + x, 1), :]
            divisor = jnp.maximum(fraction, 1.0)
            for component in range(3):
                voxels = final[pl.ds(8 * z + 2 * component + x, 1), :]
                velocity_ref[component, x, pl.ds(z, 1), :] = voxels / divisor / velocity_scale
            magnitude_ref[x, pl.ds(z, 1), :] = fraction / 64.0


def local(gx_size, gy_size, populations, fluid):
    padded = (NX + 2, NY + 2 * TOP, NZ)
    vmem, dma = pltpu.VMEM, pltpu.SemaphoreType.DMA
    f32 = jnp.float32
    blurred = pl.pallas_call(
        functools.partial(kernel, gx_size, gy_size),
        out_shape=jax.ShapeDtypeStruct((16, 128), f32),
        in_specs=[pl.BlockSpec(memory_space=pltpu.HBM)] * 2,
        out_specs=pl.BlockSpec(memory_space=pltpu.VMEM),
        scratch_shapes=[
            vmem((19, NX, NY, NZ), f32),
            vmem((NX, NY, NZ), jnp.int32),
            vmem((len(ORDER), *padded), f32),
            vmem((len(ORDER), *padded), f32),
            vmem((3, *padded), f32),
            vmem((256, 128), f32),
            vmem((32, 128), f32),
            vmem((256, 256), f32),
            vmem((2, 16, 128), f32),
            vmem((3, 16, 128), f32),
            vmem((16, 128), f32),
            pltpu.SemaphoreType.REGULAR((4,)),
            dma((8,)),
            dma,
            dma((2, 11)),
            dma((2, 11)),
            dma((3,)),
            dma((3,)),
        ],
        compiler_params=pltpu.CompilerParams(
            collective_id=0, has_side_effects=True, vmem_limit_bytes=55200 * 1024
        ),
    )(populations, fluid)
    velocity, magnitude = pl.pallas_call(
        finish,
        out_shape=(
            jax.ShapeDtypeStruct((3, 2, 2, 128), f32),
            jax.ShapeDtypeStruct((2, 2, 128), f32),
        ),
        in_specs=[pl.BlockSpec(memory_space=pltpu.VMEM)],
        out_specs=(pl.BlockSpec(memory_space=pltpu.VMEM),) * 2,
        compiler_params=pltpu.CompilerParams(vmem_limit_bytes=1024 * 1024),
    )(blurred)
    return jnp.swapaxes(velocity, 2, 3), jnp.swapaxes(magnitude, 1, 2)


def solution(mesh):
    return jax.shard_map(
        functools.partial(local, mesh.shape["gx"], mesh.shape["gy"]),
        mesh=mesh,
        in_specs=(P(None, "gx", "gy", None), P("gx", "gy", None)),
        out_specs=(P(None, "gx", None, "gy"), P("gx", None, "gy")),
        check_vma=False,
    )
```

```python
import functools

import jax
import jax.numpy as jnp
from jax import lax
from jax.experimental import pallas as pl
from jax.experimental.pallas import tpu as pltpu
from jax.sharding import PartitionSpec as P

MESH = pl.DeviceIdType.MESH

VELOCITIES = (
    (0, 0, 0),
    (1, 0, 0),
    (-1, 0, 0),
    (0, 1, 0),
    (0, -1, 0),
    (0, 0, 1),
    (0, 0, -1),
    (1, 1, 0),
    (-1, -1, 0),
    (1, -1, 0),
    (-1, 1, 0),
    (1, 0, 1),
    (-1, 0, -1),
    (1, 0, -1),
    (-1, 0, 1),
    (0, 1, 1),
    (0, -1, -1),
    (0, 1, -1),
    (0, -1, 1),
)
OPPOSITE = (0, 2, 1, 4, 3, 6, 5, 8, 7, 10, 9, 12, 11, 14, 13, 16, 15, 18, 17)
FLAG = -1
ORDER = (FLAG, 9, 1, 11, 13, 7, FLAG, 3, 15, 17, FLAG, 10, 2, 14, 12, 8, FLAG, 4, 18, 16, 0, 5, 6)
SLOT = tuple(ORDER.index(channel) for channel in range(19))
relax_rate = 1.0 / 0.6
velocity_scale = 0.002

NX, NY, NZ = 8, 32, 128
TOP = 8
LAST = TOP + NY - 1
TILES = NY // 8


def moments(f):
    s = [f[i] + f[i + 1] for i in range(1, 19, 2)]
    d = [f[i] - f[i + 1] for i in range(1, 19, 2)]
    rho = (f[0] + s[8]) + ((s[0] + s[1]) + (s[2] + s[3])) + ((s[4] + s[5]) + (s[6] + s[7]))
    mx = d[0] + (d[3] + d[4]) + (d[5] + d[6])
    my = d[1] + (d[3] - d[4]) + (d[7] + d[8])
    mz = d[2] + (d[5] - d[6]) + (d[7] - d[8])
    return rho, mx, my, mz


def collide(f):
    rho, mx, my, mz = moments(f)
    inverse = 1.0 / rho
    ux, uy, uz = mx * inverse, my * inverse, mz * inverse
    base = rho - 1.5 * (mx * ux + my * uy + mz * uz)
    keep = 1.0 - relax_rate
    relaxed = [keep * f[0] + (relax_rate / 3.0) * base]
    vx, vy, vz = 1.5 * ux, 1.5 * uy, 1.5 * uz
    near = (relax_rate / 18.0) * base
    far = (relax_rate / 36.0) * base
    ax, ay, az = (relax_rate / 6.0) * mx, (relax_rate / 6.0) * my, (relax_rate / 6.0) * mz
    bx, by, bz = 0.5 * ax, 0.5 * ay, 0.5 * az
    for channel, level, flow, speed in (
        (1, near, ax, vx),
        (3, near, ay, vy),
        (5, near, az, vz),
        (7, far, bx + by, vx + vy),
        (9, far, bx - by, vx - vy),
        (11, far, bx + bz, vx + vz),
        (13, far, bx - bz, vx - vz),
        (15, far, by + bz, vy + vz),
        (17, far, by - bz, vy - vz),
    ):
        even = level + flow * speed
        relaxed.append(keep * f[channel] + (even + flow))
        relaxed.append(keep * f[channel + 1] + (even - flow))
    return relaxed


def pulled(held, walls, x, tile):
    f = []
    for channel in range(19):
        cx, cy, cz = VELOCITIES[channel]
        rows = pl.ds(TOP + 8 * tile, 8)
        if channel == 0:
            f.append(held[SLOT[0], x + 1, rows, :])
            continue
        from_rows = pl.ds(TOP + 8 * tile - cy, 8)
        source = held[SLOT[channel], x + 1 - cx, from_rows, :]
        if cz:
            source = pltpu.roll(source, cz % NZ, 1)
        open_site = walls[cz % 3, x + 1 - cx, from_rows, :]
        f.append(jnp.where(open_site > 0, source, held[SLOT[OPPOSITE[channel]], x + 1, rows, :]))
    return f


def kernel(
    gx_size,
    gy_size,
    populations,
    fluid,
    final,
    start,
    solid,
    first,
    second,
    walls,
    sums,
    zmat,
    ymat,
    table,
    gathered,
    mixed,
    ready,
    load_sem,
    fluid_sem,
    halo_send,
    halo_recv,
    all_send,
    all_recv,
):
    gx, gy = lax.axis_index("gx"), lax.axis_index("gy")
    f32 = jnp.float32
    has_left, has_right = gx > 0, gx < gx_size - 1
    has_below, has_above = gy > 0, gy < gy_size - 1

    def number(*conditions):
        return sum(condition.astype(jnp.int32) for condition in conditions)

    barrier = pltpu.get_barrier_semaphore()
    beside_x = ((-1, has_left), (1, has_right), (0, None))
    beside_y = ((-1, has_below), (0, None), (1, has_above))
    for dx, in_x in beside_x:
        for dy, in_y in beside_y:
            if dx == 0 and dy == 0:
                continue
            there = in_y if in_x is None else in_x if in_y is None else in_x & in_y

            @pl.when(there)
            def _():
                pl.semaphore_signal(barrier, inc=1, device_id=(gx + dx, gy + dy), device_id_type=MESH)

    def load(x):
        return pltpu.make_async_copy(populations.at[:, x], start.at[:, x], load_sem.at[x])

    fluid_copy = pltpu.make_async_copy(fluid, solid, fluid_sem)
    load(7).start()
    load(0).start()
    fluid_copy.start()
    for x in range(1, NX - 1):
        load(x).start()

    def tell(stage):
        for way in (-(2**stage), 2**stage):

            @pl.when((gy + way >= 0) & (gy + way < gy_size))
            def _():
                pl.semaphore_signal(ready.at[stage], inc=1, device_id=(gx, gy + way), device_id_type=MESH)

    def hear(stage):
        pl.semaphore_wait(ready.at[stage], number(gy >= 2**stage, gy + 2**stage < gy_size))

    def lane_walls(slab, rows):
        flags = walls[0, slab, rows, :]
        lane = lax.broadcasted_iota(jnp.int32, flags.shape, flags.ndim - 1)
        walls[1, slab, rows, :] = jnp.where(lane == 0, 0.0, pltpu.roll(flags, 1, flags.ndim - 1))
        walls[2, slab, rows, :] = jnp.where(lane == NZ - 1, 0.0, pltpu.roll(flags, NZ - 1, flags.ndim - 1))

    def inner_walls(x, carry):
        for tile in range(TILES):
            rows = pl.ds(TOP + 8 * tile, 8)
            walls[0, x + 1, rows, :] = solid[x, pl.ds(8 * tile, 8), :].astype(jnp.float32)
            lane_walls(x + 1, rows)
        return carry

    def face_flags(x, carry):
        upper = solid[x, pl.ds(NY - 8, 8), :].astype(jnp.float32)
        lower = solid[x, pl.ds(0, 8), :].astype(jnp.float32)
        for slot in (6, 10):
            first[slot, x + 1, pl.ds(TOP + NY - 8, 8), :] = upper
            second[slot, x + 1, pl.ds(TOP + NY - 8, 8), :] = upper
        first[16, x + 1, pl.ds(TOP, 8), :] = lower
        second[16, x + 1, pl.ds(TOP, 8), :] = lower
        return carry

    inner, block = pl.ds(1, NX), pl.ds(TOP, NY)
    low, high = pl.ds(TOP - 1, 1), pl.ds(LAST + 1, 1)
    bottom, top = pl.ds(TOP, 1), pl.ds(LAST, 1)

    def x_sides(flags, cut):
        sides = []
        for start_row, count in ((TOP, cut), (TOP + cut, NY - cut)):
            rows = pl.ds(start_row, count)
            sides += [
                (pl.ds(1, 5 + flags), (NX, rows), (0, rows), (1, 0), has_right, has_left),
                (pl.ds(11, 5 + flags), (1, rows), (NX + 1, rows), (-1, 0), has_left, has_right),
            ]
        below_corners = [
            (pl.ds(1 - flags, 1 + flags), (NX, bottom), (0, high), (1, -1), has_right & has_below, has_left & has_above),
            (pl.ds(15, 1 + flags), (1, bottom), (NX + 1, high), (-1, -1), has_left & has_below, has_right & has_above),
        ]
        above_corners = [
            (pl.ds(5, 1 + flags), (NX, top), (0, low), (1, 1), has_right & has_above, has_left & has_below),
            (pl.ds(11 - flags, 1 + flags), (1, top), (NX + 1, low), (-1, 1), has_left & has_above, has_right & has_below),
        ]
        return below_corners + sides[:2] + above_corners + sides[2:]

    y_sides = [
        (pl.ds(5, 7), (inner, top), (inner, low), (0, 1), has_above, has_below),
        (pl.ds(15, 5), (inner, bottom), (inner, high), (0, -1), has_below, has_above),
        (pl.ds(1, 1), (inner, bottom), (inner, high), (0, -1), has_below, has_above),
    ]

    class Sides:
        def __init__(self, buffer, sides, send, recv, offset):
            self.copies = [
                (
                    pltpu.make_async_remote_copy(
                        src_ref=buffer.at[(channels, *source)],
                        dst_ref=buffer.at[(channels, *target)],
                        send_sem=send.at[offset + i],
                        recv_sem=recv.at[offset + i],
                        device_id=(gx + way[0], gy + way[1]),
                        device_id_type=MESH,
                    ),
                    sent,
                    arrives,
                )
                for i, (channels, source, target, way, sent, arrives) in enumerate(sides)
            ]

        def start(self, *which):
            for i in which or range(len(self.copies)):
                copy, sent, _ = self.copies[i]
                pl.when(sent)(copy.start)

        def wait_recv(self, *which):
            for i in which or range(len(self.copies)):
                copy, _, arrives = self.copies[i]
                pl.when(arrives)(copy.wait_recv)

        def wait_send(self):
            for copy, sent, _ in self.copies:
                pl.when(sent)(copy.wait_send)

    first_x = Sides(first, x_sides(1, 17), halo_send.at[0], halo_recv.at[0], 0)
    first_y = Sides(first, y_sides, halo_send.at[0], halo_recv.at[0], 8)
    second_x = Sides(second, x_sides(0, 16), halo_send.at[1], halo_recv.at[1], 0)
    second_y = Sides(second, y_sides, halo_send.at[1], halo_recv.at[1], 8)

    def relax_tile(x, tile):
        rows = pl.ds(8 * tile, 8)
        relaxed = collide([start[channel, x, rows, :] for channel in range(19)])
        for channel in range(19):
            first[SLOT[channel], x + 1, pl.ds(TOP + 8 * tile, 8), :] = relaxed[channel]

    def step_tile(x, tile):
        relaxed = collide(pulled(first, walls, x, tile))
        for channel in range(19):
            second[SLOT[channel], x + 1, pl.ds(TOP + 8 * tile, 8), :] = relaxed[channel]

    def sum_tile(x, tile):
        rho, mx, my, mz = moments(pulled(second, walls, x, tile))
        here = walls[0, x + 1, pl.ds(TOP + 8 * tile, 8), :]
        scale = here / rho
        for component, value in enumerate((mx * scale, my * scale, mz * scale, here)):
            rows = pl.ds(pl.multiple_of(component * 64 + (x // 4) * 32 + 8 * tile, 8), 8)
            sums[rows, :] = sums[rows, :] + value

    def over_slabs(body, edge, tiles):
        def inner_slab(x, carry):
            for tile in tiles:
                body(x, tile)
            return carry

        if edge:
            for tile in tiles:
                for x in (NX - 1, 0):
                    body(x, tile)
        else:
            lax.fori_loop(1, NX - 1, inner_slab, 0)

    every, outer, middle = range(TILES), (0, TILES - 1), range(1, TILES - 1)

    sums[...] = jnp.zeros(sums.shape, jnp.float32)
    row = lax.broadcasted_iota(jnp.int32, (32, NZ), 0)
    lane = lax.broadcasted_iota(jnp.int32, (32, NZ), 1)
    distance = jnp.abs(2 * (row & 15) + (row >> 4) - (lane >> 2))
    zmat[...] = jnp.where(distance == 0, 0.5, jnp.where(distance == 1, 0.25, 0.0)).astype(jnp.bfloat16)

    turn = 8 * gy + 8

    def y_rows(step, carry):
        at = pl.multiple_of(16 * step, 16)
        row = (lax.broadcasted_iota(jnp.int32, (16, 256), 0) + (at - turn + 256)) & 127
        column = lax.broadcasted_iota(jnp.int32, (16, 256), 1)
        hit = (((row >> 4) & 3) == 3 - (column >> 6)) & ((row & 7) == ((column >> 2) & 7))
        same = ((row >> 3) & 1) != ((column >> 5) & 1)
        ymat[pl.ds(at, 16), :] = jnp.where(hit, jnp.where(same, 0.5, 0.25), 0.0).astype(jnp.bfloat16)
        ymat[pl.ds(pl.multiple_of(at + 128, 16), 16), :] = jnp.where(hit & ~same, 0.25, 0.0).astype(jnp.bfloat16)
        return carry

    lax.fori_loop(0, 8, y_rows, 0)

    @pl.when(gx == 0)
    def _():
        first[6, 0, pl.ds(TOP, NY), :] = jnp.zeros((NY, NZ), f32)
        first[6, 0, low, :] = jnp.zeros((1, NZ), f32)
        first[0, 0, high, :] = jnp.zeros((1, NZ), f32)
        gathered[1] = jnp.zeros((16, 128), f32)

    @pl.when(gx == gx_size - 1)
    def _():
        first[16, NX + 1, pl.ds(TOP, NY), :] = jnp.zeros((NY, NZ), f32)
        first[10, NX + 1, low, :] = jnp.zeros((1, NZ), f32)
        first[16, NX + 1, high, :] = jnp.zeros((1, NZ), f32)
        gathered[2] = jnp.zeros((16, 128), f32)

    @pl.when(gy == 0)
    def _():
        first[6, inner, TOP - 1, :] = jnp.zeros((NX, NZ), f32)
        first[6, 0, low, :] = jnp.zeros((1, NZ), f32)
        first[10, NX + 1, low, :] = jnp.zeros((1, NZ), f32)

    @pl.when(gy == gy_size - 1)
    def _():
        first[16, inner, LAST + 1, :] = jnp.zeros((NX, NZ), f32)
        first[0, 0, high, :] = jnp.zeros((1, NZ), f32)
        first[16, NX + 1, high, :] = jnp.zeros((1, NZ), f32)

    load(7).wait()
    load(0).wait()
    over_slabs(relax_tile, True, every)
    fluid_copy.wait()
    lax.fori_loop(0, NX, face_flags, 0)
    for tile in range(TILES):
        rows, own = pl.ds(TOP + 8 * tile, 8), pl.ds(8 * tile, 8)
        first[6, NX, rows, :] = solid[NX - 1, own, :].astype(f32)
        first[16, 1, rows, :] = solid[0, own, :].astype(f32)
    first[0, NX, pl.ds(TOP, 8), :] = solid[NX - 1, pl.ds(0, 8), :].astype(f32)
    for x in range(1, NX - 1):
        load(x).wait()
    over_slabs(relax_tile, False, outer)
    pl.semaphore_wait(barrier, (1 + number(has_left, has_right)) * (1 + number(has_below, has_above)) - 1)
    first_x.start(0, 1, 4, 5, 2, 3, 6, 7)
    first_y.start()
    tell(0)

    over_slabs(relax_tile, False, middle)
    lax.fori_loop(0, NX, inner_walls, 0)
    over_slabs(step_tile, False, middle)
    hear(0)
    tell(1)

    first_y.wait_recv()
    for slot, row in ((6, TOP - 1), (16, LAST + 1)):
        walls[0, inner, row, :] = first[slot, inner, row, :]
        lane_walls(inner, row)
    over_slabs(step_tile, False, outer)
    hear(1)
    tell(2)
    first_x.wait_recv(2, 3, 4, 5)
    for slot, slab, row in ((6, 0, low), (10, NX + 1, low), (6, 0, pl.ds(TOP + 16, 1)), (16, NX + 1, pl.ds(TOP + 16, 1))):
        walls[0, slab, row, :] = first[slot, slab, row, :]

    def halo_walls(tiles):
        for slot, slab in ((6, 0), (16, NX + 1)):
            for tile in tiles:
                rows = pl.ds(TOP + 8 * tile, 8)
                walls[0, slab, rows, :] = first[slot, slab, rows, :]
                lane_walls(slab, rows)

    halo_walls((0, 1))
    over_slabs(step_tile, True, (0, 1))
    second_x.start(0, 1, 2, 3)
    first_x.wait_recv(0, 1, 6, 7)
    for slot, slab, row in ((0, 0, high), (16, NX + 1, high)):
        walls[0, slab, row, :] = first[slot, slab, row, :]
    halo_walls((2, 3))
    over_slabs(step_tile, True, (2, 3))
    second_x.start(4, 5, 6, 7)
    second_y.start()
    hear(2)
    tell(3)

    over_slabs(sum_tile, False, middle)
    for sides in (first_x, first_y):
        sides.wait_send()
    second_y.wait_recv()
    over_slabs(sum_tile, False, outer)
    second_x.wait_recv()
    over_slabs(sum_tile, True, every)

    def parts(value):
        upper = value.astype(jnp.bfloat16)
        return upper, (value - upper.astype(jnp.float32)).astype(jnp.bfloat16)

    weights = ymat[...]
    over_y = sum(jnp.dot(weights, part, preferred_element_type=jnp.float32) for part in parts(sums[...]))
    weights = zmat[...]
    over_z = sum(
        lax.dot_general(weights, part, (((1,), (1,)), ((), ())), preferred_element_type=jnp.float32)
        for part in parts(over_y)
    )
    lane = lax.broadcasted_iota(jnp.int32, (16, 128), 1)
    first_z = ((lane - turn + 256) & 64) != 0
    for part in range(2):
        lanes = slice(128 * part, 128 * part + 128)
        table[part] = jnp.where(first_z, over_z[:16, lanes], over_z[16:, lanes])
    hear(3)

    def exchange(place, x, partner):
        return pltpu.make_async_remote_copy(
            src_ref=table.at[min(place, 1), pl.ds(partner, 1)],
            dst_ref=gathered.at[place, pl.ds(gy, 1)],
            send_sem=all_send.at[place],
            recv_sem=all_recv.at[place],
            device_id=(x, partner),
            device_id_type=MESH,
        )

    def send(place, x, steps):
        for step in steps:
            exchange(place, x, lax.rem(gy + step, gy_size)).start()

    middle_step = gy_size // 2
    steps = sorted(range(gy_size), key=lambda step: abs(step - middle_step))
    for some in (steps[:7], steps[7:]):
        pl.when(has_right)(lambda: send(1, gx + 1, some))
        send(0, gx, [step for step in some if step])
        pl.when(has_left)(lambda: send(2, gx - 1, some))
    gathered[0, pl.ds(gy, 1), :] = table[0, pl.ds(gy, 1), :]

    def everyone(place, count):
        return pltpu.make_async_remote_copy(
            src_ref=table.at[min(place, 1), pl.ds(0, count)],
            dst_ref=gathered.at[place, pl.ds(0, count)],
            send_sem=all_send.at[place],
            recv_sem=all_recv.at[place],
            device_id=(gx, lax.rem(gy + 1, gy_size)),
            device_id_type=MESH,
        )

    column, from_left, from_right = everyone(0, gy_size - 1), everyone(1, gy_size), everyone(2, gy_size)
    second_x.wait_send()
    second_y.wait_send()
    column.wait_send()
    pl.when(has_left)(from_right.wait_send)
    pl.when(has_right)(from_left.wait_send)
    column.wait_recv()
    pl.when(has_left)(from_left.wait_recv)
    pl.when(has_right)(from_right.wait_recv)

    row = lax.broadcasted_iota(jnp.int32, (16, 128), 0)
    lower = (((lane >> 3) - row) & 1) == 0
    mixed[...] = gathered[0] + jnp.where(lower, gathered[1], gathered[2])

    lane = lax.broadcasted_iota(jnp.int32, (8, 128), 1)
    halves = [jnp.zeros((8, 128), jnp.float32) for _ in range(2)]
    for source in range(gy_size):
        spread = jnp.broadcast_to(mixed[pl.ds(source, 1), :], (8, 128))
        for half in range(2):
            turned = pltpu.roll(spread, 64 * half, 1, stride=8, stride_axis=0)
            halves[half] = jnp.where(lane >> 3 == source, turned, halves[half])
    for half in range(2):
        whole = halves[half]
        before = jnp.where(lane == 0, 0.0, pltpu.roll(whole, 1, 1))
        after = jnp.where(lane == 127, 0.0, pltpu.roll(whole, 127, 1))
        final[pl.ds(8 * half, 8), :] = 0.5 * whole + 0.25 * (before + after)


def finish(final, velocity_ref, magnitude_ref):
    for x in range(2):
        for z in range(2):
            fraction = final[pl.ds(8 * z + 6 + x, 1), :]
            scale = 1.0 / (jnp.maximum(fraction, 1.0) * velocity_scale)
            for component in range(3):
                voxels = final[pl.ds(8 * z + 2 * component + x, 1), :]
                velocity_ref[component, x, pl.ds(z, 1), :] = voxels * scale
            magnitude_ref[x, pl.ds(z, 1), :] = fraction / 64.0


def local(gx_size, gy_size, populations, fluid):
    padded = (NX + 2, NY + 2 * TOP, NZ)
    vmem, dma = pltpu.VMEM, pltpu.SemaphoreType.DMA
    f32 = jnp.float32
    blurred = pl.pallas_call(
        functools.partial(kernel, gx_size, gy_size),
        out_shape=jax.ShapeDtypeStruct((16, 128), f32),
        in_specs=[pl.BlockSpec(memory_space=pltpu.HBM)] * 2,
        out_specs=pl.BlockSpec(memory_space=pltpu.VMEM),
        scratch_shapes=[
            vmem((19, NX, NY, NZ), f32),
            vmem((NX, NY, NZ), jnp.int32),
            vmem((len(ORDER), *padded), f32),
            vmem((len(ORDER), *padded), f32),
            vmem((3, *padded), f32),
            vmem((256, 128), f32),
            vmem((32, 128), jnp.bfloat16),
            vmem((256, 256), jnp.bfloat16),
            vmem((2, 16, 128), f32),
            vmem((3, 16, 128), f32),
            vmem((16, 128), f32),
            pltpu.SemaphoreType.REGULAR((4,)),
            dma((8,)),
            dma,
            dma((2, 11)),
            dma((2, 11)),
            dma((3,)),
            dma((3,)),
        ],
        compiler_params=pltpu.CompilerParams(
            collective_id=0, has_side_effects=True, vmem_limit_bytes=55200 * 1024
        ),
    )(populations, fluid)
    velocity, magnitude = pl.pallas_call(
        finish,
        out_shape=(
            jax.ShapeDtypeStruct((3, 2, 2, 128), f32),
            jax.ShapeDtypeStruct((2, 2, 128), f32),
        ),
        in_specs=[pl.BlockSpec(memory_space=pltpu.VMEM)],
        out_specs=(pl.BlockSpec(memory_space=pltpu.VMEM),) * 2,
        compiler_params=pltpu.CompilerParams(vmem_limit_bytes=1024 * 1024),
    )(blurred)
    return jnp.swapaxes(velocity, 2, 3), jnp.swapaxes(magnitude, 1, 2)


def solution(mesh):
    return jax.shard_map(
        functools.partial(local, mesh.shape["gx"], mesh.shape["gy"]),
        mesh=mesh,
        in_specs=(P(None, "gx", "gy", None), P("gx", "gy", None)),
        out_specs=(P(None, "gx", None, "gy"), P("gx", None, "gy")),
        check_vma=False,
    )
```

```python
import functools

import jax
import jax.numpy as jnp
from jax import lax
from jax.experimental import pallas as pl
from jax.experimental.pallas import tpu as pltpu
from jax.sharding import PartitionSpec as P

MESH = pl.DeviceIdType.MESH

VELOCITIES = (
    (0, 0, 0),
    (1, 0, 0),
    (-1, 0, 0),
    (0, 1, 0),
    (0, -1, 0),
    (0, 0, 1),
    (0, 0, -1),
    (1, 1, 0),
    (-1, -1, 0),
    (1, -1, 0),
    (-1, 1, 0),
    (1, 0, 1),
    (-1, 0, -1),
    (1, 0, -1),
    (-1, 0, 1),
    (0, 1, 1),
    (0, -1, -1),
    (0, 1, -1),
    (0, -1, 1),
)
OPPOSITE = (0, 2, 1, 4, 3, 6, 5, 8, 7, 10, 9, 12, 11, 14, 13, 16, 15, 18, 17)
FLAG = -1
ORDER = (FLAG, 9, 1, 11, 13, 7, FLAG, 3, 15, 17, FLAG, 10, 2, 14, 12, 8, FLAG, 4, 18, 16, 0, 5, 6)
SLOT = tuple(ORDER.index(channel) for channel in range(19))
relax_rate = 1.0 / 0.6
velocity_scale = 0.002

NX, NY, NZ = 8, 32, 128
TOP = 8
LAST = TOP + NY - 1
TILES = NY // 8


def moments(f):
    s = [f[i] + f[i + 1] for i in range(1, 19, 2)]
    d = [f[i] - f[i + 1] for i in range(1, 19, 2)]
    rho = (f[0] + s[8]) + ((s[0] + s[1]) + (s[2] + s[3])) + ((s[4] + s[5]) + (s[6] + s[7]))
    mx = d[0] + (d[3] + d[4]) + (d[5] + d[6])
    my = d[1] + (d[3] - d[4]) + (d[7] + d[8])
    mz = d[2] + (d[5] - d[6]) + (d[7] - d[8])
    return rho, mx, my, mz


def collide(f):
    rho, mx, my, mz = moments(f)
    inverse = 1.0 / rho
    ux, uy, uz = mx * inverse, my * inverse, mz * inverse
    base = rho - 1.5 * (mx * ux + my * uy + mz * uz)
    keep = 1.0 - relax_rate
    relaxed = [keep * f[0] + (relax_rate / 3.0) * base]
    vx, vy, vz = 1.5 * ux, 1.5 * uy, 1.5 * uz
    near = (relax_rate / 18.0) * base
    far = (relax_rate / 36.0) * base
    ax, ay, az = (relax_rate / 6.0) * mx, (relax_rate / 6.0) * my, (relax_rate / 6.0) * mz
    bx, by, bz = 0.5 * ax, 0.5 * ay, 0.5 * az
    for channel, level, flow, speed in (
        (1, near, ax, vx),
        (3, near, ay, vy),
        (5, near, az, vz),
        (7, far, bx + by, vx + vy),
        (9, far, bx - by, vx - vy),
        (11, far, bx + bz, vx + vz),
        (13, far, bx - bz, vx - vz),
        (15, far, by + bz, vy + vz),
        (17, far, by - bz, vy - vz),
    ):
        even = level + flow * speed
        relaxed.append(keep * f[channel] + (even + flow))
        relaxed.append(keep * f[channel + 1] + (even - flow))
    return relaxed


def pulled(held, walls, x, tile):
    f = []
    for channel in range(19):
        cx, cy, cz = VELOCITIES[channel]
        rows = pl.ds(TOP + 8 * tile, 8)
        if channel == 0:
            f.append(held[SLOT[0], x + 1, rows, :])
            continue
        from_rows = pl.ds(TOP + 8 * tile - cy, 8)
        source = held[SLOT[channel], x + 1 - cx, from_rows, :]
        if cz:
            source = pltpu.roll(source, cz % NZ, 1)
        open_site = walls[cz % 3, x + 1 - cx, from_rows, :]
        f.append(jnp.where(open_site > 0, source, held[SLOT[OPPOSITE[channel]], x + 1, rows, :]))
    return f


def kernel(
    gx_size,
    gy_size,
    populations,
    fluid,
    final,
    start,
    solid,
    first,
    second,
    walls,
    sums,
    zmat,
    ymat,
    table,
    gathered,
    mixed,
    ready,
    load_sem,
    fluid_sem,
    halo_send,
    halo_recv,
    all_send,
    all_recv,
):
    gx, gy = lax.axis_index("gx"), lax.axis_index("gy")
    f32 = jnp.float32
    has_left, has_right = gx > 0, gx < gx_size - 1
    has_below, has_above = gy > 0, gy < gy_size - 1

    def number(*conditions):
        return sum(condition.astype(jnp.int32) for condition in conditions)

    barrier = pltpu.get_barrier_semaphore()
    beside_x = ((-1, has_left), (1, has_right), (0, None))
    beside_y = ((-1, has_below), (0, None), (1, has_above))
    for dx, in_x in beside_x:
        for dy, in_y in beside_y:
            if dx == 0 and dy == 0:
                continue
            there = in_y if in_x is None else in_x if in_y is None else in_x & in_y

            @pl.when(there)
            def _():
                pl.semaphore_signal(barrier, inc=1, device_id=(gx + dx, gy + dy), device_id_type=MESH)

    def load(x):
        return pltpu.make_async_copy(populations.at[:, x], start.at[:, x], load_sem.at[x])

    fluid_copy = pltpu.make_async_copy(fluid, solid, fluid_sem)
    load(7).start()
    load(0).start()
    fluid_copy.start()
    for x in range(1, NX - 1):
        load(x).start()

    def tell(stage):
        for way in (-(2**stage), 2**stage):

            @pl.when((gy + way >= 0) & (gy + way < gy_size))
            def _():
                pl.semaphore_signal(ready.at[stage], inc=1, device_id=(gx, gy + way), device_id_type=MESH)

    def hear(stage):
        pl.semaphore_wait(ready.at[stage], number(gy >= 2**stage, gy + 2**stage < gy_size))

    def lane_walls(slab, rows):
        flags = walls[0, slab, rows, :]
        lane = lax.broadcasted_iota(jnp.int32, flags.shape, flags.ndim - 1)
        walls[1, slab, rows, :] = jnp.where(lane == 0, 0.0, pltpu.roll(flags, 1, flags.ndim - 1))
        walls[2, slab, rows, :] = jnp.where(lane == NZ - 1, 0.0, pltpu.roll(flags, NZ - 1, flags.ndim - 1))

    def inner_walls(x, carry):
        for tile in range(TILES):
            rows = pl.ds(TOP + 8 * tile, 8)
            walls[0, x + 1, rows, :] = solid[x, pl.ds(8 * tile, 8), :].astype(jnp.float32)
            lane_walls(x + 1, rows)
        return carry

    def face_flags(x, carry):
        upper = solid[x, pl.ds(NY - 8, 8), :].astype(jnp.float32)
        lower = solid[x, pl.ds(0, 8), :].astype(jnp.float32)
        for slot in (6, 10):
            first[slot, x + 1, pl.ds(TOP + NY - 8, 8), :] = upper
            second[slot, x + 1, pl.ds(TOP + NY - 8, 8), :] = upper
        first[16, x + 1, pl.ds(TOP, 8), :] = lower
        second[16, x + 1, pl.ds(TOP, 8), :] = lower
        return carry

    inner, block = pl.ds(1, NX), pl.ds(TOP, NY)
    low, high = pl.ds(TOP - 1, 1), pl.ds(LAST + 1, 1)
    bottom, top = pl.ds(TOP, 1), pl.ds(LAST, 1)

    def x_sides(flags, cut):
        sides = []
        for start_row, count in ((TOP, cut), (TOP + cut, NY - cut)):
            rows = pl.ds(start_row, count)
            sides += [
                (pl.ds(1, 5 + flags), (NX, rows), (0, rows), (1, 0), has_right, has_left),
                (pl.ds(11, 5 + flags), (1, rows), (NX + 1, rows), (-1, 0), has_left, has_right),
            ]
        below_corners = [
            (pl.ds(1 - flags, 1 + flags), (NX, bottom), (0, high), (1, -1), has_right & has_below, has_left & has_above),
            (pl.ds(15, 1 + flags), (1, bottom), (NX + 1, high), (-1, -1), has_left & has_below, has_right & has_above),
        ]
        above_corners = [
            (pl.ds(5, 1 + flags), (NX, top), (0, low), (1, 1), has_right & has_above, has_left & has_below),
            (pl.ds(11 - flags, 1 + flags), (1, top), (NX + 1, low), (-1, 1), has_left & has_above, has_right & has_below),
        ]
        return below_corners + sides[:2] + above_corners + sides[2:]

    y_sides = [
        (pl.ds(5, 7), (inner, top), (inner, low), (0, 1), has_above, has_below),
        (pl.ds(15, 5), (inner, bottom), (inner, high), (0, -1), has_below, has_above),
        (pl.ds(1, 1), (inner, bottom), (inner, high), (0, -1), has_below, has_above),
    ]

    class Sides:
        def __init__(self, buffer, sides, send, recv, offset):
            self.copies = [
                (
                    pltpu.make_async_remote_copy(
                        src_ref=buffer.at[(channels, *source)],
                        dst_ref=buffer.at[(channels, *target)],
                        send_sem=send.at[offset + i],
                        recv_sem=recv.at[offset + i],
                        device_id=(gx + way[0], gy + way[1]),
                        device_id_type=MESH,
                    ),
                    sent,
                    arrives,
                )
                for i, (channels, source, target, way, sent, arrives) in enumerate(sides)
            ]

        def start(self, *which):
            for i in which or range(len(self.copies)):
                copy, sent, _ = self.copies[i]
                pl.when(sent)(copy.start)

        def wait_recv(self, *which):
            for i in which or range(len(self.copies)):
                copy, _, arrives = self.copies[i]
                pl.when(arrives)(copy.wait_recv)

        def wait_send(self):
            for copy, sent, _ in self.copies:
                pl.when(sent)(copy.wait_send)

    first_x = Sides(first, x_sides(1, 17), halo_send.at[0], halo_recv.at[0], 0)
    first_y = Sides(first, y_sides, halo_send.at[0], halo_recv.at[0], 8)
    second_x = Sides(second, x_sides(0, 16), halo_send.at[1], halo_recv.at[1], 0)
    second_y = Sides(second, y_sides, halo_send.at[1], halo_recv.at[1], 8)

    def relax_tile(x, tile):
        rows = pl.ds(8 * tile, 8)
        relaxed = collide([start[channel, x, rows, :] for channel in range(19)])
        for channel in range(19):
            first[SLOT[channel], x + 1, pl.ds(TOP + 8 * tile, 8), :] = relaxed[channel]

    def step_tile(x, tile):
        relaxed = collide(pulled(first, walls, x, tile))
        for channel in range(19):
            second[SLOT[channel], x + 1, pl.ds(TOP + 8 * tile, 8), :] = relaxed[channel]

    def sum_tile(x, tile):
        rho, mx, my, mz = moments(pulled(second, walls, x, tile))
        here = walls[0, x + 1, pl.ds(TOP + 8 * tile, 8), :]
        scale = here / rho
        for component, value in enumerate((mx * scale, my * scale, mz * scale, here)):
            rows = pl.ds(pl.multiple_of(component * 64 + (x // 4) * 32 + 8 * tile, 8), 8)
            sums[rows, :] = sums[rows, :] + value

    def over_slabs(body, edge, tiles):
        def inner_slab(x, carry):
            for tile in tiles:
                body(x, tile)
            return carry

        if edge:
            for tile in tiles:
                for x in (NX - 1, 0):
                    body(x, tile)
        else:
            lax.fori_loop(1, NX - 1, inner_slab, 0)

    every, outer, middle = range(TILES), (0, TILES - 1), range(1, TILES - 1)

    sums[...] = jnp.zeros(sums.shape, jnp.float32)
    row = lax.broadcasted_iota(jnp.int32, (32, NZ), 0)
    lane = lax.broadcasted_iota(jnp.int32, (32, NZ), 1)
    distance = jnp.abs(2 * (row & 15) + (row >> 4) - (lane >> 2))
    zmat[...] = jnp.where(distance == 0, 0.5, jnp.where(distance == 1, 0.25, 0.0)).astype(jnp.bfloat16)

    turn = 8 * gy + 8

    def y_rows(step, carry):
        at = pl.multiple_of(16 * step, 16)
        row = (lax.broadcasted_iota(jnp.int32, (16, 256), 0) + (at - turn + 256)) & 127
        column = lax.broadcasted_iota(jnp.int32, (16, 256), 1)
        hit = (((row >> 4) & 3) == 3 - (column >> 6)) & ((row & 7) == ((column >> 2) & 7))
        same = ((row >> 3) & 1) != ((column >> 5) & 1)
        ymat[pl.ds(at, 16), :] = jnp.where(hit, jnp.where(same, 0.5, 0.25), 0.0).astype(jnp.bfloat16)
        ymat[pl.ds(pl.multiple_of(at + 128, 16), 16), :] = jnp.where(hit & ~same, 0.25, 0.0).astype(jnp.bfloat16)
        return carry

    lax.fori_loop(0, 8, y_rows, 0)

    @pl.when(gx == 0)
    def _():
        first[6, 0, pl.ds(TOP, NY), :] = jnp.zeros((NY, NZ), f32)
        first[6, 0, low, :] = jnp.zeros((1, NZ), f32)
        first[0, 0, high, :] = jnp.zeros((1, NZ), f32)
        gathered[1] = jnp.zeros((16, 128), f32)

    @pl.when(gx == gx_size - 1)
    def _():
        first[16, NX + 1, pl.ds(TOP, NY), :] = jnp.zeros((NY, NZ), f32)
        first[10, NX + 1, low, :] = jnp.zeros((1, NZ), f32)
        first[16, NX + 1, high, :] = jnp.zeros((1, NZ), f32)
        gathered[2] = jnp.zeros((16, 128), f32)

    @pl.when(gy == 0)
    def _():
        first[6, inner, TOP - 1, :] = jnp.zeros((NX, NZ), f32)
        first[6, 0, low, :] = jnp.zeros((1, NZ), f32)
        first[10, NX + 1, low, :] = jnp.zeros((1, NZ), f32)

    @pl.when(gy == gy_size - 1)
    def _():
        first[16, inner, LAST + 1, :] = jnp.zeros((NX, NZ), f32)
        first[0, 0, high, :] = jnp.zeros((1, NZ), f32)
        first[16, NX + 1, high, :] = jnp.zeros((1, NZ), f32)

    load(7).wait()
    load(0).wait()
    over_slabs(relax_tile, True, every)
    fluid_copy.wait()
    lax.fori_loop(0, NX, face_flags, 0)
    for tile in range(TILES):
        rows, own = pl.ds(TOP + 8 * tile, 8), pl.ds(8 * tile, 8)
        first[6, NX, rows, :] = solid[NX - 1, own, :].astype(f32)
        first[16, 1, rows, :] = solid[0, own, :].astype(f32)
    first[0, NX, pl.ds(TOP, 8), :] = solid[NX - 1, pl.ds(0, 8), :].astype(f32)
    for x in range(1, NX - 1):
        load(x).wait()
    over_slabs(relax_tile, False, outer)
    pl.semaphore_wait(barrier, (1 + number(has_left, has_right)) * (1 + number(has_below, has_above)) - 1)
    first_x.start(0, 1, 4, 5, 2, 3, 6, 7)
    first_y.start()
    tell(0)

    over_slabs(relax_tile, False, middle)
    lax.fori_loop(0, NX, inner_walls, 0)
    over_slabs(step_tile, False, middle)
    hear(0)
    tell(1)

    first_y.wait_recv()
    for slot, row in ((6, TOP - 1), (16, LAST + 1)):
        walls[0, inner, row, :] = first[slot, inner, row, :]
        lane_walls(inner, row)
    over_slabs(step_tile, False, outer)
    hear(1)
    tell(2)
    first_x.wait_recv(2, 3, 4, 5)
    for slot, slab, row in ((6, 0, low), (10, NX + 1, low), (6, 0, pl.ds(TOP + 16, 1)), (16, NX + 1, pl.ds(TOP + 16, 1))):
        walls[0, slab, row, :] = first[slot, slab, row, :]

    def halo_walls(tiles):
        for slot, slab in ((6, 0), (16, NX + 1)):
            for tile in tiles:
                rows = pl.ds(TOP + 8 * tile, 8)
                walls[0, slab, rows, :] = first[slot, slab, rows, :]
                lane_walls(slab, rows)

    halo_walls((0, 1))
    over_slabs(step_tile, True, (0, 1))
    second_x.start(0, 1, 2, 3)
    first_x.wait_recv(0, 1, 6, 7)
    for slot, slab, row in ((0, 0, high), (16, NX + 1, high)):
        walls[0, slab, row, :] = first[slot, slab, row, :]
    halo_walls((2, 3))
    over_slabs(step_tile, True, (2, 3))
    second_x.start(4, 5, 6, 7)
    second_y.start()
    hear(2)
    tell(3)

    over_slabs(sum_tile, False, middle)
    for sides in (first_x, first_y):
        sides.wait_send()
    second_y.wait_recv()
    over_slabs(sum_tile, False, outer)
    second_x.wait_recv()
    over_slabs(sum_tile, True, every)

    def parts(value):
        upper = value.astype(jnp.bfloat16)
        return upper, (value - upper.astype(jnp.float32)).astype(jnp.bfloat16)

    weights = ymat[...]
    over_y = jnp.dot(
        jnp.concatenate([weights, weights], axis=1),
        jnp.concatenate(parts(sums[...]), axis=0),
        preferred_element_type=jnp.float32,
    )
    weights = zmat[...]
    over_z = sum(
        lax.dot_general(weights, part, (((1,), (1,)), ((), ())), preferred_element_type=jnp.float32)
        for part in parts(over_y)
    )
    lane = lax.broadcasted_iota(jnp.int32, (16, 128), 1)
    first_z = ((lane - turn + 256) & 64) != 0
    for part in range(2):
        lanes = slice(128 * part, 128 * part + 128)
        table[part] = jnp.where(first_z, over_z[:16, lanes], over_z[16:, lanes])
    hear(3)

    def exchange(place, x, partner):
        return pltpu.make_async_remote_copy(
            src_ref=table.at[min(place, 1), pl.ds(partner, 1)],
            dst_ref=gathered.at[place, pl.ds(gy, 1)],
            send_sem=all_send.at[place],
            recv_sem=all_recv.at[place],
            device_id=(x, partner),
            device_id_type=MESH,
        )

    def send(place, x, steps):
        for step in steps:
            exchange(place, x, lax.rem(gy + step, gy_size)).start()

    middle_step = gy_size // 2
    steps = sorted(range(gy_size), key=lambda step: abs(step - middle_step))
    for some in (steps[:7], steps[7:]):
        pl.when(has_right)(lambda: send(1, gx + 1, some))
        send(0, gx, [step for step in some if step])
        pl.when(has_left)(lambda: send(2, gx - 1, some))
    gathered[0, pl.ds(gy, 1), :] = table[0, pl.ds(gy, 1), :]

    def everyone(place, count):
        return pltpu.make_async_remote_copy(
            src_ref=table.at[min(place, 1), pl.ds(0, count)],
            dst_ref=gathered.at[place, pl.ds(0, count)],
            send_sem=all_send.at[place],
            recv_sem=all_recv.at[place],
            device_id=(gx, lax.rem(gy + 1, gy_size)),
            device_id_type=MESH,
        )

    column, from_left, from_right = everyone(0, gy_size - 1), everyone(1, gy_size), everyone(2, gy_size)
    second_x.wait_send()
    second_y.wait_send()
    column.wait_send()
    pl.when(has_left)(from_right.wait_send)
    pl.when(has_right)(from_left.wait_send)
    column.wait_recv()
    pl.when(has_left)(from_left.wait_recv)
    pl.when(has_right)(from_right.wait_recv)

    row = lax.broadcasted_iota(jnp.int32, (16, 128), 0)
    lower = (((lane >> 3) - row) & 1) == 0
    mixed[...] = gathered[0] + jnp.where(lower, gathered[1], gathered[2])

    lane = lax.broadcasted_iota(jnp.int32, (8, 128), 1)
    halves = [jnp.zeros((8, 128), jnp.float32) for _ in range(2)]
    for source in range(gy_size):
        spread = jnp.broadcast_to(mixed[pl.ds(source, 1), :], (8, 128))
        for half in range(2):
            turned = pltpu.roll(spread, 64 * half, 1, stride=8, stride_axis=0)
            halves[half] = jnp.where(lane >> 3 == source, turned, halves[half])
    for half in range(2):
        whole = halves[half]
        before = jnp.where(lane == 0, 0.0, pltpu.roll(whole, 1, 1))
        after = jnp.where(lane == 127, 0.0, pltpu.roll(whole, 127, 1))
        final[pl.ds(8 * half, 8), :] = 0.5 * whole + 0.25 * (before + after)


def finish(final, velocity_ref, magnitude_ref):
    for x in range(2):
        for z in range(2):
            fraction = final[pl.ds(8 * z + 6 + x, 1), :]
            scale = 1.0 / (jnp.maximum(fraction, 1.0) * velocity_scale)
            for component in range(3):
                voxels = final[pl.ds(8 * z + 2 * component + x, 1), :]
                velocity_ref[component, x, pl.ds(z, 1), :] = voxels * scale
            magnitude_ref[x, pl.ds(z, 1), :] = fraction / 64.0


def local(gx_size, gy_size, populations, fluid):
    padded = (NX + 2, NY + 2 * TOP, NZ)
    vmem, dma = pltpu.VMEM, pltpu.SemaphoreType.DMA
    f32 = jnp.float32
    blurred = pl.pallas_call(
        functools.partial(kernel, gx_size, gy_size),
        out_shape=jax.ShapeDtypeStruct((16, 128), f32),
        in_specs=[pl.BlockSpec(memory_space=pltpu.HBM)] * 2,
        out_specs=pl.BlockSpec(memory_space=pltpu.VMEM),
        scratch_shapes=[
            vmem((19, NX, NY, NZ), f32),
            vmem((NX, NY, NZ), jnp.int32),
            vmem((len(ORDER), *padded), f32),
            vmem((len(ORDER), *padded), f32),
            vmem((3, *padded), f32),
            vmem((256, 128), f32),
            vmem((32, 128), jnp.bfloat16),
            vmem((256, 256), jnp.bfloat16),
            vmem((2, 16, 128), f32),
            vmem((3, 16, 128), f32),
            vmem((16, 128), f32),
            pltpu.SemaphoreType.REGULAR((4,)),
            dma((8,)),
            dma,
            dma((2, 11)),
            dma((2, 11)),
            dma((3,)),
            dma((3,)),
        ],
        compiler_params=pltpu.CompilerParams(
            collective_id=0, has_side_effects=True, vmem_limit_bytes=55200 * 1024
        ),
    )(populations, fluid)
    velocity, magnitude = pl.pallas_call(
        finish,
        out_shape=(
            jax.ShapeDtypeStruct((3, 2, 2, 128), f32),
            jax.ShapeDtypeStruct((2, 2, 128), f32),
        ),
        in_specs=[pl.BlockSpec(memory_space=pltpu.VMEM)],
        out_specs=(pl.BlockSpec(memory_space=pltpu.VMEM),) * 2,
        compiler_params=pltpu.CompilerParams(vmem_limit_bytes=1024 * 1024),
    )(blurred)
    return jnp.swapaxes(velocity, 2, 3), jnp.swapaxes(magnitude, 1, 2)


def solution(mesh):
    return jax.shard_map(
        functools.partial(local, mesh.shape["gx"], mesh.shape["gy"]),
        mesh=mesh,
        in_specs=(P(None, "gx", "gy", None), P("gx", "gy", None)),
        out_specs=(P(None, "gx", None, "gy"), P("gx", None, "gy")),
        check_vma=False,
    )
```

```python
import functools

import jax
import jax.numpy as jnp
from jax import lax
from jax.experimental import pallas as pl
from jax.experimental.pallas import tpu as pltpu
from jax.sharding import PartitionSpec as P

MESH = pl.DeviceIdType.MESH

VELOCITIES = (
    (0, 0, 0),
    (1, 0, 0),
    (-1, 0, 0),
    (0, 1, 0),
    (0, -1, 0),
    (0, 0, 1),
    (0, 0, -1),
    (1, 1, 0),
    (-1, -1, 0),
    (1, -1, 0),
    (-1, 1, 0),
    (1, 0, 1),
    (-1, 0, -1),
    (1, 0, -1),
    (-1, 0, 1),
    (0, 1, 1),
    (0, -1, -1),
    (0, 1, -1),
    (0, -1, 1),
)
OPPOSITE = (0, 2, 1, 4, 3, 6, 5, 8, 7, 10, 9, 12, 11, 14, 13, 16, 15, 18, 17)
FLAG = -1
ORDER = (FLAG, 9, 1, 11, 13, 7, FLAG, 3, 15, 17, FLAG, 10, 2, 14, 12, 8, FLAG, 4, 18, 16, 0, 5, 6)
SLOT = tuple(ORDER.index(channel) for channel in range(19))
relax_rate = 1.0 / 0.6
velocity_scale = 0.002

NX, NY, NZ = 8, 32, 128
TOP = 8
LAST = TOP + NY - 1
TILES = NY // 8


def moments(f):
    s = [f[i] + f[i + 1] for i in range(1, 19, 2)]
    d = [f[i] - f[i + 1] for i in range(1, 19, 2)]
    rho = (f[0] + s[8]) + ((s[0] + s[1]) + (s[2] + s[3])) + ((s[4] + s[5]) + (s[6] + s[7]))
    mx = d[0] + (d[3] + d[4]) + (d[5] + d[6])
    my = d[1] + (d[3] - d[4]) + (d[7] + d[8])
    mz = d[2] + (d[5] - d[6]) + (d[7] - d[8])
    return rho, mx, my, mz


def collide(f):
    rho, mx, my, mz = moments(f)
    inverse = 1.0 / rho
    ux, uy, uz = mx * inverse, my * inverse, mz * inverse
    base = rho - 1.5 * (mx * ux + my * uy + mz * uz)
    keep = 1.0 - relax_rate
    relaxed = [keep * f[0] + (relax_rate / 3.0) * base]
    vx, vy, vz = 1.5 * ux, 1.5 * uy, 1.5 * uz
    near = (relax_rate / 18.0) * base
    far = (relax_rate / 36.0) * base
    ax, ay, az = (relax_rate / 6.0) * mx, (relax_rate / 6.0) * my, (relax_rate / 6.0) * mz
    bx, by, bz = 0.5 * ax, 0.5 * ay, 0.5 * az
    for channel, level, flow, speed in (
        (1, near, ax, vx),
        (3, near, ay, vy),
        (5, near, az, vz),
        (7, far, bx + by, vx + vy),
        (9, far, bx - by, vx - vy),
        (11, far, bx + bz, vx + vz),
        (13, far, bx - bz, vx - vz),
        (15, far, by + bz, vy + vz),
        (17, far, by - bz, vy - vz),
    ):
        even = level + flow * speed
        relaxed.append(keep * f[channel] + (even + flow))
        relaxed.append(keep * f[channel + 1] + (even - flow))
    return relaxed


def pulled(held, walls, x, tile):
    f = []
    for channel in range(19):
        cx, cy, cz = VELOCITIES[channel]
        rows = pl.ds(TOP + 8 * tile, 8)
        if channel == 0:
            f.append(held[SLOT[0], x + 1, rows, :])
            continue
        from_rows = pl.ds(TOP + 8 * tile - cy, 8)
        source = held[SLOT[channel], x + 1 - cx, from_rows, :]
        if cz:
            source = pltpu.roll(source, cz % NZ, 1)
        open_site = walls[cz % 3, x + 1 - cx, from_rows, :]
        f.append(jnp.where(open_site > 0, source, held[SLOT[OPPOSITE[channel]], x + 1, rows, :]))
    return f


def kernel(
    gx_size,
    gy_size,
    populations,
    fluid,
    final,
    start,
    solid,
    first,
    second,
    walls,
    sums,
    zmat,
    ymat,
    table,
    gathered,
    mixed,
    ready,
    load_sem,
    fluid_sem,
    halo_send,
    halo_recv,
    all_send,
    all_recv,
):
    gx, gy = lax.axis_index("gx"), lax.axis_index("gy")
    f32 = jnp.float32
    has_left, has_right = gx > 0, gx < gx_size - 1
    has_below, has_above = gy > 0, gy < gy_size - 1

    def number(*conditions):
        return sum(condition.astype(jnp.int32) for condition in conditions)

    barrier = pltpu.get_barrier_semaphore()
    beside_x = ((-1, has_left), (1, has_right), (0, None))
    beside_y = ((-1, has_below), (0, None), (1, has_above))
    for dx, in_x in beside_x:
        for dy, in_y in beside_y:
            if dx == 0 and dy == 0:
                continue
            there = in_y if in_x is None else in_x if in_y is None else in_x & in_y

            @pl.when(there)
            def _():
                pl.semaphore_signal(barrier, inc=1, device_id=(gx + dx, gy + dy), device_id_type=MESH)

    def load(x):
        return pltpu.make_async_copy(populations.at[:, x], start.at[:, x], load_sem.at[x])

    fluid_copy = pltpu.make_async_copy(fluid, solid, fluid_sem)
    load(7).start()
    load(0).start()
    fluid_copy.start()
    for x in range(1, NX - 1):
        load(x).start()

    def tell(stage):
        for way in (-(2**stage), 2**stage):

            @pl.when((gy + way >= 0) & (gy + way < gy_size))
            def _():
                pl.semaphore_signal(ready.at[stage], inc=1, device_id=(gx, gy + way), device_id_type=MESH)

    def hear(stage):
        pl.semaphore_wait(ready.at[stage], number(gy >= 2**stage, gy + 2**stage < gy_size))

    def lane_walls(slab, rows):
        flags = walls[0, slab, rows, :]
        lane = lax.broadcasted_iota(jnp.int32, flags.shape, flags.ndim - 1)
        walls[1, slab, rows, :] = jnp.where(lane == 0, 0.0, pltpu.roll(flags, 1, flags.ndim - 1))
        walls[2, slab, rows, :] = jnp.where(lane == NZ - 1, 0.0, pltpu.roll(flags, NZ - 1, flags.ndim - 1))

    def inner_walls(x, carry):
        for tile in range(TILES):
            rows = pl.ds(TOP + 8 * tile, 8)
            walls[0, x + 1, rows, :] = solid[x, pl.ds(8 * tile, 8), :].astype(jnp.float32)
            lane_walls(x + 1, rows)
        return carry

    def face_flags(x, carry):
        upper = solid[x, pl.ds(NY - 8, 8), :].astype(jnp.float32)
        lower = solid[x, pl.ds(0, 8), :].astype(jnp.float32)
        for slot in (6, 10):
            first[slot, x + 1, pl.ds(TOP + NY - 8, 8), :] = upper
            second[slot, x + 1, pl.ds(TOP + NY - 8, 8), :] = upper
        first[16, x + 1, pl.ds(TOP, 8), :] = lower
        second[16, x + 1, pl.ds(TOP, 8), :] = lower
        return carry

    inner, block = pl.ds(1, NX), pl.ds(TOP, NY)
    low, high = pl.ds(TOP - 1, 1), pl.ds(LAST + 1, 1)
    bottom, top = pl.ds(TOP, 1), pl.ds(LAST, 1)

    def x_sides(flags, cut):
        sides = []
        for start_row, count in ((TOP, cut), (TOP + cut, NY - cut)):
            rows = pl.ds(start_row, count)
            sides += [
                (pl.ds(1, 5 + flags), (NX, rows), (0, rows), (1, 0), has_right, has_left),
                (pl.ds(11, 5 + flags), (1, rows), (NX + 1, rows), (-1, 0), has_left, has_right),
            ]
        below_corners = [
            (pl.ds(1 - flags, 1 + flags), (NX, bottom), (0, high), (1, -1), has_right & has_below, has_left & has_above),
            (pl.ds(15, 1 + flags), (1, bottom), (NX + 1, high), (-1, -1), has_left & has_below, has_right & has_above),
        ]
        above_corners = [
            (pl.ds(5, 1 + flags), (NX, top), (0, low), (1, 1), has_right & has_above, has_left & has_below),
            (pl.ds(11 - flags, 1 + flags), (1, top), (NX + 1, low), (-1, 1), has_left & has_above, has_right & has_below),
        ]
        return below_corners + sides[:2] + above_corners + sides[2:]

    y_sides = [
        (pl.ds(5, 7), (inner, top), (inner, low), (0, 1), has_above, has_below),
        (pl.ds(15, 5), (inner, bottom), (inner, high), (0, -1), has_below, has_above),
        (pl.ds(1, 1), (inner, bottom), (inner, high), (0, -1), has_below, has_above),
    ]

    class Sides:
        def __init__(self, buffer, sides, send, recv, offset):
            self.copies = [
                (
                    pltpu.make_async_remote_copy(
                        src_ref=buffer.at[(channels, *source)],
                        dst_ref=buffer.at[(channels, *target)],
                        send_sem=send.at[offset + i],
                        recv_sem=recv.at[offset + i],
                        device_id=(gx + way[0], gy + way[1]),
                        device_id_type=MESH,
                    ),
                    sent,
                    arrives,
                )
                for i, (channels, source, target, way, sent, arrives) in enumerate(sides)
            ]

        def start(self, *which):
            for i in which or range(len(self.copies)):
                copy, sent, _ = self.copies[i]
                pl.when(sent)(copy.start)

        def wait_recv(self, *which):
            for i in which or range(len(self.copies)):
                copy, _, arrives = self.copies[i]
                pl.when(arrives)(copy.wait_recv)

        def wait_send(self):
            for copy, sent, _ in self.copies:
                pl.when(sent)(copy.wait_send)

    first_x = Sides(first, x_sides(1, 17), halo_send.at[0], halo_recv.at[0], 0)
    first_y = Sides(first, y_sides, halo_send.at[0], halo_recv.at[0], 8)
    second_x = Sides(second, x_sides(0, 16), halo_send.at[1], halo_recv.at[1], 0)
    second_y = Sides(second, y_sides, halo_send.at[1], halo_recv.at[1], 8)

    def relax_tile(x, tile):
        rows = pl.ds(8 * tile, 8)
        relaxed = collide([start[channel, x, rows, :] for channel in range(19)])
        for channel in range(19):
            first[SLOT[channel], x + 1, pl.ds(TOP + 8 * tile, 8), :] = relaxed[channel]

    def step_tile(x, tile):
        relaxed = collide(pulled(first, walls, x, tile))
        for channel in range(19):
            second[SLOT[channel], x + 1, pl.ds(TOP + 8 * tile, 8), :] = relaxed[channel]

    def sum_tile(x, tile):
        rho, mx, my, mz = moments(pulled(second, walls, x, tile))
        here = walls[0, x + 1, pl.ds(TOP + 8 * tile, 8), :]
        scale = here / rho
        for component, value in enumerate((mx * scale, my * scale, mz * scale, here)):
            rows = pl.ds(pl.multiple_of(component * 64 + (x // 4) * 32 + 8 * tile, 8), 8)
            sums[rows, :] = sums[rows, :] + value

    def over_slabs(body, edge, tiles):
        def inner_slab(x, carry):
            for tile in tiles:
                body(x, tile)
            return carry

        if edge:
            for tile in tiles:
                for x in (NX - 1, 0):
                    body(x, tile)
        else:
            lax.fori_loop(1, NX - 1, inner_slab, 0)

    every, outer, middle = range(TILES), (0, TILES - 1), range(1, TILES - 1)

    sums[...] = jnp.zeros(sums.shape, jnp.float32)
    row = lax.broadcasted_iota(jnp.int32, (32, NZ), 0)
    lane = lax.broadcasted_iota(jnp.int32, (32, NZ), 1)
    distance = jnp.abs(2 * (row & 15) + (row >> 4) - (lane >> 2))
    zmat[...] = jnp.where(distance == 0, 0.5, jnp.where(distance == 1, 0.25, 0.0)).astype(jnp.bfloat16)

    turn = 8 * gy + 8

    def y_rows(step, carry):
        at = pl.multiple_of(16 * step, 16)
        row = (lax.broadcasted_iota(jnp.int32, (16, 256), 0) + (at - turn + 256)) & 127
        column = lax.broadcasted_iota(jnp.int32, (16, 256), 1)
        hit = (((row >> 4) & 3) == 3 - (column >> 6)) & ((row & 7) == ((column >> 2) & 7))
        same = ((row >> 3) & 1) != ((column >> 5) & 1)
        ymat[pl.ds(at, 16), :] = jnp.where(hit, jnp.where(same, 0.5, 0.25), 0.0).astype(jnp.bfloat16)
        ymat[pl.ds(pl.multiple_of(at + 128, 16), 16), :] = jnp.where(hit & ~same, 0.25, 0.0).astype(jnp.bfloat16)
        return carry

    lax.fori_loop(0, 8, y_rows, 0)

    @pl.when(gx == 0)
    def _():
        first[6, 0, pl.ds(TOP, NY), :] = jnp.zeros((NY, NZ), f32)
        first[6, 0, low, :] = jnp.zeros((1, NZ), f32)
        first[0, 0, high, :] = jnp.zeros((1, NZ), f32)
        gathered[1] = jnp.zeros((16, 128), f32)

    @pl.when(gx == gx_size - 1)
    def _():
        first[16, NX + 1, pl.ds(TOP, NY), :] = jnp.zeros((NY, NZ), f32)
        first[10, NX + 1, low, :] = jnp.zeros((1, NZ), f32)
        first[16, NX + 1, high, :] = jnp.zeros((1, NZ), f32)
        gathered[2] = jnp.zeros((16, 128), f32)

    @pl.when(gy == 0)
    def _():
        first[6, inner, TOP - 1, :] = jnp.zeros((NX, NZ), f32)
        first[6, 0, low, :] = jnp.zeros((1, NZ), f32)
        first[10, NX + 1, low, :] = jnp.zeros((1, NZ), f32)

    @pl.when(gy == gy_size - 1)
    def _():
        first[16, inner, LAST + 1, :] = jnp.zeros((NX, NZ), f32)
        first[0, 0, high, :] = jnp.zeros((1, NZ), f32)
        first[16, NX + 1, high, :] = jnp.zeros((1, NZ), f32)

    load(7).wait()
    load(0).wait()
    over_slabs(relax_tile, True, every)
    fluid_copy.wait()
    lax.fori_loop(0, NX, face_flags, 0)
    for tile in range(TILES):
        rows, own = pl.ds(TOP + 8 * tile, 8), pl.ds(8 * tile, 8)
        first[6, NX, rows, :] = solid[NX - 1, own, :].astype(f32)
        first[16, 1, rows, :] = solid[0, own, :].astype(f32)
    first[0, NX, pl.ds(TOP, 8), :] = solid[NX - 1, pl.ds(0, 8), :].astype(f32)
    for x in range(1, NX - 1):
        load(x).wait()
    over_slabs(relax_tile, False, outer)
    pl.semaphore_wait(barrier, (1 + number(has_left, has_right)) * (1 + number(has_below, has_above)) - 1)
    first_x.start(0, 1, 4, 5, 2, 3, 6, 7)
    first_y.start()
    tell(0)

    over_slabs(relax_tile, False, middle)
    lax.fori_loop(0, NX, inner_walls, 0)
    over_slabs(step_tile, False, middle)
    hear(0)
    tell(1)

    first_y.wait_recv()
    for slot, row in ((6, TOP - 1), (16, LAST + 1)):
        walls[0, inner, row, :] = first[slot, inner, row, :]
        lane_walls(inner, row)
    over_slabs(step_tile, False, outer)
    hear(1)
    tell(2)
    first_x.wait_recv(2, 3, 4, 5)
    for slot, slab, row in ((6, 0, low), (10, NX + 1, low), (6, 0, pl.ds(TOP + 16, 1)), (16, NX + 1, pl.ds(TOP + 16, 1))):
        walls[0, slab, row, :] = first[slot, slab, row, :]

    def halo_walls(tiles):
        for slot, slab in ((6, 0), (16, NX + 1)):
            for tile in tiles:
                rows = pl.ds(TOP + 8 * tile, 8)
                walls[0, slab, rows, :] = first[slot, slab, rows, :]
                lane_walls(slab, rows)

    halo_walls((0, 1))
    over_slabs(step_tile, True, (0, 1))
    second_x.start(0, 1, 2, 3)
    first_x.wait_recv(0, 1, 6, 7)
    for slot, slab, row in ((0, 0, high), (16, NX + 1, high)):
        walls[0, slab, row, :] = first[slot, slab, row, :]
    halo_walls((2, 3))
    over_slabs(step_tile, True, (2, 3))
    second_x.start(4, 5, 6, 7)
    second_y.start()
    hear(2)
    tell(3)

    over_slabs(sum_tile, False, middle)
    for sides in (first_x, first_y):
        sides.wait_send()
    second_y.wait_recv()
    over_slabs(sum_tile, False, outer)
    second_x.wait_recv()
    over_slabs(sum_tile, True, every)

    def parts(value):
        upper = value.astype(jnp.bfloat16)
        return upper, (value - upper.astype(jnp.float32)).astype(jnp.bfloat16)

    weights = ymat[...]
    over_y = jnp.dot(
        jnp.concatenate([weights, weights], axis=1),
        jnp.concatenate(parts(sums[...]), axis=0),
        preferred_element_type=jnp.float32,
    )
    weights = zmat[...]
    over_z = sum(
        lax.dot_general(weights, part, (((1,), (1,)), ((), ())), preferred_element_type=jnp.float32)
        for part in parts(over_y)
    )
    lane = lax.broadcasted_iota(jnp.int32, (16, 128), 1)
    first_z = ((lane - turn + 256) & 64) != 0
    for part in range(2):
        lanes = slice(128 * part, 128 * part + 128)
        table[part] = jnp.where(first_z, over_z[:16, lanes], over_z[16:, lanes])
    hear(3)

    def exchange(place, x, partner):
        return pltpu.make_async_remote_copy(
            src_ref=table.at[min(place, 1), pl.ds(partner, 1)],
            dst_ref=gathered.at[place, pl.ds(gy, 1)],
            send_sem=all_send.at[place],
            recv_sem=all_recv.at[place],
            device_id=(x, partner),
            device_id_type=MESH,
        )

    def send(place, x, steps):
        for step in steps:
            exchange(place, x, lax.rem(gy + step, gy_size)).start()

    middle_step = gy_size // 2
    steps = sorted(range(gy_size), key=lambda step: abs(step - middle_step))
    for some in (steps[:3], steps[3:7], steps[7:]):
        pl.when(has_right)(lambda: send(1, gx + 1, some))
        send(0, gx, [step for step in some if step])
        pl.when(has_left)(lambda: send(2, gx - 1, some))
    gathered[0, pl.ds(gy, 1), :] = table[0, pl.ds(gy, 1), :]

    def everyone(place, count):
        return pltpu.make_async_remote_copy(
            src_ref=table.at[min(place, 1), pl.ds(0, count)],
            dst_ref=gathered.at[place, pl.ds(0, count)],
            send_sem=all_send.at[place],
            recv_sem=all_recv.at[place],
            device_id=(gx, lax.rem(gy + 1, gy_size)),
            device_id_type=MESH,
        )

    column, from_left, from_right = everyone(0, gy_size - 1), everyone(1, gy_size), everyone(2, gy_size)
    second_x.wait_send()
    second_y.wait_send()
    column.wait_send()
    pl.when(has_left)(from_right.wait_send)
    pl.when(has_right)(from_left.wait_send)
    column.wait_recv()
    pl.when(has_left)(from_left.wait_recv)
    pl.when(has_right)(from_right.wait_recv)

    row = lax.broadcasted_iota(jnp.int32, (16, 128), 0)
    lower = (((lane >> 3) - row) & 1) == 0
    mixed[...] = gathered[0] + jnp.where(lower, gathered[1], gathered[2])

    lane = lax.broadcasted_iota(jnp.int32, (8, 128), 1)
    halves = [jnp.zeros((8, 128), jnp.float32) for _ in range(2)]
    for source in range(gy_size):
        spread = jnp.broadcast_to(mixed[pl.ds(source, 1), :], (8, 128))
        for half in range(2):
            turned = pltpu.roll(spread, 64 * half, 1, stride=8, stride_axis=0)
            halves[half] = jnp.where(lane >> 3 == source, turned, halves[half])
    for half in range(2):
        whole = halves[half]
        before = jnp.where(lane == 0, 0.0, pltpu.roll(whole, 1, 1))
        after = jnp.where(lane == 127, 0.0, pltpu.roll(whole, 127, 1))
        final[pl.ds(8 * half, 8), :] = 0.5 * whole + 0.25 * (before + after)


def finish(final, velocity_ref, magnitude_ref):
    for x in range(2):
        for z in range(2):
            fraction = final[pl.ds(8 * z + 6 + x, 1), :]
            scale = 1.0 / (jnp.maximum(fraction, 1.0) * velocity_scale)
            for component in range(3):
                voxels = final[pl.ds(8 * z + 2 * component + x, 1), :]
                velocity_ref[component, x, pl.ds(z, 1), :] = voxels * scale
            magnitude_ref[x, pl.ds(z, 1), :] = fraction / 64.0


def local(gx_size, gy_size, populations, fluid):
    padded = (NX + 2, NY + 2 * TOP, NZ)
    vmem, dma = pltpu.VMEM, pltpu.SemaphoreType.DMA
    f32 = jnp.float32
    blurred = pl.pallas_call(
        functools.partial(kernel, gx_size, gy_size),
        out_shape=jax.ShapeDtypeStruct((16, 128), f32),
        in_specs=[pl.BlockSpec(memory_space=pltpu.HBM)] * 2,
        out_specs=pl.BlockSpec(memory_space=pltpu.VMEM),
        scratch_shapes=[
            vmem((19, NX, NY, NZ), f32),
            vmem((NX, NY, NZ), jnp.int32),
            vmem((len(ORDER), *padded), f32),
            vmem((len(ORDER), *padded), f32),
            vmem((3, *padded), f32),
            vmem((256, 128), f32),
            vmem((32, 128), jnp.bfloat16),
            vmem((256, 256), jnp.bfloat16),
            vmem((2, 16, 128), f32),
            vmem((3, 16, 128), f32),
            vmem((16, 128), f32),
            pltpu.SemaphoreType.REGULAR((4,)),
            dma((8,)),
            dma,
            dma((2, 11)),
            dma((2, 11)),
            dma((3,)),
            dma((3,)),
        ],
        compiler_params=pltpu.CompilerParams(
            collective_id=0, has_side_effects=True, vmem_limit_bytes=55200 * 1024
        ),
    )(populations, fluid)
    velocity, magnitude = pl.pallas_call(
        finish,
        out_shape=(
            jax.ShapeDtypeStruct((3, 2, 2, 128), f32),
            jax.ShapeDtypeStruct((2, 2, 128), f32),
        ),
        in_specs=[pl.BlockSpec(memory_space=pltpu.VMEM)],
        out_specs=(pl.BlockSpec(memory_space=pltpu.VMEM),) * 2,
        compiler_params=pltpu.CompilerParams(vmem_limit_bytes=1024 * 1024),
    )(blurred)
    return jnp.swapaxes(velocity, 2, 3), jnp.swapaxes(magnitude, 1, 2)


def solution(mesh):
    return jax.shard_map(
        functools.partial(local, mesh.shape["gx"], mesh.shape["gy"]),
        mesh=mesh,
        in_specs=(P(None, "gx", "gy", None), P("gx", "gy", None)),
        out_specs=(P(None, "gx", None, "gy"), P("gx", None, "gy")),
        check_vma=False,
    )
```
